32 devices in a mesh: row: 4 (over y, x), col: 8 (over z, core).
Axes of the slice: x: 2, y: 2, z: 4, core: 2. Of those that a mesh axis runs over, the one named last changes fastest.
Arguments:
- tokens_in: bfloat16 [4096, 5120], P('row', 'col'), may hold values from -6 to 6
- token_grad: bfloat16 [4096, 5120], P('row', 'col'), may hold values from -6 to 6
- gate_gain: float32 [5120], replicated, may hold values from -4 to 4
- inner_weight: bfloat16 [5120, 13824], P(None, 'col'), may hold values from -0.078125 to 0.078125
- inner_bias: float32 [13824], P('col'), may hold values from -4 to 4
- outer_weight: bfloat16 [5120, 13824], P(None, 'col'), may hold values from -0.0546875 to 0.0546875
- inner_down: bfloat16 [5120, 64], replicated, may hold values from -0.078125 to 0.078125
- inner_up: bfloat16 [64, 13824], P(None, 'col'), may hold values from -0.1796875 to 0.1796875
- outer_down: bfloat16 [13824, 64], P('col'), may hold values from -0.0546875 to 0.0546875
- outer_up: bfloat16 [64, 5120], replicated, may hold values from -0.1796875 to 0.1796875
Outputs:
- tokens_grad: bfloat16 [4096, 5120], P('row', 'col')
- inner_down_grad: float32 [5120, 64], P('col')
- inner_up_grad: float32 [64, 13824], P(None, 'col')
- outer_down_grad: float32 [13824, 64], P('col')
- outer_up_grad: float32 [64, 5120], P(None, 'col')
The draws below stay inside these ranges and needn't reach their ends.
All inputs are finite; a program needn't handle non-finite values.
Results may differ from the reference program's by a relative error of at most 0.023.
Values may be sent and summed in bfloat16 or wider, within the bound.
No kernel may reach another device: no remote copies, remote signals or barrier semaphores. Data moves between devices by JAX's collectives and lax.ppermute only.
A program may use at most 128 MiB of HBM per device.

```python
import math
import jax
import jax.numpy as jnp
from jax import lax

D = 5120
FF = 13824
R = 64
TOKENS = 4096
FF_BLOCK = 1728
N_COL = 8


def level_of(rng, shape, pieces, smallest, largest):
    gain, own = 1.0, jax.random.fold_in(rng, 6)
    for position, parts in pieces:
        draws = jnp.exp(jax.random.uniform(jax.random.fold_in(own, position), (parts,), jnp.float32, smallest / len(pieces), largest / len(pieces)))
        gain = gain * jnp.repeat(draws, shape[position] // parts).reshape([-1 if axis == position else 1 for axis in range(len(shape))])
    return gain


def normal_values(key, dims, width, reach, split=(), held_as=jnp.bfloat16):
    entries = width * jax.random.normal(key, dims, jnp.float32)
    if split:
        entries = entries * level_of(key, dims, split, -0.22, 0.18)
    return jnp.clip(entries, -reach, reach).astype(held_as)


def setup_inputs(seed: int = 0) -> dict:
    arg_keys = jax.random.split(jax.random.key(seed), 11)
    tokens_in = normal_values(arg_keys[0], (TOKENS, D), 1.0, 6.0, ((0, 4), (1, 8)))
    token_grad = normal_values(arg_keys[1], (TOKENS, D), 1.0, 6.0, ((0, 4), (1, 8)))
    gate_gain = normal_values(arg_keys[2], (D,), 1.0, 4.0, (), jnp.float32)
    inner_weight = normal_values(arg_keys[3], (D, FF), D ** -0.5, 0.078125, ((1, 8),))
    inner_bias = normal_values(arg_keys[4], (FF,), 1.0, 4.0, ((0, 8),), jnp.float32)
    outer_weight = normal_values(arg_keys[5], (D, FF), FF ** -0.5, 0.0546875, ((1, 8),))
    inner_down = normal_values(arg_keys[6], (D, R), D ** -0.5, 0.078125)
    inner_up = normal_values(arg_keys[7], (R, FF), 0.03, 0.1796875, ((1, 8),))
    outer_down = normal_values(arg_keys[8], (FF, R), FF ** -0.5, 0.0546875, ((0, 8),))
    outer_up = normal_values(arg_keys[9], (R, D), 0.03, 0.1796875)
    return dict(tokens_in=tokens_in, token_grad=token_grad, gate_gain=gate_gain, inner_weight=inner_weight, inner_bias=inner_bias, outer_weight=outer_weight, inner_down=inner_down, inner_up=inner_up, outer_down=outer_down, outer_up=outer_up)


SLOPE_SCALE = 0.7978845608028654
CUBIC = 0.044715

def gelu_value(pre):
    inner = SLOPE_SCALE * (pre + CUBIC * pre * pre * pre)
    return 0.5 * pre * (1.0 + jnp.tanh(inner))

def gelu_slope(pre):
    tangent = jnp.tanh(SLOPE_SCALE * (pre + CUBIC * pre * pre * pre))
    return 0.5 * (1.0 + tangent) + 0.5 * pre * (1.0 - tangent * tangent) * SLOPE_SCALE * (1.0 + 3.0 * CUBIC * pre * pre)

def reference(tokens_in, token_grad, gate_gain, inner_weight, inner_bias, outer_weight, inner_down, inner_up, outer_down, outer_up):
    f32 = jnp.float32
    bf16 = jnp.bfloat16
    gated = (gate_gain[None, :] * token_grad.astype(f32)).astype(bf16)
    inner_low = jnp.dot(tokens_in, inner_down, preferred_element_type=f32).astype(bf16)
    pre = jnp.dot(tokens_in, inner_weight, preferred_element_type=f32) + jnp.dot(inner_low, inner_up, preferred_element_type=f32) + inner_bias[None, :]
    hidden = gelu_value(pre).astype(bf16)
    hidden_low = jnp.dot(hidden, outer_down, preferred_element_type=f32).astype(bf16)
    grad_low = jnp.dot(gated, outer_up.T, preferred_element_type=f32).astype(bf16)
    grad_hidden = jnp.dot(gated, outer_weight, preferred_element_type=f32) + jnp.dot(grad_low, outer_down.T, preferred_element_type=f32)
    grad_pre = (grad_hidden * gelu_slope(pre)).astype(bf16)
    pre_low = jnp.dot(grad_pre, inner_up.T, preferred_element_type=f32).astype(bf16)

    def add_block(total, index):
        start = index * FF_BLOCK
        piece = lax.dynamic_slice_in_dim(grad_pre, start, FF_BLOCK, 1)
        weights = lax.dynamic_slice_in_dim(inner_weight, start, FF_BLOCK, 1)
        part = jnp.dot(piece, weights.T, preferred_element_type=f32).astype(bf16)
        part = lax.optimization_barrier(part)
        return (total + part.astype(f32), None)
    start_total = jnp.zeros((tokens_in.shape[0], tokens_in.shape[1]), f32)
    total, _ = lax.scan(add_block, start_total, jnp.arange(N_COL, dtype=jnp.int32))
    tokens_grad = (total + jnp.dot(pre_low, inner_down.T, preferred_element_type=f32)).astype(bf16)
    scale = 1.0 / math.sqrt(tokens_in.shape[0])
    inner_down_grad = jnp.dot(tokens_in.T, pre_low, preferred_element_type=f32) * scale
    inner_up_grad = jnp.dot(inner_low.T, grad_pre, preferred_element_type=f32) * scale
    outer_down_grad = jnp.dot(hidden.T, grad_low, preferred_element_type=f32) * scale
    outer_up_grad = jnp.dot(hidden_low.T, gated, preferred_element_type=f32) * scale
    return (tokens_grad, inner_down_grad, inner_up_grad, outer_down_grad, outer_up_grad)
```

```python
import functools
import math

import jax
import jax.numpy as jnp
from jax import lax
from jax.experimental import pallas as pl
from jax.experimental.pallas import tpu as pltpu
from jax.sharding import PartitionSpec as P

SLOPE_SCALE = 0.7978845608028654
CUBIC = 0.044715
F32 = jnp.float32
BF16 = jnp.bfloat16
LANES = 128
COLS = 256
VMEM_BYTES = 52 * 1024 * 1024
SPLIT = (384, 320, 192, 128)


def dot_nn(left, right):
    return jnp.dot(left, right, preferred_element_type=F32)


def dot_nt(left, right):
    return lax.dot_general(left, right, (((1,), (1,)), ((), ())), preferred_element_type=F32)


def dot_tn(left, right):
    return lax.dot_general(left, right, (((0,), (0,)), ((), ())), preferred_element_type=F32)


def hidden_kernel(ff, both_ref, inner_ref, outer_ref, bias_ref, up_ref, down_lo_ref, down_hi_ref, *refs):
    grad_ref, low_ref, grads_ref, pre_acc, hid_acc, hidden_ref = refs[-6:]
    step = pl.program_id(0)
    _, _, tokens, width = both_ref.shape
    padded = pre_acc.shape[1]

    def product(which, weight_ref):
        first, second = both_ref[0, which], both_ref[1, which]
        if width % LANES == 0:
            return dot_nt(jnp.concatenate([first, second], axis=1), weight_ref[...])
        return dot_nt(first, weight_ref[:, :width]) + dot_nt(second, weight_ref[:, width:])

    @pl.when(step == 0)
    def _():
        pre_acc[...] = product(0, inner_ref)
        hid_acc[...] = product(1, outer_ref)

    @pl.when(step > 0)
    def _():
        pre_acc[...] += product(0, inner_ref)
        hid_acc[...] += product(1, outer_ref)

    @pl.when(step == pl.num_programs(0) - 1)
    def _():
        tail = slice(padded - LANES, padded)
        inner_low = pre_acc[:, tail].astype(BF16)
        grad_low = hid_acc[:, tail].astype(BF16)
        rank = LANES // 2
        low = jnp.zeros((tokens, LANES), F32)
        for start in range(0, padded, COLS):
            cols = slice(start, start + COLS)
            pre = pre_acc[:, cols] + dot_nn(inner_low, up_ref[:, cols]) + bias_ref[:, cols]
            square = pre * pre
            tangent = jnp.tanh(SLOPE_SCALE * pre * (1.0 + CUBIC * square))
            half = 0.5 + 0.5 * tangent
            hidden = (pre * half).astype(BF16)
            slope = half + 0.5 * pre * (1.0 - tangent * tangent) * (
                SLOPE_SCALE + 3.0 * CUBIC * SLOPE_SCALE * square
            )
            grad_hidden = hid_acc[:, cols] + dot_nn(grad_low, down_hi_ref[:, cols])
            grad_pre = (grad_hidden * slope).astype(BF16)
            hidden_ref[:, cols] = hidden
            grad_ref[:, cols] = grad_pre
        low = dot_nt(hidden_ref[...], down_lo_ref[...]) + dot_nt(grad_ref[...], up_ref[...])
        low = low.astype(BF16)
        low_ref[...] = low
        grads_ref[:rank] = dot_tn(inner_low, grad_ref[...])[rank:]
        grads_ref[rank:] = dot_tn(grad_low, hidden_ref[...])[rank:]
        lane = lax.broadcasted_iota(jnp.int32, (tokens, LANES), 1)
        keep = lane + (padded - LANES) < ff
        filled = jnp.where(lane >= rank, low, jnp.zeros_like(low))
        grad_ref[:, tail] = jnp.where(keep, grad_ref[:, tail], filled)
        for start in range(0, padded - LANES, LANES):
            if start + LANES > ff:
                here = slice(start, start + LANES)
                grad_ref[:, here] = jnp.where(lane + start < ff, grad_ref[:, here], jnp.zeros_like(low))


def hidden_call(both, inner_cat, outer_cat, bias, up, down_lo, down_hi, ff, after=()):
    devices, _, tokens, width = both.shape
    padded = inner_cat.shape[0]
    steps = devices // 2
    whole = lambda k: (0, 0)
    flops = 4 * tokens * devices * width * padded
    return pl.pallas_call(
        functools.partial(hidden_kernel, ff),
        grid=(steps,),
        in_specs=[
            pl.BlockSpec((2, 2, tokens, width), lambda k: (k, 0, 0, 0)),
            pl.BlockSpec((padded, 2 * width), lambda k: (0, k)),
            pl.BlockSpec((padded, 2 * width), lambda k: (0, k)),
            pl.BlockSpec((1, padded), whole),
            pl.BlockSpec((LANES, padded), whole),
            pl.BlockSpec((LANES, padded), whole),
            pl.BlockSpec((LANES, padded), whole),
        ] + [pl.BlockSpec(memory_space=pl.ANY)] * len(after),
        out_specs=[
            pl.BlockSpec((tokens, padded), whole),
            pl.BlockSpec((tokens, LANES), whole),
            pl.BlockSpec((LANES, padded), whole),
        ],
        out_shape=[
            jax.ShapeDtypeStruct((tokens, padded), BF16),
            jax.ShapeDtypeStruct((tokens, LANES), BF16),
            jax.ShapeDtypeStruct((LANES, padded), F32),
        ],
        scratch_shapes=[
            pltpu.VMEM((tokens, padded), F32),
            pltpu.VMEM((tokens, padded), F32),
            pltpu.VMEM((tokens, padded), BF16),
        ],
        compiler_params=pltpu.CompilerParams(vmem_limit_bytes=VMEM_BYTES),
        cost_estimate=pl.CostEstimate(
            flops=flops, bytes_accessed=4 * devices * width * padded, transcendentals=tokens * padded
        ),
    )(both, inner_cat, outer_cat, bias, up, down_lo, down_hi, *after)


def share_kernel(place_ref, grad_ref, weight_ref, *refs):
    own_ref, other_ref = refs[-2:]
    width = own_ref.shape[2]
    if width % LANES == 0:
        share = dot_nn(grad_ref[...], weight_ref[...]).astype(BF16)
        first, second = share[:, :width], share[:, width:]
    else:
        first = dot_nn(grad_ref[...], weight_ref[:, :width]).astype(BF16)
        second = dot_nn(grad_ref[...], weight_ref[:, width:]).astype(BF16)

    @pl.when(place_ref[1] == 0)
    def _():
        own_ref[0] = first
        other_ref[0] = second

    @pl.when(place_ref[1] != 0)
    def _():
        own_ref[0] = second
        other_ref[0] = first


def share_call(place, grad, weight, chips, after=()):
    tokens, padded = grad.shape
    width = weight.shape[1] // (2 * chips)
    out = pl.BlockSpec((1, tokens, width), lambda j, place: (j, 0, 0))
    shape = jax.ShapeDtypeStruct((chips, tokens, width), BF16)
    return pl.pallas_call(
        share_kernel,
        grid_spec=pltpu.PrefetchScalarGridSpec(
            num_scalar_prefetch=1,
            grid=(chips,),
            in_specs=[
                pl.BlockSpec((tokens, padded), lambda j, place: (0, 0)),
                pl.BlockSpec((padded, 2 * width), lambda j, place: (0, lax.rem(place[0] + j, chips))),
            ] + [pl.BlockSpec(memory_space=pl.ANY)] * len(after),
            out_specs=[out, out],
        ),
        out_shape=[shape, shape],
        compiler_params=pltpu.CompilerParams(vmem_limit_bytes=VMEM_BYTES),
        cost_estimate=pl.CostEstimate(
            flops=4 * tokens * chips * width * padded,
            bytes_accessed=4 * chips * width * padded,
            transcendentals=0,
        ),
    )(place, grad, weight, *after)


def lane_pairs(pairs):
    return [(2 * a + core, 2 * b + core) for a, b in pairs for core in (0, 1)]


def send(value, pairs):
    return lax.ppermute(value, "col", lane_pairs(pairs))


def swap_cores(value, chips):
    return lax.ppermute(value, "col", [(i, i ^ 1) for i in range(2 * chips)])


def add(*terms):
    total = terms[0].astype(F32)
    for term in terms[1:]:
        total = total + term.astype(F32)
    return total


class Shares:
    def __init__(self, own, other, chips):
        arrived = swap_cores(other, chips)
        self.shares = [add(own[j], arrived[j]) for j in range(chips)]
        self.chips, self.step, self.up, self.down = chips, 0, None, None

    def hop(self):
        self.step += 1
        s, chips = self.step, self.chips
        up, down = self.shares[chips - s], self.shares[s]
        if s > 1:
            up, down = up + self.up.astype(F32), down + self.down.astype(F32)
        up, down = up.astype(BF16), down.astype(BF16)
        self.up = send(up, [(z, z + 1) for z in range(s)])
        self.down = send(down, [(z, z - 1) for z in range(chips - s, chips)])
        return [up, down]

    def left(self):
        return self.chips - 1 - self.step

    def result(self):
        return add(self.shares[0], self.up, self.down).astype(BF16)


def sum_low(low, core, chips):
    half = low.shape[0] // 2
    first, second = low[:half], low[half:]
    mine = jnp.where(core == 0, first, second)
    theirs = jnp.where(core == 0, second, first)
    mine = add(mine, swap_cores(theirs, chips))
    up = down = jnp.zeros(mine.shape, F32)
    for s in range(chips - 1):
        up = up + send((mine + up).astype(BF16), [(s, s + 1)]).astype(F32)
        down = down + send((mine + down).astype(BF16), [(chips - 1 - s, chips - 2 - s)]).astype(F32)
    total = (mine + up + down).astype(BF16)
    others = swap_cores(total, chips)
    first = jnp.where(core == 0, total, others)
    second = jnp.where(core == 0, others, total)
    return jnp.concatenate([first, second], axis=0)


def sum_rows(value):
    rows = lax.axis_size("row")
    if rows & (rows - 1):
        return lax.psum(value, "row").astype(F32)
    bits = [1 << b for b in range(rows.bit_length() - 1)]
    half = value.shape[0] // 2
    pieces = [(value[:half], bits), (value[half:], bits[::-1])]
    sums = []
    for piece, order in pieces:
        for bit in order:
            got = lax.ppermute(piece.astype(BF16), "row", [(i, i ^ bit) for i in range(rows)])
            piece = piece.astype(BF16).astype(F32) + got.astype(F32)
        sums.append(piece)
    return jnp.concatenate(sums, axis=0)


def local(
    tokens_in, token_grad, gate_gain, inner_weight, inner_bias, outer_weight,
    inner_down, inner_up, outer_down, outer_up,
):
    chips = lax.axis_size("col") // 2
    col_index = lax.axis_index("col")
    core = lax.rem(col_index, 2)
    place = jnp.stack([lax.div(col_index, 2), core]).astype(jnp.int32)
    tok_rows, width = token_grad.shape
    features, ff = inner_weight.shape
    rank = inner_down.shape[1]
    padded = -(-(ff + rank) // COLS) * COLS
    scale = 1.0 / math.sqrt(tok_rows * lax.axis_size("row"))

    gain_local = lax.dynamic_slice_in_dim(gate_gain, col_index * width, width, 0)
    total = sum(SPLIT)
    sizes = [tok_rows * part // total for part in SPLIT]
    starts = [sum(sizes[:i]) for i in range(len(sizes))]

    gathered, gated_parts = [], []
    for start, size in zip(starts, sizes):
        gated = (gain_local[None, :] * token_grad[start : start + size].astype(F32)).astype(BF16)
        both = jnp.stack([tokens_in[start : start + size], gated])
        gathered.append(lax.all_gather(both, "col", axis=0))
        gated_parts.append(gated)

    gap = padded - ff - rank
    blank = jnp.zeros((gap, features), BF16)
    inner_cat = jnp.concatenate([inner_weight.T, blank, inner_down.T], axis=0)
    outer_cat = jnp.concatenate([outer_weight.T, blank, outer_up], axis=0)
    bias = jnp.pad(inner_bias, (0, padded - ff))[None, :]
    up_hi = jnp.pad(inner_up, ((LANES - rank, 0), (0, padded - ff)))
    down_hi = jnp.pad(outer_down.T, ((LANES - rank, 0), (0, padded - ff)))
    down_lo = jnp.pad(outer_down.T, ((0, LANES - rank), (0, padded - ff)))

    last = len(sizes) - 1
    moving, lows, grads = [], [], None
    early = None
    for index, both in enumerate(gathered):
        before = moving[-1] if moving else None
        after = []
        while before is not None and before.left() > 1:
            after = before.hop()
        if index == last and last > 1:
            early = sum_low(jnp.concatenate(lows[:-1], axis=0), core, chips)
            after = after + [early]
        grad_pre, low, grad = hidden_call(
            both, inner_cat, outer_cat, bias, up_hi, down_lo, down_hi, ff, after
        )
        lows.append(low)
        grads = grad if grads is None else grads + grad
        after = before.hop() if before is not None else []
        if index == last:
            hidden_part = (grads[:, :ff] * scale).astype(BF16)
            after = after + [hidden_part]
        own, other = share_call(place, grad_pre, inner_cat, chips, after)
        moving.append(Shares(own, other, chips))
    while moving[-1].left():
        moving[-1].hop()
    tokens_grad = jnp.concatenate([shares.result() for shares in moving], axis=0)

    hidden_sums = sum_rows(hidden_part)
    inner_up_grad = hidden_sums[:rank]
    outer_down_grad = hidden_sums[rank:].T

    late = sum_low(jnp.concatenate(lows[max(last - 1, 0) :], axis=0), core, chips)
    low = late if early is None else jnp.concatenate([early, late], axis=0)
    gated_local = jnp.concatenate(gated_parts, axis=0)
    small = jnp.concatenate(
        [dot_tn(low[:, :rank], gated_local), dot_tn(low[:, rank:], tokens_in)], axis=0
    )
    small_sums = sum_rows((small * scale).astype(BF16))
    outer_up_grad = small_sums[:rank]
    inner_down_grad = small_sums[rank:].T
    return (tokens_grad, inner_down_grad, inner_up_grad, outer_down_grad, outer_up_grad)


def solution(mesh):
    placed = (
        P("row", "col"),
        P("row", "col"),
        P(),
        P(None, "col"),
        P("col"),
        P(None, "col"),
        P(),
        P(None, "col"),
        P("col", None),
        P(),
    )
    return jax.shard_map(
        local,
        mesh=mesh,
        in_specs=placed,
        out_specs=(P("row", "col"), P("col", None), P(None, "col"), P("col", None), P(None, "col")),
        check_vma=False,
    )
```

```python
import functools
import math

import jax
import jax.numpy as jnp
from jax import lax
from jax.experimental import pallas as pl
from jax.experimental.pallas import tpu as pltpu
from jax.sharding import PartitionSpec as P

SLOPE_SCALE = 0.7978845608028654
CUBIC = 0.044715
F32 = jnp.float32
BF16 = jnp.bfloat16
LANES = 128
COLS = 256
VMEM_BYTES = 52 * 1024 * 1024
COST = pl.CostEstimate(flops=20_000_000_000, bytes_accessed=36_000_000, transcendentals=0)
SPLIT = (384, 320, 192, 128)


def dot_nn(left, right):
    return jnp.dot(left, right, preferred_element_type=F32)


def dot_nt(left, right):
    return lax.dot_general(left, right, (((1,), (1,)), ((), ())), preferred_element_type=F32)


def dot_tn(left, right):
    return lax.dot_general(left, right, (((0,), (0,)), ((), ())), preferred_element_type=F32)


def hidden_kernel(ff, both_ref, inner_ref, outer_ref, bias_ref, up_ref, down_lo_ref, down_hi_ref, *refs):
    grad_ref, low_ref, grads_ref, pre_acc, hid_acc, hidden_ref = refs[-6:]
    step = pl.program_id(0)
    _, _, tokens, width = both_ref.shape
    padded = pre_acc.shape[1]

    def product(which, weight_ref):
        first, second = both_ref[0, which], both_ref[1, which]
        if width % LANES == 0:
            return dot_nt(jnp.concatenate([first, second], axis=1), weight_ref[...])
        return dot_nt(first, weight_ref[:, :width]) + dot_nt(second, weight_ref[:, width:])

    @pl.when(step == 0)
    def _():
        pre_acc[...] = product(0, inner_ref)
        hid_acc[...] = product(1, outer_ref)

    @pl.when(step > 0)
    def _():
        pre_acc[...] += product(0, inner_ref)
        hid_acc[...] += product(1, outer_ref)

    @pl.when(step == pl.num_programs(0) - 1)
    def _():
        tail = slice(padded - LANES, padded)
        inner_low = pre_acc[:, tail].astype(BF16)
        grad_low = hid_acc[:, tail].astype(BF16)
        rank = LANES // 2
        low = jnp.zeros((tokens, LANES), F32)
        for start in range(0, padded, COLS):
            cols = slice(start, start + COLS)
            pre = pre_acc[:, cols] + dot_nn(inner_low, up_ref[:, cols]) + bias_ref[:, cols]
            square = pre * pre
            tangent = jnp.tanh(SLOPE_SCALE * pre * (1.0 + CUBIC * square))
            half = 0.5 + 0.5 * tangent
            hidden = (pre * half).astype(BF16)
            slope = half + 0.5 * pre * (1.0 - tangent * tangent) * (
                SLOPE_SCALE + 3.0 * CUBIC * SLOPE_SCALE * square
            )
            grad_hidden = hid_acc[:, cols] + dot_nn(grad_low, down_hi_ref[:, cols])
            grad_pre = (grad_hidden * slope).astype(BF16)
            hidden_ref[:, cols] = hidden
            grad_ref[:, cols] = grad_pre
        low = dot_nt(hidden_ref[...], down_lo_ref[...]) + dot_nt(grad_ref[...], up_ref[...])
        low = low.astype(BF16)
        low_ref[...] = low
        grads_ref[:rank] = dot_tn(inner_low, grad_ref[...])[rank:]
        grads_ref[rank:] = dot_tn(grad_low, hidden_ref[...])[rank:]
        lane = lax.broadcasted_iota(jnp.int32, (tokens, LANES), 1)
        keep = lane + (padded - LANES) < ff
        filled = jnp.where(lane >= rank, low, jnp.zeros_like(low))
        grad_ref[:, tail] = jnp.where(keep, grad_ref[:, tail], filled)
        for start in range(0, padded - LANES, LANES):
            if start + LANES > ff:
                here = slice(start, start + LANES)
                grad_ref[:, here] = jnp.where(lane + start < ff, grad_ref[:, here], jnp.zeros_like(low))


def hidden_call(both, inner_cat, outer_cat, bias, up, down_lo, down_hi, ff, after=()):
    devices, _, tokens, width = both.shape
    padded = inner_cat.shape[0]
    steps = devices // 2
    whole = lambda k: (0, 0)
    return pl.pallas_call(
        functools.partial(hidden_kernel, ff),
        grid=(steps,),
        in_specs=[
            pl.BlockSpec((2, 2, tokens, width), lambda k: (k, 0, 0, 0)),
            pl.BlockSpec((padded, 2 * width), lambda k: (0, k)),
            pl.BlockSpec((padded, 2 * width), lambda k: (0, k)),
            pl.BlockSpec((1, padded), whole),
            pl.BlockSpec((LANES, padded), whole),
            pl.BlockSpec((LANES, padded), whole),
            pl.BlockSpec((LANES, padded), whole),
        ] + [pl.BlockSpec(memory_space=pl.ANY)] * len(after),
        out_specs=[
            pl.BlockSpec((tokens, padded), whole),
            pl.BlockSpec((tokens, LANES), whole),
            pl.BlockSpec((LANES, padded), whole),
        ],
        out_shape=[
            jax.ShapeDtypeStruct((tokens, padded), BF16),
            jax.ShapeDtypeStruct((tokens, LANES), BF16),
            jax.ShapeDtypeStruct((LANES, padded), F32),
        ],
        scratch_shapes=[
            pltpu.VMEM((tokens, padded), F32),
            pltpu.VMEM((tokens, padded), F32),
            pltpu.VMEM((tokens, padded), BF16),
        ],
        compiler_params=pltpu.CompilerParams(vmem_limit_bytes=VMEM_BYTES),
        cost_estimate=COST,
    )(both, inner_cat, outer_cat, bias, up, down_lo, down_hi, *after)


def share_kernel(place_ref, grad_ref, weight_ref, *refs):
    own_ref, other_ref = refs[-2:]
    width = own_ref.shape[2]
    if width % LANES == 0:
        share = dot_nn(grad_ref[...], weight_ref[...]).astype(BF16)
        first, second = share[:, :width], share[:, width:]
    else:
        first = dot_nn(grad_ref[...], weight_ref[:, :width]).astype(BF16)
        second = dot_nn(grad_ref[...], weight_ref[:, width:]).astype(BF16)

    @pl.when(place_ref[1] == 0)
    def _():
        own_ref[0] = first
        other_ref[0] = second

    @pl.when(place_ref[1] != 0)
    def _():
        own_ref[0] = second
        other_ref[0] = first


def share_call(place, grad, weight, chips, after=()):
    tokens, padded = grad.shape
    width = weight.shape[1] // (2 * chips)
    out = pl.BlockSpec((1, tokens, width), lambda j, place: (j, 0, 0))
    shape = jax.ShapeDtypeStruct((chips, tokens, width), BF16)
    return pl.pallas_call(
        share_kernel,
        grid_spec=pltpu.PrefetchScalarGridSpec(
            num_scalar_prefetch=1,
            grid=(chips,),
            in_specs=[
                pl.BlockSpec((tokens, padded), lambda j, place: (0, 0)),
                pl.BlockSpec((padded, 2 * width), lambda j, place: (0, lax.rem(place[0] + j, chips))),
            ] + [pl.BlockSpec(memory_space=pl.ANY)] * len(after),
            out_specs=[out, out],
        ),
        out_shape=[shape, shape],
        compiler_params=pltpu.CompilerParams(vmem_limit_bytes=VMEM_BYTES),
        cost_estimate=COST,
    )(place, grad, weight, *after)


def lane_pairs(pairs):
    return [(2 * a + core, 2 * b + core) for a, b in pairs for core in (0, 1)]


def send(value, pairs):
    return lax.ppermute(value, "col", lane_pairs(pairs))


def swap_cores(value, chips):
    return lax.ppermute(value, "col", [(i, i ^ 1) for i in range(2 * chips)])


def add(*terms):
    total = terms[0].astype(F32)
    for term in terms[1:]:
        total = total + term.astype(F32)
    return total


class Shares:
    def __init__(self, own, other, chips):
        arrived = swap_cores(other, chips)
        self.shares = [add(own[j], arrived[j]) for j in range(chips)]
        self.chips, self.step, self.up, self.down = chips, 0, None, None

    def hop(self):
        self.step += 1
        s, chips = self.step, self.chips
        up, down = self.shares[chips - s], self.shares[s]
        if s > 1:
            up, down = up + self.up.astype(F32), down + self.down.astype(F32)
        up, down = up.astype(BF16), down.astype(BF16)
        self.up = send(up, [(z, z + 1) for z in range(s)])
        self.down = send(down, [(z, z - 1) for z in range(chips - s, chips)])
        return [up, down]

    def left(self):
        return self.chips - 1 - self.step

    def result(self):
        return add(self.shares[0], self.up, self.down).astype(BF16)


class LowSum:
    def __init__(self, low, chips):
        self.chips, self.low = chips, low
        self.other = swap_cores(low, chips)

    def spread(self):
        self.mine = add(self.low, self.other).astype(BF16)
        chips = self.chips
        self.got = [send(self.mine, [(z, (z + d) % chips) for z in range(chips)]) for d in range(1, chips)]
        return [self.mine]

    def result(self):
        return add(self.mine, *self.got).astype(BF16)


def sum_rows(value):
    rows = lax.axis_size("row")
    if rows & (rows - 1):
        return lax.psum(value, "row").astype(F32)
    bits = [1 << b for b in range(rows.bit_length() - 1)]
    half = value.shape[0] // 2
    pieces = [(value[:half], bits), (value[half:], bits[::-1])]
    sums = []
    for piece, order in pieces:
        for bit in order:
            got = lax.ppermute(piece.astype(BF16), "row", [(i, i ^ bit) for i in range(rows)])
            piece = piece.astype(BF16).astype(F32) + got.astype(F32)
        sums.append(piece)
    return jnp.concatenate(sums, axis=0)


def local(
    tokens_in, token_grad, gate_gain, inner_weight, inner_bias, outer_weight,
    inner_down, inner_up, outer_down, outer_up,
):
    chips = lax.axis_size("col") // 2
    col_index = lax.axis_index("col")
    core = lax.rem(col_index, 2)
    place = jnp.stack([lax.div(col_index, 2), core]).astype(jnp.int32)
    tok_rows, width = token_grad.shape
    features, ff = inner_weight.shape
    rank = inner_down.shape[1]
    padded = -(-(ff + rank) // COLS) * COLS
    scale = 1.0 / math.sqrt(tok_rows * lax.axis_size("row"))

    gain_local = lax.dynamic_slice_in_dim(gate_gain, col_index * width, width, 0)
    total = sum(SPLIT)
    sizes = [tok_rows * part // total for part in SPLIT]
    starts = [sum(sizes[:i]) for i in range(len(sizes))]

    gathered, gated_parts = [], []
    for start, size in zip(starts, sizes):
        gated = (gain_local[None, :] * token_grad[start : start + size].astype(F32)).astype(BF16)
        both = jnp.stack([tokens_in[start : start + size], gated])
        gathered.append(lax.all_gather(both, "col", axis=0))
        gated_parts.append(gated)

    gap = padded - ff - rank
    blank = jnp.zeros((gap, features), BF16)
    inner_cat = jnp.concatenate([inner_weight.T, blank, inner_down.T], axis=0)
    outer_cat = jnp.concatenate([outer_weight.T, blank, outer_up], axis=0)
    bias = jnp.pad(inner_bias, (0, padded - ff))[None, :]
    up_hi = jnp.pad(inner_up, ((LANES - rank, 0), (0, padded - ff)))
    down_hi = jnp.pad(outer_down.T, ((LANES - rank, 0), (0, padded - ff)))
    down_lo = jnp.pad(outer_down.T, ((0, LANES - rank), (0, padded - ff)))

    last = len(sizes) - 1
    moving, lows, grads, early = [], [], None, None
    for index, both in enumerate(gathered):
        after = []
        if index >= 1:
            after += moving[index - 1].hop()
        if index >= 2:
            while moving[index - 2].left():
                after += moving[index - 2].hop()
        if early is not None:
            after += early.spread()
        grad_pre, low, grad = hidden_call(
            both, inner_cat, outer_cat, bias, up_hi, down_lo, down_hi, ff, after
        )
        lows.append(low)
        grads = grad if grads is None else grads + grad
        after = []
        if index >= 1:
            after += moving[index - 1].hop()
        if index == last - 1:
            lows = [jnp.concatenate(lows, axis=0)]
            early = LowSum(lows[0], chips)
            after += lows
            lows = []
        if index == last:
            late = LowSum(low, chips)
            hidden_part = (grads[:, :ff] * scale).astype(BF16)
            after += [low, hidden_part]
        own, other = share_call(place, grad_pre, inner_cat, chips, after)
        moving.append(Shares(own, other, chips))
    late.spread()
    while moving[-1].left():
        if last and moving[-2].left():
            moving[-2].hop()
        moving[-1].hop()
    tokens_grad = jnp.concatenate([shares.result() for shares in moving], axis=0)

    hidden_sums = sum_rows(hidden_part)
    inner_up_grad = hidden_sums[:rank]
    outer_down_grad = hidden_sums[rank:].T

    gated_local = jnp.concatenate(gated_parts, axis=0)
    small = 0.0
    for rows, piece in ((slice(0, starts[last]), early), (slice(starts[last], None), late)):
        low = piece.result()
        small = small + jnp.concatenate(
            [dot_tn(low[:, :rank], gated_local[rows]), dot_tn(low[:, rank:], tokens_in[rows])], axis=0
        )
    small_sums = sum_rows((small * scale).astype(BF16))
    outer_up_grad = small_sums[:rank]
    inner_down_grad = small_sums[rank:].T
    return (tokens_grad, inner_down_grad, inner_up_grad, outer_down_grad, outer_up_grad)


def solution(mesh):
    placed = (
        P("row", "col"),
        P("row", "col"),
        P(),
        P(None, "col"),
        P("col"),
        P(None, "col"),
        P(),
        P(None, "col"),
        P("col", None),
        P(),
    )
    return jax.shard_map(
        local,
        mesh=mesh,
        in_specs=placed,
        out_specs=(P("row", "col"), P("col", None), P(None, "col"), P("col", None), P(None, "col")),
        check_vma=False,
    )
```

```python
import functools
import math

import jax
import jax.numpy as jnp
from jax import lax
from jax.experimental import pallas as pl
from jax.experimental.pallas import tpu as pltpu
from jax.sharding import PartitionSpec as P

SLOPE_SCALE = 0.7978845608028654
CUBIC = 0.044715
F32 = jnp.float32
BF16 = jnp.bfloat16
LANES = 128
COLS = 256
VMEM_BYTES = 52 * 1024 * 1024
COST = pl.CostEstimate(flops=20_000_000_000, bytes_accessed=36_000_000, transcendentals=0)
SPLIT = (320, 448, 256)


def dot_nn(left, right):
    return jnp.dot(left, right, preferred_element_type=F32)


def dot_nt(left, right):
    return lax.dot_general(left, right, (((1,), (1,)), ((), ())), preferred_element_type=F32)


def dot_tn(left, right):
    return lax.dot_general(left, right, (((0,), (0,)), ((), ())), preferred_element_type=F32)


def hidden_kernel(ff, both_ref, inner_ref, outer_ref, bias_ref, up_ref, down_lo_ref, down_hi_ref, *refs):
    grad_ref, low_ref, grads_ref, pre_acc, hid_acc, hidden_ref = refs[-6:]
    step = pl.program_id(0)
    _, _, tokens, width = both_ref.shape
    padded = pre_acc.shape[1]

    def product(which, weight_ref):
        first, second = both_ref[0, which], both_ref[1, which]
        if width % LANES == 0:
            return dot_nt(jnp.concatenate([first, second], axis=1), weight_ref[...])
        return dot_nt(first, weight_ref[:, :width]) + dot_nt(second, weight_ref[:, width:])

    @pl.when(step == 0)
    def _():
        pre_acc[...] = product(0, inner_ref)
        hid_acc[...] = product(1, outer_ref)

    @pl.when(step > 0)
    def _():
        pre_acc[...] += product(0, inner_ref)
        hid_acc[...] += product(1, outer_ref)

    @pl.when(step == pl.num_programs(0) - 1)
    def _():
        tail = slice(padded - LANES, padded)
        inner_low = pre_acc[:, tail].astype(BF16)
        grad_low = hid_acc[:, tail].astype(BF16)
        rank = LANES // 2
        low = jnp.zeros((tokens, LANES), F32)
        for start in range(0, padded, COLS):
            cols = slice(start, start + COLS)
            pre = pre_acc[:, cols] + dot_nn(inner_low, up_ref[:, cols]) + bias_ref[:, cols]
            square = pre * pre
            tangent = jnp.tanh(SLOPE_SCALE * pre * (1.0 + CUBIC * square))
            half = 0.5 + 0.5 * tangent
            hidden = (pre * half).astype(BF16)
            slope = half + 0.5 * pre * (1.0 - tangent * tangent) * (
                SLOPE_SCALE + 3.0 * CUBIC * SLOPE_SCALE * square
            )
            grad_hidden = hid_acc[:, cols] + dot_nn(grad_low, down_hi_ref[:, cols])
            grad_pre = (grad_hidden * slope).astype(BF16)
            hidden_ref[:, cols] = hidden
            grad_ref[:, cols] = grad_pre
        low = dot_nt(hidden_ref[...], down_lo_ref[...]) + dot_nt(grad_ref[...], up_ref[...])
        low = low.astype(BF16)
        low_ref[...] = low
        grads_ref[:rank] = dot_tn(inner_low, grad_ref[...])[rank:]
        grads_ref[rank:] = dot_tn(grad_low, hidden_ref[...])[rank:]
        lane = lax.broadcasted_iota(jnp.int32, (tokens, LANES), 1)
        keep = lane + (padded - LANES) < ff
        filled = jnp.where(lane >= rank, low, jnp.zeros_like(low))
        grad_ref[:, tail] = jnp.where(keep, grad_ref[:, tail], filled)
        for start in range(0, padded - LANES, LANES):
            if start + LANES > ff:
                here = slice(start, start + LANES)
                grad_ref[:, here] = jnp.where(lane + start < ff, grad_ref[:, here], jnp.zeros_like(low))


def hidden_call(both, inner_cat, outer_cat, bias, up, down_lo, down_hi, ff, after=()):
    devices, _, tokens, width = both.shape
    padded = inner_cat.shape[0]
    steps = devices // 2
    whole = lambda k: (0, 0)
    return pl.pallas_call(
        functools.partial(hidden_kernel, ff),
        grid=(steps,),
        in_specs=[
            pl.BlockSpec((2, 2, tokens, width), lambda k: (k, 0, 0, 0)),
            pl.BlockSpec((padded, 2 * width), lambda k: (0, k)),
            pl.BlockSpec((padded, 2 * width), lambda k: (0, k)),
            pl.BlockSpec((1, padded), whole),
            pl.BlockSpec((LANES, padded), whole),
            pl.BlockSpec((LANES, padded), whole),
            pl.BlockSpec((LANES, padded), whole),
        ] + [pl.BlockSpec(memory_space=pl.ANY)] * len(after),
        out_specs=[
            pl.BlockSpec((tokens, padded), whole),
            pl.BlockSpec((tokens, LANES), whole),
            pl.BlockSpec((LANES, padded), whole),
        ],
        out_shape=[
            jax.ShapeDtypeStruct((tokens, padded), BF16),
            jax.ShapeDtypeStruct((tokens, LANES), BF16),
            jax.ShapeDtypeStruct((LANES, padded), F32),
        ],
        scratch_shapes=[
            pltpu.VMEM((tokens, padded), F32),
            pltpu.VMEM((tokens, padded), F32),
            pltpu.VMEM((tokens, padded), BF16),
        ],
        compiler_params=pltpu.CompilerParams(vmem_limit_bytes=VMEM_BYTES),
        cost_estimate=COST,
    )(both, inner_cat, outer_cat, bias, up, down_lo, down_hi, *after)


def share_kernel(place_ref, grad_ref, weight_ref, low_ref, scale_ref, *refs):
    own_ref, other_ref, low_out_ref, scale_out_ref = refs[-4:]
    low_out_ref[...] = low_ref[...]
    scale_out_ref[...] = scale_ref[...]
    width = own_ref.shape[2]
    if width % LANES == 0:
        share = dot_nn(grad_ref[...], weight_ref[...]).astype(BF16)
        first, second = share[:, :width], share[:, width:]
    else:
        first = dot_nn(grad_ref[...], weight_ref[:, :width]).astype(BF16)
        second = dot_nn(grad_ref[...], weight_ref[:, width:]).astype(BF16)

    @pl.when(place_ref[1] == 0)
    def _():
        own_ref[0] = first
        other_ref[0] = second

    @pl.when(place_ref[1] != 0)
    def _():
        own_ref[0] = second
        other_ref[0] = first


def share_call(place, grad, weight, low, scale, chips, after=()):
    tokens, padded = grad.shape
    width = weight.shape[1] // (2 * chips)
    out = pl.BlockSpec((1, tokens, width), lambda j, place: (j, 0, 0))
    shape = jax.ShapeDtypeStruct((chips, tokens, width), BF16)
    whole = lambda value: pl.BlockSpec(value.shape, lambda j, place: (0, 0))
    return pl.pallas_call(
        share_kernel,
        grid_spec=pltpu.PrefetchScalarGridSpec(
            num_scalar_prefetch=1,
            grid=(chips,),
            in_specs=[
                pl.BlockSpec((tokens, padded), lambda j, place: (0, 0)),
                pl.BlockSpec((padded, 2 * width), lambda j, place: (0, lax.rem(place[0] + j, chips))),
                whole(low),
                whole(scale),
            ] + [pl.BlockSpec(memory_space=pl.ANY)] * len(after),
            out_specs=[out, out, whole(low), whole(scale)],
        ),
        out_shape=[shape, shape]
        + [jax.ShapeDtypeStruct(value.shape, value.dtype) for value in (low, scale)],
        compiler_params=pltpu.CompilerParams(vmem_limit_bytes=VMEM_BYTES),
        cost_estimate=COST,
    )(place, grad, weight, low, scale, *after)


def lane_pairs(pairs):
    return [(2 * a + core, 2 * b + core) for a, b in pairs for core in (0, 1)]


def send(value, pairs):
    return lax.ppermute(value, "col", lane_pairs(pairs))


def swap_cores(value, chips):
    return lax.ppermute(value, "col", [(i, i ^ 1) for i in range(2 * chips)])


def add(*terms):
    total = terms[0].astype(F32)
    for term in terms[1:]:
        total = total + term.astype(F32)
    return total


class Shares:
    def __init__(self, own, other, chips):
        arrived = swap_cores(other, chips)
        self.shares = [add(own[j], arrived[j]) for j in range(chips)]
        self.chips, self.step, self.up, self.down = chips, 0, None, None

    def hop(self):
        self.step += 1
        s, chips = self.step, self.chips
        up, down = self.shares[chips - s], self.shares[s]
        if s > 1:
            up, down = up + self.up.astype(F32), down + self.down.astype(F32)
        up, down = up.astype(BF16), down.astype(BF16)
        self.up = send(up, [(z, z + 1) for z in range(s)])
        self.down = send(down, [(z, z - 1) for z in range(chips - s, chips)])
        return [up, down]

    def left(self):
        return self.chips - 1 - self.step

    def result(self):
        return add(self.shares[0], self.up, self.down).astype(BF16)


class LowSum:
    def __init__(self, low, chips):
        self.chips, self.low = chips, low
        self.other = swap_cores(low, chips)

    def spread(self):
        self.mine = add(self.low, self.other).astype(BF16)
        chips = self.chips
        self.got = [send(self.mine, [(z, (z + d) % chips) for z in range(chips)]) for d in range(1, chips)]
        return [self.mine]

    def result(self):
        return add(self.mine, *self.got).astype(BF16)


def sum_rows(value):
    rows = lax.axis_size("row")
    if rows & (rows - 1):
        return lax.psum(value, "row").astype(F32)
    bits = [1 << b for b in range(rows.bit_length() - 1)]
    half = value.shape[0] // 2
    pieces = [(value[:half], bits), (value[half:], bits[::-1])]
    sums = []
    for piece, order in pieces:
        for bit in order:
            got = lax.ppermute(piece.astype(BF16), "row", [(i, i ^ bit) for i in range(rows)])
            piece = piece.astype(BF16).astype(F32) + got.astype(F32)
        sums.append(piece)
    return jnp.concatenate(sums, axis=0)


def local(
    tokens_in, token_grad, gate_gain, inner_weight, inner_bias, outer_weight,
    inner_down, inner_up, outer_down, outer_up,
):
    chips = lax.axis_size("col") // 2
    col_index = lax.axis_index("col")
    core = lax.rem(col_index, 2)
    place = jnp.stack([lax.div(col_index, 2), core]).astype(jnp.int32)
    tok_rows, width = token_grad.shape
    features, ff = inner_weight.shape
    rank = inner_down.shape[1]
    padded = -(-(ff + rank) // COLS) * COLS
    scale = 1.0 / math.sqrt(tok_rows * lax.axis_size("row"))

    gain_local = lax.dynamic_slice_in_dim(gate_gain, col_index * width, width, 0)
    total = sum(SPLIT)
    sizes = [tok_rows * part // total for part in SPLIT]
    starts = [sum(sizes[:i]) for i in range(len(sizes))]

    gathered, gated_parts = [], []
    for start, size in zip(starts, sizes):
        gated = (gain_local[None, :] * token_grad[start : start + size].astype(F32)).astype(BF16)
        both = jnp.stack([tokens_in[start : start + size], gated])
        gathered.append(lax.all_gather(both, "col", axis=0))
        gated_parts.append(gated)

    gap = padded - ff - rank
    blank = jnp.zeros((gap, features), BF16)
    inner_cat = jnp.concatenate([inner_weight.T, blank, inner_down.T], axis=0)
    outer_cat = jnp.concatenate([outer_weight.T, blank, outer_up], axis=0)
    bias = jnp.pad(inner_bias, (0, padded - ff))[None, :]
    up_hi = jnp.pad(inner_up, ((LANES - rank, 0), (0, padded - ff)))
    down_hi = jnp.pad(outer_down.T, ((LANES - rank, 0), (0, padded - ff)))
    down_lo = jnp.pad(outer_down.T, ((0, LANES - rank), (0, padded - ff)))

    last = len(sizes) - 1
    moving, outs, lows, grads, early = [], [], [], None, None
    scales = jnp.full((1, LANES), scale, F32)
    for index, both in enumerate(gathered):
        after = []
        if index >= 1:
            while moving[-1].left() > (2 if index == last else 0):
                after += moving[-1].hop()
            if index < last:
                outs.append(moving[-1].result())
                after = [outs[-1]]
        if early is not None:
            after += early.spread()
        grad_pre, low, grad = hidden_call(
            both, inner_cat, outer_cat, bias, up_hi, down_lo, down_hi, ff, after
        )
        grads = grad if grads is None else grads + grad
        after = []
        if index >= 1 and moving[-1].left() > 1:
            after += moving[-1].hop()
        own, other, low, scale_after = share_call(place, grad_pre, inner_cat, low, scales, chips, after)
        lows.append(low)
        moving.append(Shares(own, other, chips))
        if index == last - 1:
            early = LowSum(jnp.concatenate(lows, axis=0), chips)
        if index == last:
            late = LowSum(low, chips)
            hidden_part = (grads[:, :ff] * scale_after[0, 0]).astype(BF16)
    late.spread()
    while moving[-1].left():
        if last and moving[-2].left():
            moving[-2].hop()
        moving[-1].hop()
    outs += [shares.result() for shares in moving[len(outs) :]]
    tokens_grad = jnp.concatenate(outs, axis=0)

    hidden_sums = sum_rows(hidden_part)
    inner_up_grad = hidden_sums[:rank]
    outer_down_grad = hidden_sums[rank:].T

    gated_local = jnp.concatenate(gated_parts, axis=0)
    small = 0.0
    for rows, piece in ((slice(0, starts[last]), early), (slice(starts[last], None), late)):
        low = piece.result()
        small = small + jnp.concatenate(
            [dot_tn(low[:, :rank], gated_local[rows]), dot_tn(low[:, rank:], tokens_in[rows])], axis=0
        )
    small_sums = sum_rows((small * scale).astype(BF16))
    outer_up_grad = small_sums[:rank]
    inner_down_grad = small_sums[rank:].T
    return (tokens_grad, inner_down_grad, inner_up_grad, outer_down_grad, outer_up_grad)


def solution(mesh):
    placed = (
        P("row", "col"),
        P("row", "col"),
        P(),
        P(None, "col"),
        P("col"),
        P(None, "col"),
        P(),
        P(None, "col"),
        P("col", None),
        P(),
    )
    return jax.shard_map(
        local,
        mesh=mesh,
        in_specs=placed,
        out_specs=(P("row", "col"), P("col", None), P(None, "col"), P("col", None), P(None, "col")),
        check_vma=False,
    )
```

```python
import functools
import math

import jax
import jax.numpy as jnp
from jax import lax
from jax.experimental import pallas as pl
from jax.experimental.pallas import tpu as pltpu
from jax.sharding import PartitionSpec as P

SLOPE_SCALE = 0.7978845608028654
CUBIC = 0.044715
F32 = jnp.float32
BF16 = jnp.bfloat16
LANES = 128
COLS = 256
VMEM_BYTES = 52 * 1024 * 1024
COST = pl.CostEstimate(flops=20_000_000_000, bytes_accessed=36_000_000, transcendentals=0)
SPLIT = (224, 352, 288, 160)


def dot_nn(left, right):
    return jnp.dot(left, right, preferred_element_type=F32)


def dot_nt(left, right):
    return lax.dot_general(left, right, (((1,), (1,)), ((), ())), preferred_element_type=F32)


def dot_tn(left, right):
    return lax.dot_general(left, right, (((0,), (0,)), ((), ())), preferred_element_type=F32)


def hidden_kernel(
    ff, both_ref, inner_ref, outer_ref, bias_ref, up_ref, down_lo_ref, down_hi_ref, tick_ref, *refs
):
    grad_ref, low_ref, grads_ref, tick_out_ref, pre_acc, hid_acc, hidden_ref = refs[-7:]
    tick_out_ref[...] = tick_ref[...]
    step = pl.program_id(0)
    _, _, tokens, width = both_ref.shape
    padded = pre_acc.shape[1]

    def product(which, weight_ref):
        first, second = both_ref[0, which], both_ref[1, which]
        if width % LANES == 0:
            return dot_nt(jnp.concatenate([first, second], axis=1), weight_ref[...])
        return dot_nt(first, weight_ref[:, :width]) + dot_nt(second, weight_ref[:, width:])

    @pl.when(step == 0)
    def _():
        pre_acc[...] = product(0, inner_ref)
        hid_acc[...] = product(1, outer_ref)

    @pl.when(step > 0)
    def _():
        pre_acc[...] += product(0, inner_ref)
        hid_acc[...] += product(1, outer_ref)

    @pl.when(step == pl.num_programs(0) - 1)
    def _():
        tail = slice(padded - LANES, padded)
        inner_low = pre_acc[:, tail].astype(BF16)
        grad_low = hid_acc[:, tail].astype(BF16)
        rank = LANES // 2
        low = jnp.zeros((tokens, LANES), F32)
        for start in range(0, padded, COLS):
            cols = slice(start, start + COLS)
            pre = pre_acc[:, cols] + dot_nn(inner_low, up_ref[:, cols]) + bias_ref[:, cols]
            square = pre * pre
            tangent = jnp.tanh(SLOPE_SCALE * pre * (1.0 + CUBIC * square))
            half = 0.5 + 0.5 * tangent
            hidden = (pre * half).astype(BF16)
            slope = half + 0.5 * pre * (1.0 - tangent * tangent) * (
                SLOPE_SCALE + 3.0 * CUBIC * SLOPE_SCALE * square
            )
            grad_hidden = hid_acc[:, cols] + dot_nn(grad_low, down_hi_ref[:, cols])
            grad_pre = (grad_hidden * slope).astype(BF16)
            hidden_ref[:, cols] = hidden
            grad_ref[:, cols] = grad_pre
        low = dot_nt(hidden_ref[...], down_lo_ref[...]) + dot_nt(grad_ref[...], up_ref[...])
        low = low.astype(BF16)
        low_ref[...] = low
        grads_ref[:rank] = dot_tn(inner_low, grad_ref[...])[rank:]
        grads_ref[rank:] = dot_tn(grad_low, hidden_ref[...])[rank:]
        lane = lax.broadcasted_iota(jnp.int32, (tokens, LANES), 1)
        keep = lane + (padded - LANES) < ff
        filled = jnp.where(lane >= rank, low, jnp.zeros_like(low))
        grad_ref[:, tail] = jnp.where(keep, grad_ref[:, tail], filled)
        for start in range(0, padded - LANES, LANES):
            if start + LANES > ff:
                here = slice(start, start + LANES)
                grad_ref[:, here] = jnp.where(lane + start < ff, grad_ref[:, here], jnp.zeros_like(low))


def hidden_call(both, inner_cat, outer_cat, bias, up, down_lo, down_hi, tick, ff, after=()):
    devices, _, tokens, width = both.shape
    padded = inner_cat.shape[0]
    steps = devices // 2
    whole = lambda k: (0, 0)
    return pl.pallas_call(
        functools.partial(hidden_kernel, ff),
        grid=(steps,),
        in_specs=[
            pl.BlockSpec((2, 2, tokens, width), lambda k: (k, 0, 0, 0)),
            pl.BlockSpec((padded, 2 * width), lambda k: (0, k)),
            pl.BlockSpec((padded, 2 * width), lambda k: (0, k)),
            pl.BlockSpec((1, padded), whole),
            pl.BlockSpec((LANES, padded), whole),
            pl.BlockSpec((LANES, padded), whole),
            pl.BlockSpec((LANES, padded), whole),
            pl.BlockSpec(tick.shape, whole),
        ] + [pl.BlockSpec(memory_space=pl.ANY)] * len(after),
        out_specs=[
            pl.BlockSpec((tokens, padded), whole),
            pl.BlockSpec((tokens, LANES), whole),
            pl.BlockSpec((LANES, padded), whole),
            pl.BlockSpec(tick.shape, whole),
        ],
        out_shape=[
            jax.ShapeDtypeStruct((tokens, padded), BF16),
            jax.ShapeDtypeStruct((tokens, LANES), BF16),
            jax.ShapeDtypeStruct((LANES, padded), F32),
            jax.ShapeDtypeStruct(tick.shape, tick.dtype),
        ],
        scratch_shapes=[
            pltpu.VMEM((tokens, padded), F32),
            pltpu.VMEM((tokens, padded), F32),
            pltpu.VMEM((tokens, padded), BF16),
        ],
        compiler_params=pltpu.CompilerParams(vmem_limit_bytes=VMEM_BYTES),
        cost_estimate=COST,
    )(both, inner_cat, outer_cat, bias, up, down_lo, down_hi, tick, *after)


def share_kernel(scale, carried, emit, place_ref, grad_ref, weight_ref, low_ref, both_ref, tick_ref, *refs):
    outs = refs[-3:] if emit else refs[-5:]
    own_ref, other_ref, tick_out_ref = outs[0], outs[1], outs[-1]
    carry_out = outs[2:4]
    tokens, width = both_ref.shape[2], own_ref.shape[2]
    rank = LANES // 2
    tick_out_ref[...] = tick_ref[...]

    if width % LANES == 0:
        share = dot_nn(grad_ref[...], weight_ref[...]).astype(BF16)
        shares = share[:, :width], share[:, width:]
    else:
        shares = [
            dot_nn(grad_ref[...], weight_ref[:, part * width : (part + 1) * width]).astype(BF16)
            for part in (0, 1)
        ]
    hidden_low, pre_low = low_ref[:, :rank], low_ref[:, rank:]

    def put(part, share_ref, carry_ref, carry_in_ref):
        share_ref[0, :tokens] = shares[part]
        for rows, left, which in ((slice(0, rank), hidden_low, 1), (slice(rank, LANES), pre_low, 0)):
            value = dot_tn(left, both_ref[part, which])
            if carried:
                value = value + carry_in_ref[0, rows]
            if emit:
                begin = tokens + rows.start
                share_ref[0, begin : begin + rank] = (value * scale).astype(BF16)
            else:
                carry_ref[0, rows] = value

    def put_both(first):
        second = 1 - first
        put(first, own_ref, None if emit else carry_out[0], refs[0])
        put(second, other_ref, None if emit else carry_out[1], refs[1])

    @pl.when(place_ref[1] == 0)
    def _():
        put_both(0)

    @pl.when(place_ref[1] != 0)
    def _():
        put_both(1)


def share_call(place, grad, weight, low, both, tick, chips, scale, carry, emit, after=()):
    tokens, padded = grad.shape
    width = weight.shape[1] // (2 * chips)
    rows = tokens + LANES if emit else tokens
    there = lambda j, place: lax.rem(place[0] + j, chips)
    whole = lambda value: pl.BlockSpec(value.shape, lambda j, place: (0, 0))
    block = lambda rows: pl.BlockSpec((1, rows, width), lambda j, place: (j, 0, 0))
    out_specs, out_shape = [block(rows)] * 2, [jax.ShapeDtypeStruct((chips, rows, width), BF16)] * 2
    if not emit:
        out_specs += [block(LANES)] * 2
        out_shape += [jax.ShapeDtypeStruct((chips, LANES, width), F32)] * 2
    outs = pl.pallas_call(
        functools.partial(share_kernel, scale, bool(carry), emit),
        grid_spec=pltpu.PrefetchScalarGridSpec(
            num_scalar_prefetch=1,
            grid=(chips,),
            in_specs=[
                whole(grad),
                pl.BlockSpec((padded, 2 * width), lambda j, place: (0, there(j, place))),
                whole(low),
                pl.BlockSpec((2, 2, tokens, width), lambda j, place: (there(j, place), 0, 0, 0)),
                whole(tick),
            ]
            + [block(LANES)] * len(carry)
            + [pl.BlockSpec(memory_space=pl.ANY)] * len(after),
            out_specs=out_specs + [whole(tick)],
        ),
        out_shape=out_shape + [jax.ShapeDtypeStruct(tick.shape, tick.dtype)],
        compiler_params=pltpu.CompilerParams(vmem_limit_bytes=VMEM_BYTES),
        cost_estimate=COST,
    )(place, grad, weight, low, both, tick, *carry, *after)
    return outs[0], outs[1], outs[2:-1], outs[-1]


def gate(value, after):
    anywhere = pl.BlockSpec(memory_space=pl.ANY)
    return pl.pallas_call(
        lambda *refs: None,
        in_specs=[anywhere] * (1 + len(after)),
        out_specs=anywhere,
        out_shape=jax.ShapeDtypeStruct(value.shape, value.dtype),
        input_output_aliases={0: 0},
    )(value, *after)


def lane_pairs(pairs):
    return [(2 * a + core, 2 * b + core) for a, b in pairs for core in (0, 1)]


def send(value, pairs):
    return lax.ppermute(value, "col", lane_pairs(pairs))


def swap_cores(value, chips):
    return lax.ppermute(value, "col", [(i, i ^ 1) for i in range(2 * chips)])


def add(*terms):
    total = terms[0].astype(F32)
    for term in terms[1:]:
        total = total + term.astype(F32)
    return total


class Shares:
    def __init__(self, own, other, chips):
        arrived = swap_cores(other, chips)
        self.shares = [add(own[j], arrived[j]) for j in range(chips)]
        self.chips, self.step, self.up, self.down = chips, 0, None, None

    def hop(self, tick):
        self.step += 1
        s, chips = self.step, self.chips
        up, down = self.shares[chips - s], self.shares[s]
        if s > 1:
            up, down = up + self.up.astype(F32) * tick[0, 0], down + self.down.astype(F32) * tick[0, 0]
        up, down = up.astype(BF16), down.astype(BF16)
        self.up = send(up, [(z, z + 1) for z in range(s)])
        self.down = send(down, [(z, z - 1) for z in range(chips - s, chips)])
        return [up, down]

    def left(self):
        return self.chips - 1 - self.step

    def result(self, tick):
        return self.shares[0] + (self.up.astype(F32) + self.down.astype(F32)) * tick[0, 0]


def sum_rows(value):
    rows = lax.axis_size("row")
    if rows & (rows - 1):
        return lax.psum(value, "row").astype(F32)
    bits = [1 << b for b in range(rows.bit_length() - 1)]
    half = value.shape[0] // 2
    pieces = [(value[:half], bits), (value[half:], bits[::-1])]
    sums = []
    for piece, order in pieces:
        for bit in order:
            got = lax.ppermute(piece.astype(BF16), "row", [(i, i ^ bit) for i in range(rows)])
            piece = piece.astype(BF16).astype(F32) + got.astype(F32)
        sums.append(piece)
    return jnp.concatenate(sums, axis=0)


def sum_rows_at_once(value):
    rows = lax.axis_size("row")
    if rows & (rows - 1):
        return lax.psum(value, "row").astype(F32)
    terms = [value] + [
        lax.ppermute(value, "row", [(i, i ^ other) for i in range(rows)]) for other in range(1, rows)
    ]
    terms = [term.astype(F32) for term in terms]
    while len(terms) > 1:
        terms = [terms[i] + terms[i + 1] for i in range(0, len(terms), 2)]
    return terms[0]


def local(
    tokens_in, token_grad, gate_gain, inner_weight, inner_bias, outer_weight,
    inner_down, inner_up, outer_down, outer_up,
):
    chips = lax.axis_size("col") // 2
    col_index = lax.axis_index("col")
    core = lax.rem(col_index, 2)
    place = jnp.stack([lax.div(col_index, 2), core]).astype(jnp.int32)
    tok_rows, width = token_grad.shape
    features, ff = inner_weight.shape
    rank = inner_down.shape[1]
    padded = -(-(ff + rank) // COLS) * COLS
    scale = 1.0 / math.sqrt(tok_rows * lax.axis_size("row"))

    gain_local = lax.dynamic_slice_in_dim(gate_gain, col_index * width, width, 0)
    sizes = [tok_rows * part // sum(SPLIT) for part in SPLIT]
    starts = [sum(sizes[:i]) for i in range(len(sizes))]

    gathered = []
    for start, size in zip(starts, sizes):
        gated = (gain_local[None, :] * token_grad[start : start + size].astype(F32)).astype(BF16)
        both = jnp.stack([tokens_in[start : start + size], gated])
        gathered.append(lax.all_gather(both, "col", axis=0))

    gap = padded - ff - rank
    blank = jnp.zeros((gap, features), BF16)
    inner_cat = jnp.concatenate([inner_weight.T, blank, inner_down.T], axis=0)
    outer_cat = jnp.concatenate([outer_weight.T, blank, outer_up], axis=0)
    bias = jnp.pad(inner_bias, (0, padded - ff))[None, :]
    up_hi = jnp.pad(inner_up, ((LANES - rank, 0), (0, padded - ff)))
    down_hi = jnp.pad(outer_down.T, ((LANES - rank, 0), (0, padded - ff)))
    down_lo = jnp.pad(outer_down.T, ((0, LANES - rank), (0, padded - ff)))

    last = len(sizes) - 1
    moving, sums, grads, carry = [], [], None, ()
    tick = jnp.ones((1, LANES), F32)
    for index, both in enumerate(gathered):
        before = moving[-1] if moving else None
        after = before.hop(tick) if before else []
        grad_pre, low, grad, tick = hidden_call(
            both, inner_cat, outer_cat, bias, up_hi, down_lo, down_hi, tick, ff, after
        )
        grads = grad if grads is None else grads + grad
        after = []
        if before:
            after += before.hop(tick)
        if index >= 2:
            sums.append(moving[index - 2].result(tick))
            after.append(sums[-1])
        own, other, carry, tick = share_call(
            place, grad_pre, inner_cat, low, both, tick, chips, scale, carry, index == last, after
        )
        if before:
            after = []
            while before.left():
                after += before.hop(tick)
            other = gate(other, after)
        moving.append(Shares(own, other, chips))
    hidden_part = (grads[:, :ff] * (scale * tick[0, 0])).astype(BF16)
    moving[-1].hop(tick)
    if last:
        sums.append(moving[-2].result(tick))
        moving[-1].up = gate(moving[-1].up, sums[-1:])
    while moving[-1].left():
        moving[-1].hop(tick)
    sums.append(moving[-1].result(tick))
    tokens_grad = jnp.concatenate([value[:size] for value, size in zip(sums, sizes)], axis=0).astype(BF16)

    hidden_sums = sum_rows(hidden_part)
    inner_up_grad = hidden_sums[:rank]
    outer_down_grad = hidden_sums[rank:].T

    feature_part = add(*[value[size:] for value, size in zip(sums, sizes) if value.shape[0] > size])
    feature_sums = sum_rows_at_once(feature_part.astype(BF16))
    outer_up_grad = feature_sums[:rank]
    inner_down_grad = feature_sums[rank:].T
    return (tokens_grad, inner_down_grad, inner_up_grad, outer_down_grad, outer_up_grad)


def solution(mesh):
    placed = (
        P("row", "col"),
        P("row", "col"),
        P(),
        P(None, "col"),
        P("col"),
        P(None, "col"),
        P(),
        P(None, "col"),
        P("col", None),
        P(),
    )
    return jax.shard_map(
        local,
        mesh=mesh,
        in_specs=placed,
        out_specs=(P("row", "col"), P("col", None), P(None, "col"), P("col", None), P(None, "col")),
        check_vma=False,
    )
```

```python
import functools
import math

import jax
import jax.numpy as jnp
from jax import lax
from jax.experimental import pallas as pl
from jax.experimental.pallas import tpu as pltpu
from jax.sharding import PartitionSpec as P

SLOPE_SCALE = 0.7978845608028654
CUBIC = 0.044715
F32 = jnp.float32
BF16 = jnp.bfloat16
LANES = 128
COLS = 256
VMEM_BYTES = 52 * 1024 * 1024
COST = pl.CostEstimate(flops=20_000_000_000, bytes_accessed=36_000_000, transcendentals=0)
SPLIT = (512, 512)


def dot_nn(left, right):
    return jnp.dot(left, right, preferred_element_type=F32)


def dot_nt(left, right):
    return lax.dot_general(left, right, (((1,), (1,)), ((), ())), preferred_element_type=F32)


def dot_tn(left, right):
    return lax.dot_general(left, right, (((0,), (0,)), ((), ())), preferred_element_type=F32)


def hidden_kernel(
    ff, both_ref, inner_ref, outer_ref, bias_ref, up_ref, down_lo_ref, down_hi_ref,
    grad_ref, low_ref, grads_ref, pre_acc, hid_acc, hidden_ref,
):
    step = pl.program_id(0)
    _, _, tokens, width = both_ref.shape
    padded = pre_acc.shape[1]

    def product(which, weight_ref):
        first, second = both_ref[0, which], both_ref[1, which]
        if width % LANES == 0:
            return dot_nt(jnp.concatenate([first, second], axis=1), weight_ref[...])
        return dot_nt(first, weight_ref[:, :width]) + dot_nt(second, weight_ref[:, width:])

    @pl.when(step == 0)
    def _():
        pre_acc[...] = product(0, inner_ref)
        hid_acc[...] = product(1, outer_ref)

    @pl.when(step > 0)
    def _():
        pre_acc[...] += product(0, inner_ref)
        hid_acc[...] += product(1, outer_ref)

    @pl.when(step == pl.num_programs(0) - 1)
    def _():
        tail = slice(padded - LANES, padded)
        inner_low = pre_acc[:, tail].astype(BF16)
        grad_low = hid_acc[:, tail].astype(BF16)
        rank = LANES // 2
        low = jnp.zeros((tokens, LANES), F32)
        for start in range(0, padded, COLS):
            cols = slice(start, start + COLS)
            pre = pre_acc[:, cols] + dot_nn(inner_low, up_ref[:, cols]) + bias_ref[:, cols]
            square = pre * pre
            tangent = jnp.tanh(SLOPE_SCALE * pre * (1.0 + CUBIC * square))
            half = 0.5 + 0.5 * tangent
            hidden = (pre * half).astype(BF16)
            slope = half + 0.5 * pre * (1.0 - tangent * tangent) * (
                SLOPE_SCALE + 3.0 * CUBIC * SLOPE_SCALE * square
            )
            grad_hidden = hid_acc[:, cols] + dot_nn(grad_low, down_hi_ref[:, cols])
            grad_pre = (grad_hidden * slope).astype(BF16)
            hidden_ref[:, cols] = hidden
            grad_ref[:, cols] = grad_pre
        low = dot_nt(hidden_ref[...], down_lo_ref[...]) + dot_nt(grad_ref[...], up_ref[...])
        low = low.astype(BF16)
        low_ref[...] = low
        grads_ref[:rank] = dot_tn(inner_low, grad_ref[...])[rank:]
        grads_ref[rank:] = dot_tn(grad_low, hidden_ref[...])[rank:]
        lane = lax.broadcasted_iota(jnp.int32, (tokens, LANES), 1)
        keep = lane + (padded - LANES) < ff
        filled = jnp.where(lane >= rank, low, jnp.zeros_like(low))
        grad_ref[:, tail] = jnp.where(keep, grad_ref[:, tail], filled)
        for start in range(0, padded - LANES, LANES):
            if start + LANES > ff:
                here = slice(start, start + LANES)
                grad_ref[:, here] = jnp.where(lane + start < ff, grad_ref[:, here], jnp.zeros_like(low))


def hidden_call(both, inner_cat, outer_cat, bias, up, down_lo, down_hi, ff):
    devices, _, tokens, width = both.shape
    padded = inner_cat.shape[0]
    steps = devices // 2
    whole = lambda k: (0, 0)
    return pl.pallas_call(
        functools.partial(hidden_kernel, ff),
        grid=(steps,),
        in_specs=[
            pl.BlockSpec((2, 2, tokens, width), lambda k: (k, 0, 0, 0)),
            pl.BlockSpec((padded, 2 * width), lambda k: (0, k)),
            pl.BlockSpec((padded, 2 * width), lambda k: (0, k)),
            pl.BlockSpec((1, padded), whole),
            pl.BlockSpec((LANES, padded), whole),
            pl.BlockSpec((LANES, padded), whole),
            pl.BlockSpec((LANES, padded), whole),
        ],
        out_specs=[
            pl.BlockSpec((tokens, padded), whole),
            pl.BlockSpec((tokens, LANES), whole),
            pl.BlockSpec((LANES, padded), whole),
        ],
        out_shape=[
            jax.ShapeDtypeStruct((tokens, padded), BF16),
            jax.ShapeDtypeStruct((tokens, LANES), BF16),
            jax.ShapeDtypeStruct((LANES, padded), F32),
        ],
        scratch_shapes=[
            pltpu.VMEM((tokens, padded), F32),
            pltpu.VMEM((tokens, padded), F32),
            pltpu.VMEM((tokens, padded), BF16),
        ],
        compiler_params=pltpu.CompilerParams(vmem_limit_bytes=VMEM_BYTES),
        cost_estimate=COST,
    )(both, inner_cat, outer_cat, bias, up, down_lo, down_hi)


def share_kernel(grad_ref, weight_ref, share_ref):
    width = share_ref.shape[2]
    if width % LANES == 0:
        share = dot_nn(grad_ref[...], weight_ref[...]).astype(BF16)
        share_ref[0], share_ref[1] = share[:, :width], share[:, width:]
    else:
        for part in (0, 1):
            here = slice(part * width, (part + 1) * width)
            share_ref[part] = dot_nn(grad_ref[...], weight_ref[:, here]).astype(BF16)


def share_call(grad, weight, devices):
    tokens, padded = grad.shape
    width = weight.shape[1] // devices
    return pl.pallas_call(
        share_kernel,
        grid=(devices // 2,),
        in_specs=[
            pl.BlockSpec((tokens, padded), lambda j: (0, 0)),
            pl.BlockSpec((padded, 2 * width), lambda j: (0, j)),
        ],
        out_specs=pl.BlockSpec((2, tokens, width), lambda j: (j, 0, 0)),
        out_shape=jax.ShapeDtypeStruct((devices, tokens, width), BF16),
        compiler_params=pltpu.CompilerParams(vmem_limit_bytes=VMEM_BYTES),
        cost_estimate=COST,
    )(grad, weight)


def lane_pairs(pairs):
    return [(2 * a + core, 2 * b + core) for a, b in pairs for core in (0, 1)]


def send(value, pairs):
    return lax.ppermute(value, "col", lane_pairs(pairs))


def swap_cores(value, chips):
    return lax.ppermute(value, "col", [(i, i ^ 1) for i in range(2 * chips)])


def add(*terms):
    total = terms[0].astype(F32)
    for term in terms[1:]:
        total = total + term.astype(F32)
    return total


class LowSum:
    def __init__(self, low, chips):
        self.chips, self.low = chips, low
        self.other = swap_cores(low, chips)

    def spread(self):
        self.mine = add(self.low, self.other).astype(BF16)
        chips = self.chips
        self.got = [send(self.mine, [(z, (z + d) % chips) for z in range(chips)]) for d in range(1, chips)]
        return [self.mine]

    def result(self):
        return add(self.mine, *self.got).astype(BF16)


def sum_rows(value):
    rows = lax.axis_size("row")
    if rows & (rows - 1):
        return lax.psum(value, "row").astype(F32)
    bits = [1 << b for b in range(rows.bit_length() - 1)]
    half = value.shape[0] // 2
    pieces = [(value[:half], bits), (value[half:], bits[::-1])]
    sums = []
    for piece, order in pieces:
        for bit in order:
            got = lax.ppermute(piece.astype(BF16), "row", [(i, i ^ bit) for i in range(rows)])
            piece = piece.astype(BF16).astype(F32) + got.astype(F32)
        sums.append(piece)
    return jnp.concatenate(sums, axis=0)


def sum_rows_at_once(value):
    rows = lax.axis_size("row")
    if rows & (rows - 1):
        return lax.psum(value, "row").astype(F32)
    terms = [value] + [
        lax.ppermute(value, "row", [(i, i ^ other) for i in range(rows)]) for other in range(1, rows)
    ]
    terms = [term.astype(F32) for term in terms]
    while len(terms) > 1:
        terms = [terms[i] + terms[i + 1] for i in range(0, len(terms), 2)]
    return terms[0]


def local(
    tokens_in, token_grad, gate_gain, inner_weight, inner_bias, outer_weight,
    inner_down, inner_up, outer_down, outer_up,
):
    chips = lax.axis_size("col") // 2
    col_index = lax.axis_index("col")
    tok_rows, width = token_grad.shape
    features, ff = inner_weight.shape
    rank = inner_down.shape[1]
    padded = -(-(ff + rank) // COLS) * COLS
    scale = 1.0 / math.sqrt(tok_rows * lax.axis_size("row"))

    gain_local = lax.dynamic_slice_in_dim(gate_gain, col_index * width, width, 0)
    sizes = [tok_rows * part // sum(SPLIT) for part in SPLIT]
    starts = [sum(sizes[:i]) for i in range(len(sizes))]

    gathered, gated_parts = [], []
    for start, size in zip(starts, sizes):
        gated = (gain_local[None, :] * token_grad[start : start + size].astype(F32)).astype(BF16)
        both = jnp.stack([tokens_in[start : start + size], gated])
        gathered.append(lax.all_gather(both, "col", axis=0))
        gated_parts.append(gated)

    gap = padded - ff - rank
    blank = jnp.zeros((gap, features), BF16)
    inner_cat = jnp.concatenate([inner_weight.T, blank, inner_down.T], axis=0)
    outer_cat = jnp.concatenate([outer_weight.T, blank, outer_up], axis=0)
    bias = jnp.pad(inner_bias, (0, padded - ff))[None, :]
    up_hi = jnp.pad(inner_up, ((LANES - rank, 0), (0, padded - ff)))
    down_hi = jnp.pad(outer_down.T, ((LANES - rank, 0), (0, padded - ff)))
    down_lo = jnp.pad(outer_down.T, ((0, LANES - rank), (0, padded - ff)))

    outs, lows, grads = [], [], None
    for both in gathered:
        grad_pre, low, grad = hidden_call(both, inner_cat, outer_cat, bias, up_hi, down_lo, down_hi, ff)
        share = share_call(grad_pre, inner_cat, 2 * chips)
        outs.append(lax.psum_scatter(share, "col", scatter_dimension=0))
        lows.append(LowSum(low, chips))
        lows[-1].spread()
        grads = grad if grads is None else grads + grad
    tokens_grad = jnp.concatenate(outs, axis=0)

    hidden_sums = sum_rows((grads[:, :ff] * scale).astype(BF16))
    inner_up_grad = hidden_sums[:rank]
    outer_down_grad = hidden_sums[rank:].T

    feature_part = 0.0
    for start, size, gated, piece in zip(starts, sizes, gated_parts, lows):
        low, tokens = piece.result(), tokens_in[start : start + size]
        feature_part = feature_part + jnp.concatenate(
            [dot_tn(low[:, :rank], gated), dot_tn(low[:, rank:], tokens)], axis=0
        )
    feature_sums = sum_rows_at_once((feature_part * scale).astype(BF16))
    outer_up_grad = feature_sums[:rank]
    inner_down_grad = feature_sums[rank:].T
    return (tokens_grad, inner_down_grad, inner_up_grad, outer_down_grad, outer_up_grad)


def solution(mesh):
    placed = (
        P("row", "col"),
        P("row", "col"),
        P(),
        P(None, "col"),
        P("col"),
        P(None, "col"),
        P(),
        P(None, "col"),
        P("col", None),
        P(),
    )
    return jax.shard_map(
        local,
        mesh=mesh,
        in_specs=placed,
        out_specs=(P("row", "col"), P("col", None), P(None, "col"), P("col", None), P(None, "col")),
        check_vma=False,
    )
```

```python
import functools
import math

import jax
import jax.numpy as jnp
from jax import lax
from jax.experimental import pallas as pl
from jax.experimental.pallas import tpu as pltpu
from jax.sharding import PartitionSpec as P

SLOPE_SCALE = 0.7978845608028654
CUBIC = 0.044715
F32 = jnp.float32
BF16 = jnp.bfloat16
LANES = 128
COLS = 256
VMEM_BYTES = 52 * 1024 * 1024
COST = pl.CostEstimate(flops=20_000_000_000, bytes_accessed=36_000_000, transcendentals=0)
SPLIT = ((512, 384), (512, 288))


def dot_nn(left, right):
    return jnp.dot(left, right, preferred_element_type=F32)


def dot_nt(left, right):
    return lax.dot_general(left, right, (((1,), (1,)), ((), ())), preferred_element_type=F32)


def dot_tn(left, right):
    return lax.dot_general(left, right, (((0,), (0,)), ((), ())), preferred_element_type=F32)


def hidden_kernel(ff, both_ref, inner_ref, outer_ref, bias_ref, up_ref, down_lo_ref, down_hi_ref, *refs):
    grad_ref, low_ref, grads_ref, pre_acc, hid_acc, hidden_ref = refs[-6:]
    step = pl.program_id(0)
    _, _, tokens, width = both_ref.shape
    padded = pre_acc.shape[1]

    def product(which, weight_ref):
        first, second = both_ref[0, which], both_ref[1, which]
        if width % LANES == 0:
            return dot_nt(jnp.concatenate([first, second], axis=1), weight_ref[...])
        return dot_nt(first, weight_ref[:, :width]) + dot_nt(second, weight_ref[:, width:])

    @pl.when(step == 0)
    def _():
        pre_acc[...] = product(0, inner_ref)
        hid_acc[...] = product(1, outer_ref)

    @pl.when(step > 0)
    def _():
        pre_acc[...] += product(0, inner_ref)
        hid_acc[...] += product(1, outer_ref)

    @pl.when(step == pl.num_programs(0) - 1)
    def _():
        tail = slice(padded - LANES, padded)
        inner_low = pre_acc[:, tail].astype(BF16)
        grad_low = hid_acc[:, tail].astype(BF16)
        rank = LANES // 2
        low = jnp.zeros((tokens, LANES), F32)
        for start in range(0, padded, COLS):
            cols = slice(start, start + COLS)
            pre = pre_acc[:, cols] + dot_nn(inner_low, up_ref[:, cols]) + bias_ref[:, cols]
            square = pre * pre
            tangent = jnp.tanh(SLOPE_SCALE * pre * (1.0 + CUBIC * square))
            half = 0.5 + 0.5 * tangent
            hidden = (pre * half).astype(BF16)
            slope = half + 0.5 * pre * (1.0 - tangent * tangent) * (
                SLOPE_SCALE + 3.0 * CUBIC * SLOPE_SCALE * square
            )
            grad_hidden = hid_acc[:, cols] + dot_nn(grad_low, down_hi_ref[:, cols])
            grad_pre = (grad_hidden * slope).astype(BF16)
            hidden_ref[:, cols] = hidden
            grad_ref[:, cols] = grad_pre
        low = dot_nt(hidden_ref[...], down_lo_ref[...]) + dot_nt(grad_ref[...], up_ref[...])
        low = low.astype(BF16)
        low_ref[...] = low
        grads_ref[:rank] = dot_tn(inner_low, grad_ref[...])[rank:]
        grads_ref[rank:] = dot_tn(grad_low, hidden_ref[...])[rank:]
        lane = lax.broadcasted_iota(jnp.int32, (tokens, LANES), 1)
        keep = lane + (padded - LANES) < ff
        filled = jnp.where(lane >= rank, low, jnp.zeros_like(low))
        grad_ref[:, tail] = jnp.where(keep, grad_ref[:, tail], filled)
        for start in range(0, padded - LANES, LANES):
            if start + LANES > ff:
                here = slice(start, start + LANES)
                grad_ref[:, here] = jnp.where(lane + start < ff, grad_ref[:, here], jnp.zeros_like(low))


def hidden_call(both, inner_cat, outer_cat, bias, up, down_lo, down_hi, ff, after=()):
    devices, _, tokens, width = both.shape
    padded = inner_cat.shape[0]
    steps = devices // 2
    whole = lambda k: (0, 0)
    return pl.pallas_call(
        functools.partial(hidden_kernel, ff),
        grid=(steps,),
        in_specs=[
            pl.BlockSpec((2, 2, tokens, width), lambda k: (k, 0, 0, 0)),
            pl.BlockSpec((padded, 2 * width), lambda k: (0, k)),
            pl.BlockSpec((padded, 2 * width), lambda k: (0, k)),
            pl.BlockSpec((1, padded), whole),
            pl.BlockSpec((LANES, padded), whole),
            pl.BlockSpec((LANES, padded), whole),
            pl.BlockSpec((LANES, padded), whole),
        ]
        + [pl.BlockSpec(memory_space=pl.ANY)] * len(after),
        out_specs=[
            pl.BlockSpec((tokens, padded), whole),
            pl.BlockSpec((tokens, LANES), whole),
            pl.BlockSpec((LANES, padded), whole),
        ],
        out_shape=[
            jax.ShapeDtypeStruct((tokens, padded), BF16),
            jax.ShapeDtypeStruct((tokens, LANES), BF16),
            jax.ShapeDtypeStruct((LANES, padded), F32),
        ],
        scratch_shapes=[
            pltpu.VMEM((tokens, padded), F32),
            pltpu.VMEM((tokens, padded), F32),
            pltpu.VMEM((tokens, padded), BF16),
        ],
        compiler_params=pltpu.CompilerParams(vmem_limit_bytes=VMEM_BYTES),
        cost_estimate=COST,
    )(both, inner_cat, outer_cat, bias, up, down_lo, down_hi, *after)


def share_kernel(place_ref, grad_ref, weight_ref, *refs):
    share_ref, own_ref, other_ref = refs[-3:]
    first, width = own_ref.shape[1:]
    if width % LANES == 0:
        share = dot_nn(grad_ref[...], weight_ref[...]).astype(BF16)
        shares = [share[:, :width], share[:, width:]]
    else:
        shares = [
            dot_nn(grad_ref[...], weight_ref[:, part * width : (part + 1) * width]).astype(BF16)
            for part in (0, 1)
        ]
    for part in (0, 1):
        share_ref[part] = shares[part][first:]

    @pl.when(place_ref[1] == 0)
    def _():
        own_ref[0], other_ref[0] = shares[0][:first], shares[1][:first]

    @pl.when(place_ref[1] != 0)
    def _():
        own_ref[0], other_ref[0] = shares[1][:first], shares[0][:first]


def share_call(place, grad, weight, chips, first, after=()):
    tokens, padded = grad.shape
    width = weight.shape[1] // (2 * chips)
    there = lambda j, place: lax.rem(place[0] + j, chips)
    near = pl.BlockSpec((1, first, width), lambda j, place: (j, 0, 0))
    near_shape = jax.ShapeDtypeStruct((chips, first, width), BF16)
    return pl.pallas_call(
        share_kernel,
        grid_spec=pltpu.PrefetchScalarGridSpec(
            num_scalar_prefetch=1,
            grid=(chips,),
            in_specs=[
                pl.BlockSpec((tokens, padded), lambda j, place: (0, 0)),
                pl.BlockSpec((padded, 2 * width), lambda j, place: (0, there(j, place))),
            ]
            + [pl.BlockSpec(memory_space=pl.ANY)] * len(after),
            out_specs=[
                pl.BlockSpec((2, tokens - first, width), lambda j, place: (there(j, place), 0, 0)),
                near,
                near,
            ],
        ),
        out_shape=[
            jax.ShapeDtypeStruct((2 * chips, tokens - first, width), BF16),
            near_shape,
            near_shape,
        ],
        compiler_params=pltpu.CompilerParams(vmem_limit_bytes=VMEM_BYTES),
        cost_estimate=COST,
    )(place, grad, weight, *after)


def lane_pairs(pairs):
    return [(2 * a + core, 2 * b + core) for a, b in pairs for core in (0, 1)]


def send(value, pairs):
    return lax.ppermute(value, "col", lane_pairs(pairs))


def swap_cores(value, chips):
    return lax.ppermute(value, "col", [(i, i ^ 1) for i in range(2 * chips)])


def add(*terms):
    total = terms[0].astype(F32)
    for term in terms[1:]:
        total = total + term.astype(F32)
    return total


class Shares:
    def __init__(self, own, other, chips):
        arrived = swap_cores(other, chips)
        self.shares = [add(own[j], arrived[j]) for j in range(chips)]
        self.chips, self.step, self.up, self.down = chips, 0, None, None

    def hop(self):
        self.step += 1
        s, chips = self.step, self.chips
        up, down = self.shares[chips - s], self.shares[s]
        if s > 1:
            up, down = up + self.up.astype(F32), down + self.down.astype(F32)
        up, down = up.astype(BF16), down.astype(BF16)
        self.up = send(up, [(z, z + 1) for z in range(s)])
        self.down = send(down, [(z, z - 1) for z in range(chips - s, chips)])
        return [up, down]

    def left(self):
        return self.chips - 1 - self.step

    def result(self):
        return add(self.shares[0], self.up, self.down).astype(BF16)


class LowSum:
    def __init__(self, low, chips):
        self.chips, self.low = chips, low
        self.other = swap_cores(low, chips)

    def spread(self):
        self.mine = add(self.low, self.other).astype(BF16)
        chips = self.chips
        self.got = [send(self.mine, [(z, (z + d) % chips) for z in range(chips)]) for d in range(1, chips)]
        return [self.mine]

    def result(self):
        return add(self.mine, *self.got).astype(BF16)


def sum_rows(value):
    rows = lax.axis_size("row")
    if rows & (rows - 1):
        return lax.psum(value, "row").astype(F32)
    bits = [1 << b for b in range(rows.bit_length() - 1)]
    half = value.shape[0] // 2
    pieces = [(value[:half], bits), (value[half:], bits[::-1])]
    sums = []
    for piece, order in pieces:
        for bit in order:
            got = lax.ppermute(piece.astype(BF16), "row", [(i, i ^ bit) for i in range(rows)])
            piece = piece.astype(BF16).astype(F32) + got.astype(F32)
        sums.append(piece)
    return jnp.concatenate(sums, axis=0)


def sum_rows_at_once(value):
    rows = lax.axis_size("row")
    if rows & (rows - 1):
        return lax.psum(value, "row").astype(F32)
    terms = [value] + [
        lax.ppermute(value, "row", [(i, i ^ other) for i in range(rows)]) for other in range(1, rows)
    ]
    terms = [term.astype(F32) for term in terms]
    while len(terms) > 1:
        terms = [terms[i] + terms[i + 1] for i in range(0, len(terms), 2)]
    return terms[0]


def local(
    tokens_in, token_grad, gate_gain, inner_weight, inner_bias, outer_weight,
    inner_down, inner_up, outer_down, outer_up,
):
    chips = lax.axis_size("col") // 2
    col_index = lax.axis_index("col")
    place = jnp.stack([lax.div(col_index, 2), lax.rem(col_index, 2)]).astype(jnp.int32)
    tok_rows, width = token_grad.shape
    features, ff = inner_weight.shape
    rank = inner_down.shape[1]
    padded = -(-(ff + rank) // COLS) * COLS
    scale = 1.0 / math.sqrt(tok_rows * lax.axis_size("row"))

    gain_local = lax.dynamic_slice_in_dim(gate_gain, col_index * width, width, 0)
    sizes = [tok_rows * part // sum(part for part, _ in SPLIT) for part, _ in SPLIT]
    firsts = [size * share // 1024 // 16 * 16 for size, (_, share) in zip(sizes, SPLIT)]
    starts = [sum(sizes[:i]) for i in range(len(sizes))]

    gathered, gated_parts = [], []
    for start, size in zip(starts, sizes):
        gated = (gain_local[None, :] * token_grad[start : start + size].astype(F32)).astype(BF16)
        both = jnp.stack([tokens_in[start : start + size], gated])
        gathered.append(lax.all_gather(both, "col", axis=0))
        gated_parts.append(gated)

    gap = padded - ff - rank
    blank = jnp.zeros((gap, features), BF16)
    inner_cat = jnp.concatenate([inner_weight.T, blank, inner_down.T], axis=0)
    outer_cat = jnp.concatenate([outer_weight.T, blank, outer_up], axis=0)
    bias = jnp.pad(inner_bias, (0, padded - ff))[None, :]
    up_hi = jnp.pad(inner_up, ((LANES - rank, 0), (0, padded - ff)))
    down_hi = jnp.pad(outer_down.T, ((LANES - rank, 0), (0, padded - ff)))
    down_lo = jnp.pad(outer_down.T, ((0, LANES - rank), (0, padded - ff)))

    near, far, lows, grads = [], [], [], None
    for index, (both, first) in enumerate(zip(gathered, firsts)):
        after = []
        if index:
            shares = moving
            while shares.left():
                after = shares.hop()
            after = after + lows[-1].spread()
        grad_pre, low, grad = hidden_call(
            both, inner_cat, outer_cat, bias, up_hi, down_lo, down_hi, ff, after
        )
        after = []
        if index:
            near.append(shares.result())
            lows[-1] = lows[-1].result()
            after = [near[-1], lows[-1]]
        share, own, other = share_call(place, grad_pre, inner_cat, chips, first, after)
        far.append(lax.psum_scatter(share, "col", scatter_dimension=0))
        moving = Shares(own, other, chips)
        lows.append(LowSum(low, chips))
        grads = grad if grads is None else grads + grad
    while moving.left():
        moving.hop()
    near.append(moving.result())
    lows[-1].spread()
    lows[-1] = lows[-1].result()
    tokens_grad = jnp.concatenate([part for pair in zip(near, far) for part in pair], axis=0)

    hidden_sums = sum_rows((grads[:, :ff] * scale).astype(BF16))
    inner_up_grad = hidden_sums[:rank]
    outer_down_grad = hidden_sums[rank:].T

    feature_part = 0.0
    for start, size, gated, low in zip(starts, sizes, gated_parts, lows):
        tokens = tokens_in[start : start + size]
        feature_part = feature_part + jnp.concatenate(
            [dot_tn(low[:, :rank], gated), dot_tn(low[:, rank:], tokens)], axis=0
        )
    feature_sums = sum_rows_at_once((feature_part * scale).astype(BF16))
    outer_up_grad = feature_sums[:rank]
    inner_down_grad = feature_sums[rank:].T
    return (tokens_grad, inner_down_grad, inner_up_grad, outer_down_grad, outer_up_grad)


def solution(mesh):
    placed = (
        P("row", "col"),
        P("row", "col"),
        P(),
        P(None, "col"),
        P("col"),
        P(None, "col"),
        P(),
        P(None, "col"),
        P("col", None),
        P(),
    )
    return jax.shard_map(
        local,
        mesh=mesh,
        in_specs=placed,
        out_specs=(P("row", "col"), P("col", None), P(None, "col"), P("col", None), P(None, "col")),
        check_vma=False,
    )
```

```python
import functools
import math

import jax
import jax.numpy as jnp
from jax import lax
from jax.experimental import pallas as pl
from jax.experimental.pallas import tpu as pltpu
from jax.sharding import PartitionSpec as P

SLOPE_SCALE = 0.7978845608028654
CUBIC = 0.044715
F32 = jnp.float32
BF16 = jnp.bfloat16
LANES = 128
COLS = 256
VMEM_BYTES = 52 * 1024 * 1024
COST = pl.CostEstimate(flops=20_000_000_000, bytes_accessed=36_000_000, transcendentals=0)
SPLIT = ((512, 384), (512, 288))


def dot_nn(left, right):
    return jnp.dot(left, right, preferred_element_type=F32)


def dot_nt(left, right):
    return lax.dot_general(left, right, (((1,), (1,)), ((), ())), preferred_element_type=F32)


def dot_tn(left, right):
    return lax.dot_general(left, right, (((0,), (0,)), ((), ())), preferred_element_type=F32)


def hidden_kernel(ff, both_ref, inner_ref, outer_ref, bias_ref, up_ref, down_lo_ref, down_hi_ref, *refs):
    grad_ref, low_ref, grads_ref, pre_acc, hid_acc, hidden_ref = refs[-6:]
    step = pl.program_id(0)
    _, _, tokens, width = both_ref.shape
    padded = pre_acc.shape[1]

    def product(which, weight_ref):
        first, second = both_ref[0, which], both_ref[1, which]
        if width % LANES == 0:
            return dot_nt(jnp.concatenate([first, second], axis=1), weight_ref[...])
        return dot_nt(first, weight_ref[:, :width]) + dot_nt(second, weight_ref[:, width:])

    @pl.when(step == 0)
    def _():
        pre_acc[...] = product(0, inner_ref)
        hid_acc[...] = product(1, outer_ref)

    @pl.when(step > 0)
    def _():
        pre_acc[...] += product(0, inner_ref)
        hid_acc[...] += product(1, outer_ref)

    @pl.when(step == pl.num_programs(0) - 1)
    def _():
        tail = slice(padded - LANES, padded)
        inner_low = pre_acc[:, tail].astype(BF16)
        grad_low = hid_acc[:, tail].astype(BF16)
        rank = LANES // 2
        low = jnp.zeros((tokens, LANES), F32)
        for start in range(0, padded, COLS):
            cols = slice(start, start + COLS)
            pre = pre_acc[:, cols] + dot_nn(inner_low, up_ref[:, cols]) + bias_ref[:, cols]
            square = pre * pre
            tangent = jnp.tanh(SLOPE_SCALE * pre * (1.0 + CUBIC * square))
            half = 0.5 + 0.5 * tangent
            hidden = (pre * half).astype(BF16)
            slope = half + 0.5 * pre * (1.0 - tangent * tangent) * (
                SLOPE_SCALE + 3.0 * CUBIC * SLOPE_SCALE * square
            )
            grad_hidden = hid_acc[:, cols] + dot_nn(grad_low, down_hi_ref[:, cols])
            grad_pre = (grad_hidden * slope).astype(BF16)
            hidden_ref[:, cols] = hidden
            grad_ref[:, cols] = grad_pre
        low = dot_nt(hidden_ref[...], down_lo_ref[...]) + dot_nt(grad_ref[...], up_ref[...])
        low = low.astype(BF16)
        low_ref[...] = low
        grads_ref[:rank] = dot_tn(inner_low, grad_ref[...])[rank:]
        grads_ref[rank:] = dot_tn(grad_low, hidden_ref[...])[rank:]
        lane = lax.broadcasted_iota(jnp.int32, (tokens, LANES), 1)
        keep = lane + (padded - LANES) < ff
        filled = jnp.where(lane >= rank, low, jnp.zeros_like(low))
        grad_ref[:, tail] = jnp.where(keep, grad_ref[:, tail], filled)
        for start in range(0, padded - LANES, LANES):
            if start + LANES > ff:
                here = slice(start, start + LANES)
                grad_ref[:, here] = jnp.where(lane + start < ff, grad_ref[:, here], jnp.zeros_like(low))


def hidden_call(both, inner_cat, outer_cat, bias, up, down_lo, down_hi, ff, after=()):
    devices, _, tokens, width = both.shape
    padded = inner_cat.shape[0]
    steps = devices // 2
    whole = lambda k: (0, 0)
    return pl.pallas_call(
        functools.partial(hidden_kernel, ff),
        grid=(steps,),
        in_specs=[
            pl.BlockSpec((2, 2, tokens, width), lambda k: (k, 0, 0, 0)),
            pl.BlockSpec((padded, 2 * width), lambda k: (0, k)),
            pl.BlockSpec((padded, 2 * width), lambda k: (0, k)),
            pl.BlockSpec((1, padded), whole),
            pl.BlockSpec((LANES, padded), whole),
            pl.BlockSpec((LANES, padded), whole),
            pl.BlockSpec((LANES, padded), whole),
        ]
        + [pl.BlockSpec(memory_space=pl.ANY)] * len(after),
        out_specs=[
            pl.BlockSpec((tokens, padded), whole),
            pl.BlockSpec((tokens, LANES), whole),
            pl.BlockSpec((LANES, padded), whole),
        ],
        out_shape=[
            jax.ShapeDtypeStruct((tokens, padded), BF16),
            jax.ShapeDtypeStruct((tokens, LANES), BF16),
            jax.ShapeDtypeStruct((LANES, padded), F32),
        ],
        scratch_shapes=[
            pltpu.VMEM((tokens, padded), F32),
            pltpu.VMEM((tokens, padded), F32),
            pltpu.VMEM((tokens, padded), BF16),
        ],
        compiler_params=pltpu.CompilerParams(vmem_limit_bytes=VMEM_BYTES),
        cost_estimate=COST,
    )(both, inner_cat, outer_cat, bias, up, down_lo, down_hi, *after)


def share_kernel(place_ref, grad_ref, weight_ref, *refs):
    share_ref, own_ref, other_ref = refs[-3:]
    first, width = own_ref.shape[1:]
    if width % LANES == 0:
        share = dot_nn(grad_ref[...], weight_ref[...]).astype(BF16)
        shares = [share[:, :width], share[:, width:]]
    else:
        shares = [
            dot_nn(grad_ref[...], weight_ref[:, part * width : (part + 1) * width]).astype(BF16)
            for part in (0, 1)
        ]
    for part in (0, 1):
        share_ref[part] = shares[part][first:]

    @pl.when(place_ref[1] == 0)
    def _():
        own_ref[0], other_ref[0] = shares[0][:first], shares[1][:first]

    @pl.when(place_ref[1] != 0)
    def _():
        own_ref[0], other_ref[0] = shares[1][:first], shares[0][:first]


def share_call(place, grad, weight, chips, first, after=()):
    tokens, padded = grad.shape
    width = weight.shape[1] // (2 * chips)
    there = lambda j, place: lax.rem(place[0] + j, chips)
    near = pl.BlockSpec((1, first, width), lambda j, place: (j, 0, 0))
    near_shape = jax.ShapeDtypeStruct((chips, first, width), BF16)
    return pl.pallas_call(
        share_kernel,
        grid_spec=pltpu.PrefetchScalarGridSpec(
            num_scalar_prefetch=1,
            grid=(chips,),
            in_specs=[
                pl.BlockSpec((tokens, padded), lambda j, place: (0, 0)),
                pl.BlockSpec((padded, 2 * width), lambda j, place: (0, there(j, place))),
            ]
            + [pl.BlockSpec(memory_space=pl.ANY)] * len(after),
            out_specs=[
                pl.BlockSpec((2, tokens - first, width), lambda j, place: (there(j, place), 0, 0)),
                near,
                near,
            ],
        ),
        out_shape=[
            jax.ShapeDtypeStruct((2 * chips, tokens - first, width), BF16),
            near_shape,
            near_shape,
        ],
        compiler_params=pltpu.CompilerParams(vmem_limit_bytes=VMEM_BYTES),
        cost_estimate=COST,
    )(place, grad, weight, *after)


def gate(value, after):
    anywhere = pl.BlockSpec(memory_space=pl.ANY)
    return pl.pallas_call(
        lambda *refs: None,
        in_specs=[anywhere] * (1 + len(after)),
        out_specs=anywhere,
        out_shape=jax.ShapeDtypeStruct(value.shape, value.dtype),
        input_output_aliases={0: 0},
    )(value, *after)


def lane_pairs(pairs):
    return [(2 * a + core, 2 * b + core) for a, b in pairs for core in (0, 1)]


def send(value, pairs):
    return lax.ppermute(value, "col", lane_pairs(pairs))


def swap_cores(value, chips):
    return lax.ppermute(value, "col", [(i, i ^ 1) for i in range(2 * chips)])


def add(*terms):
    total = terms[0].astype(F32)
    for term in terms[1:]:
        total = total + term.astype(F32)
    return total


class Shares:
    def __init__(self, own, other, chips):
        arrived = swap_cores(other, chips)
        self.shares = [add(own[j], arrived[j]) for j in range(chips)]
        self.chips, self.step, self.up, self.down = chips, 0, None, None

    def hop(self):
        self.step += 1
        s, chips = self.step, self.chips
        up, down = self.shares[chips - s], self.shares[s]
        if s > 1:
            up, down = up + self.up.astype(F32), down + self.down.astype(F32)
        up, down = up.astype(BF16), down.astype(BF16)
        self.up = send(up, [(z, z + 1) for z in range(s)])
        self.down = send(down, [(z, z - 1) for z in range(chips - s, chips)])
        return [up, down]

    def left(self):
        return self.chips - 1 - self.step

    def result(self):
        return add(self.shares[0], self.up, self.down).astype(BF16)


class LowSum:
    def __init__(self, low, core, chips):
        self.core, self.chips, self.step = core, chips, 0
        half = low.shape[0] // 2
        first, second = low[:half], low[half:]
        got = swap_cores(jnp.where(core == 0, second, first), chips)
        self.mine = add(jnp.where(core == 0, first, second), got)
        self.up = self.down = jnp.zeros(self.mine.shape, F32)

    def hop(self, after):
        s, chips = self.step, self.chips
        self.step += 1
        to_up = gate((self.mine + self.up).astype(BF16), after)
        to_down = (self.mine + self.down).astype(BF16)
        self.up = self.up + send(to_up, [(s, s + 1)]).astype(F32)
        self.down = self.down + send(to_down, [(chips - 1 - s, chips - 2 - s)]).astype(F32)
        return [to_up, to_down]

    def result(self):
        total = (self.mine + self.up + self.down).astype(BF16)
        other = swap_cores(total, self.chips)
        return jnp.concatenate(
            [jnp.where(self.core == 0, total, other), jnp.where(self.core == 0, other, total)], axis=0
        )


def sum_rows(value):
    rows = lax.axis_size("row")
    if rows & (rows - 1):
        return lax.psum(value, "row").astype(F32)
    bits = [1 << b for b in range(rows.bit_length() - 1)]
    half = value.shape[0] // 2
    pieces = [(value[:half], bits), (value[half:], bits[::-1])]
    sums = []
    for piece, order in pieces:
        for bit in order:
            got = lax.ppermute(piece.astype(BF16), "row", [(i, i ^ bit) for i in range(rows)])
            piece = piece.astype(BF16).astype(F32) + got.astype(F32)
        sums.append(piece)
    return jnp.concatenate(sums, axis=0)


def sum_rows_at_once(value):
    rows = lax.axis_size("row")
    if rows & (rows - 1):
        return lax.psum(value, "row").astype(F32)
    terms = [value] + [
        lax.ppermute(value, "row", [(i, i ^ other) for i in range(rows)]) for other in range(1, rows)
    ]
    terms = [term.astype(F32) for term in terms]
    while len(terms) > 1:
        terms = [terms[i] + terms[i + 1] for i in range(0, len(terms), 2)]
    return terms[0]


def local(
    tokens_in, token_grad, gate_gain, inner_weight, inner_bias, outer_weight,
    inner_down, inner_up, outer_down, outer_up,
):
    chips = lax.axis_size("col") // 2
    col_index = lax.axis_index("col")
    core = lax.rem(col_index, 2)
    place = jnp.stack([lax.div(col_index, 2), core]).astype(jnp.int32)
    tok_rows, width = token_grad.shape
    features, ff = inner_weight.shape
    rank = inner_down.shape[1]
    padded = -(-(ff + rank) // COLS) * COLS
    scale = 1.0 / math.sqrt(tok_rows * lax.axis_size("row"))

    gain_local = lax.dynamic_slice_in_dim(gate_gain, col_index * width, width, 0)
    sizes = [tok_rows * part // sum(part for part, _ in SPLIT) for part, _ in SPLIT]
    firsts = [size * share // 1024 // 16 * 16 for size, (_, share) in zip(sizes, SPLIT)]
    starts = [sum(sizes[:i]) for i in range(len(sizes))]

    gathered, gated_parts = [], []
    for start, size in zip(starts, sizes):
        gated = (gain_local[None, :] * token_grad[start : start + size].astype(F32)).astype(BF16)
        both = jnp.stack([tokens_in[start : start + size], gated])
        gathered.append(lax.all_gather(both, "col", axis=0))
        gated_parts.append(gated)

    gap = padded - ff - rank
    blank = jnp.zeros((gap, features), BF16)
    inner_cat = jnp.concatenate([inner_weight.T, blank, inner_down.T], axis=0)
    outer_cat = jnp.concatenate([outer_weight.T, blank, outer_up], axis=0)
    bias = jnp.pad(inner_bias, (0, padded - ff))[None, :]
    up_hi = jnp.pad(inner_up, ((LANES - rank, 0), (0, padded - ff)))
    down_hi = jnp.pad(outer_down.T, ((LANES - rank, 0), (0, padded - ff)))
    down_lo = jnp.pad(outer_down.T, ((0, LANES - rank), (0, padded - ff)))

    near, far, lows, grads = [], [], [], None
    for index, (both, first) in enumerate(zip(gathered, firsts)):
        after = []
        if index:
            while moving.left():
                sent = moving.hop()
                after = sent + summing.hop(sent)
        grad_pre, low, grad = hidden_call(
            both, inner_cat, outer_cat, bias, up_hi, down_lo, down_hi, ff, after
        )
        after = []
        if index:
            near.append(moving.result())
            lows.append(summing.result())
            after = [near[-1], lows[-1]]
        share, own, other = share_call(place, grad_pre, inner_cat, chips, first, after)
        far.append(lax.psum_scatter(share, "col", scatter_dimension=0))
        moving = Shares(own, other, chips)
        summing = LowSum(low, core, chips)
        grads = grad if grads is None else grads + grad
    hidden_part = (grads[:, :ff] * scale).astype(BF16)
    while moving.left():
        sent = moving.hop()
        summing.hop(sent)
        if moving.step == 1:
            hidden_part = gate(hidden_part, sent)
    near.append(moving.result())
    lows.append(summing.result())
    tokens_grad = jnp.concatenate([part for pair in zip(near, far) for part in pair], axis=0)

    hidden_sums = sum_rows(hidden_part)
    inner_up_grad = hidden_sums[:rank]
    outer_down_grad = hidden_sums[rank:].T

    feature_part = 0.0
    for start, size, gated, low in zip(starts, sizes, gated_parts, lows):
        tokens = tokens_in[start : start + size]
        feature_part = feature_part + jnp.concatenate(
            [dot_tn(low[:, :rank], gated), dot_tn(low[:, rank:], tokens)], axis=0
        )
    feature_sums = sum_rows_at_once((feature_part * scale).astype(BF16))
    outer_up_grad = feature_sums[:rank]
    inner_down_grad = feature_sums[rank:].T
    return (tokens_grad, inner_down_grad, inner_up_grad, outer_down_grad, outer_up_grad)


def solution(mesh):
    placed = (
        P("row", "col"),
        P("row", "col"),
        P(),
        P(None, "col"),
        P("col"),
        P(None, "col"),
        P(),
        P(None, "col"),
        P("col", None),
        P(),
    )
    return jax.shard_map(
        local,
        mesh=mesh,
        in_specs=placed,
        out_specs=(P("row", "col"), P("col", None), P(None, "col"), P("col", None), P(None, "col")),
        check_vma=False,
    )
```

```python
import functools
import math

import jax
import jax.numpy as jnp
from jax import lax
from jax.experimental import pallas as pl
from jax.experimental.pallas import tpu as pltpu
from jax.sharding import PartitionSpec as P

SLOPE_SCALE = 0.7978845608028654
CUBIC = 0.044715
F32 = jnp.float32
BF16 = jnp.bfloat16
LANES = 128
COLS = 256
VMEM_BYTES = 52 * 1024 * 1024
COST = pl.CostEstimate(flops=20_000_000_000, bytes_accessed=36_000_000, transcendentals=0)
SPLIT = ((512, 256), (512, 0))


def dot_nn(left, right):
    return jnp.dot(left, right, preferred_element_type=F32)


def dot_nt(left, right):
    return lax.dot_general(left, right, (((1,), (1,)), ((), ())), preferred_element_type=F32)


def dot_tn(left, right):
    return lax.dot_general(left, right, (((0,), (0,)), ((), ())), preferred_element_type=F32)


def hidden_kernel(ff, both_ref, inner_ref, outer_ref, bias_ref, up_ref, down_lo_ref, down_hi_ref, *refs):
    grad_ref, low_ref, grads_ref, pre_acc, hid_acc, hidden_ref = refs[-6:]
    step = pl.program_id(0)
    _, _, tokens, width = both_ref.shape
    padded = pre_acc.shape[1]

    def product(which, weight_ref):
        first, second = both_ref[0, which], both_ref[1, which]
        if width % LANES == 0:
            return dot_nt(jnp.concatenate([first, second], axis=1), weight_ref[...])
        return dot_nt(first, weight_ref[:, :width]) + dot_nt(second, weight_ref[:, width:])

    @pl.when(step == 0)
    def _():
        pre_acc[...] = product(0, inner_ref)
        hid_acc[...] = product(1, outer_ref)

    @pl.when(step > 0)
    def _():
        pre_acc[...] += product(0, inner_ref)
        hid_acc[...] += product(1, outer_ref)

    @pl.when(step == pl.num_programs(0) - 1)
    def _():
        tail = slice(padded - LANES, padded)
        inner_low = pre_acc[:, tail].astype(BF16)
        grad_low = hid_acc[:, tail].astype(BF16)
        rank = LANES // 2
        low = jnp.zeros((tokens, LANES), F32)
        for start in range(0, padded, COLS):
            cols = slice(start, start + COLS)
            pre = pre_acc[:, cols] + dot_nn(inner_low, up_ref[:, cols]) + bias_ref[:, cols]
            square = pre * pre
            tangent = jnp.tanh(SLOPE_SCALE * pre * (1.0 + CUBIC * square))
            half = 0.5 + 0.5 * tangent
            hidden = (pre * half).astype(BF16)
            slope = half + 0.5 * pre * (1.0 - tangent * tangent) * (
                SLOPE_SCALE + 3.0 * CUBIC * SLOPE_SCALE * square
            )
            grad_hidden = hid_acc[:, cols] + dot_nn(grad_low, down_hi_ref[:, cols])
            grad_pre = (grad_hidden * slope).astype(BF16)
            hidden_ref[:, cols] = hidden
            grad_ref[:, cols] = grad_pre
        low = dot_nt(hidden_ref[...], down_lo_ref[...]) + dot_nt(grad_ref[...], up_ref[...])
        low = low.astype(BF16)
        low_ref[...] = low
        grads_ref[:rank] = dot_tn(inner_low, grad_ref[...])[rank:]
        grads_ref[rank:] = dot_tn(grad_low, hidden_ref[...])[rank:]
        lane = lax.broadcasted_iota(jnp.int32, (tokens, LANES), 1)
        keep = lane + (padded - LANES) < ff
        filled = jnp.where(lane >= rank, low, jnp.zeros_like(low))
        grad_ref[:, tail] = jnp.where(keep, grad_ref[:, tail], filled)
        for start in range(0, padded - LANES, LANES):
            if start + LANES > ff:
                here = slice(start, start + LANES)
                grad_ref[:, here] = jnp.where(lane + start < ff, grad_ref[:, here], jnp.zeros_like(low))


def hidden_call(both, inner_cat, outer_cat, bias, up, down_lo, down_hi, ff, after=()):
    devices, _, tokens, width = both.shape
    padded = inner_cat.shape[0]
    steps = devices // 2
    whole = lambda k: (0, 0)
    return pl.pallas_call(
        functools.partial(hidden_kernel, ff),
        grid=(steps,),
        in_specs=[
            pl.BlockSpec((2, 2, tokens, width), lambda k: (k, 0, 0, 0)),
            pl.BlockSpec((padded, 2 * width), lambda k: (0, k)),
            pl.BlockSpec((padded, 2 * width), lambda k: (0, k)),
            pl.BlockSpec((1, padded), whole),
            pl.BlockSpec((LANES, padded), whole),
            pl.BlockSpec((LANES, padded), whole),
            pl.BlockSpec((LANES, padded), whole),
        ]
        + [pl.BlockSpec(memory_space=pl.ANY)] * len(after),
        out_specs=[
            pl.BlockSpec((tokens, padded), whole),
            pl.BlockSpec((tokens, LANES), whole),
            pl.BlockSpec((LANES, padded), whole),
        ],
        out_shape=[
            jax.ShapeDtypeStruct((tokens, padded), BF16),
            jax.ShapeDtypeStruct((tokens, LANES), BF16),
            jax.ShapeDtypeStruct((LANES, padded), F32),
        ],
        scratch_shapes=[
            pltpu.VMEM((tokens, padded), F32),
            pltpu.VMEM((tokens, padded), F32),
            pltpu.VMEM((tokens, padded), BF16),
        ],
        compiler_params=pltpu.CompilerParams(vmem_limit_bytes=VMEM_BYTES),
        cost_estimate=COST,
    )(both, inner_cat, outer_cat, bias, up, down_lo, down_hi, *after)


def share_kernel(first, place_ref, grad_ref, weight_ref, *refs):
    share_ref, near_refs = (refs[-3], refs[-2:]) if first else (refs[-1], ())
    width = share_ref.shape[2]
    if width % LANES == 0:
        share = dot_nn(grad_ref[...], weight_ref[...]).astype(BF16)
        shares = [share[:, :width], share[:, width:]]
    else:
        shares = [
            dot_nn(grad_ref[...], weight_ref[:, part * width : (part + 1) * width]).astype(BF16)
            for part in (0, 1)
        ]
    for part in (0, 1):
        share_ref[part] = shares[part][first:]
    for turn, near_ref in enumerate(near_refs):

        @pl.when(place_ref[1] == 0)
        def _():
            near_ref[0] = shares[turn][:first]

        @pl.when(place_ref[1] != 0)
        def _():
            near_ref[0] = shares[1 - turn][:first]


def share_call(place, grad, weight, chips, first, after=()):
    tokens, padded = grad.shape
    width = weight.shape[1] // (2 * chips)
    there = lambda j, place: lax.rem(place[0] + j, chips)
    out_specs = [pl.BlockSpec((2, tokens - first, width), lambda j, place: (there(j, place), 0, 0))]
    out_shape = [jax.ShapeDtypeStruct((2 * chips, tokens - first, width), BF16)]
    if first:
        out_specs += [pl.BlockSpec((1, first, width), lambda j, place: (j, 0, 0))] * 2
        out_shape += [jax.ShapeDtypeStruct((chips, first, width), BF16)] * 2
    return pl.pallas_call(
        functools.partial(share_kernel, first),
        grid_spec=pltpu.PrefetchScalarGridSpec(
            num_scalar_prefetch=1,
            grid=(chips,),
            in_specs=[
                pl.BlockSpec((tokens, padded), lambda j, place: (0, 0)),
                pl.BlockSpec((padded, 2 * width), lambda j, place: (0, there(j, place))),
            ]
            + [pl.BlockSpec(memory_space=pl.ANY)] * len(after),
            out_specs=out_specs,
        ),
        out_shape=out_shape,
        compiler_params=pltpu.CompilerParams(vmem_limit_bytes=VMEM_BYTES),
        cost_estimate=COST,
    )(place, grad, weight, *after)


def gate(value, after):
    anywhere = pl.BlockSpec(memory_space=pl.ANY)
    return pl.pallas_call(
        lambda *refs: None,
        in_specs=[anywhere] * (1 + len(after)),
        out_specs=anywhere,
        out_shape=jax.ShapeDtypeStruct(value.shape, value.dtype),
        input_output_aliases={0: 0},
    )(value, *after)


def lane_pairs(pairs):
    return [(2 * a + core, 2 * b + core) for a, b in pairs for core in (0, 1)]


def send(value, pairs):
    return lax.ppermute(value, "col", lane_pairs(pairs))


def swap_cores(value, chips):
    return lax.ppermute(value, "col", [(i, i ^ 1) for i in range(2 * chips)])


def add(*terms):
    total = terms[0].astype(F32)
    for term in terms[1:]:
        total = total + term.astype(F32)
    return total


class Shares:
    def __init__(self, own, other, chips):
        arrived = swap_cores(other, chips)
        self.shares = [add(own[j], arrived[j]) for j in range(chips)]
        self.chips, self.step, self.up, self.down = chips, 0, None, None

    def hop(self):
        self.step += 1
        s, chips = self.step, self.chips
        up, down = self.shares[chips - s], self.shares[s]
        if s > 1:
            up, down = up + self.up.astype(F32), down + self.down.astype(F32)
        up, down = up.astype(BF16), down.astype(BF16)
        self.up = send(up, [(z, z + 1) for z in range(s)])
        self.down = send(down, [(z, z - 1) for z in range(chips - s, chips)])
        return [up, down]

    def left(self):
        return self.chips - 1 - self.step

    def result(self):
        return add(self.shares[0], self.up, self.down).astype(BF16)


class LowSum:
    def __init__(self, low, core, chips):
        self.core, self.chips, self.step = core, chips, 0
        half = low.shape[0] // 2
        first, second = low[:half], low[half:]
        got = swap_cores(jnp.where(core == 0, second, first), chips)
        self.mine = add(jnp.where(core == 0, first, second), got)
        self.up = self.down = jnp.zeros(self.mine.shape, F32)

    def hop(self, after):
        s, chips = self.step, self.chips
        self.step += 1
        to_up = (self.mine + self.up).astype(BF16)
        to_up = gate(to_up, after) if after else to_up
        to_down = (self.mine + self.down).astype(BF16)
        self.up = self.up + send(to_up, [(s, s + 1)]).astype(F32)
        self.down = self.down + send(to_down, [(chips - 1 - s, chips - 2 - s)]).astype(F32)
        return [to_up, to_down]

    def left(self):
        return self.chips - 1 - self.step

    def result(self):
        total = (self.mine + self.up + self.down).astype(BF16)
        other = swap_cores(total, self.chips)
        return jnp.concatenate(
            [jnp.where(self.core == 0, total, other), jnp.where(self.core == 0, other, total)], axis=0
        )


def sum_rows(value):
    rows = lax.axis_size("row")
    if rows & (rows - 1):
        return lax.psum(value, "row").astype(F32)
    bits = [1 << b for b in range(rows.bit_length() - 1)]
    half = value.shape[0] // 2
    pieces = [(value[:half], bits), (value[half:], bits[::-1])]
    sums = []
    for piece, order in pieces:
        for bit in order:
            got = lax.ppermute(piece.astype(BF16), "row", [(i, i ^ bit) for i in range(rows)])
            piece = piece.astype(BF16).astype(F32) + got.astype(F32)
        sums.append(piece)
    return jnp.concatenate(sums, axis=0)


def sum_rows_at_once(value):
    rows = lax.axis_size("row")
    if rows & (rows - 1):
        return lax.psum(value, "row").astype(F32)
    terms = [value] + [
        lax.ppermute(value, "row", [(i, i ^ other) for i in range(rows)]) for other in range(1, rows)
    ]
    terms = [term.astype(F32) for term in terms]
    while len(terms) > 1:
        terms = [terms[i] + terms[i + 1] for i in range(0, len(terms), 2)]
    return terms[0]


def local(
    tokens_in, token_grad, gate_gain, inner_weight, inner_bias, outer_weight,
    inner_down, inner_up, outer_down, outer_up,
):
    chips = lax.axis_size("col") // 2
    col_index = lax.axis_index("col")
    core = lax.rem(col_index, 2)
    place = jnp.stack([lax.div(col_index, 2), core]).astype(jnp.int32)
    tok_rows, width = token_grad.shape
    features, ff = inner_weight.shape
    rank = inner_down.shape[1]
    padded = -(-(ff + rank) // COLS) * COLS
    scale = 1.0 / math.sqrt(tok_rows * lax.axis_size("row"))

    gain_local = lax.dynamic_slice_in_dim(gate_gain, col_index * width, width, 0)
    sizes = [tok_rows * part // sum(part for part, _ in SPLIT) for part, _ in SPLIT]
    firsts = [size * share // 1024 // 16 * 16 for size, (_, share) in zip(sizes, SPLIT)]
    starts = [sum(sizes[:i]) for i in range(len(sizes))]

    gathered, gated_parts = [], []
    for start, size in zip(starts, sizes):
        gated = (gain_local[None, :] * token_grad[start : start + size].astype(F32)).astype(BF16)
        both = jnp.stack([tokens_in[start : start + size], gated])
        gathered.append(lax.all_gather(both, "col", axis=0))
        gated_parts.append(gated)

    gap = padded - ff - rank
    blank = jnp.zeros((gap, features), BF16)
    inner_cat = jnp.concatenate([inner_weight.T, blank, inner_down.T], axis=0)
    outer_cat = jnp.concatenate([outer_weight.T, blank, outer_up], axis=0)
    bias = jnp.pad(inner_bias, (0, padded - ff))[None, :]
    up_hi = jnp.pad(inner_up, ((LANES - rank, 0), (0, padded - ff)))
    down_hi = jnp.pad(outer_down.T, ((LANES - rank, 0), (0, padded - ff)))
    down_lo = jnp.pad(outer_down.T, ((0, LANES - rank), (0, padded - ff)))

    far, moving, lows, grads = [], [], [], None
    for index, (both, first) in enumerate(zip(gathered, firsts)):
        def advance(left):
            sent = []
            while index and lows[-1].left() > left:
                ready = moving[-1].hop() if moving[-1] else []
                sent = ready + lows[-1].hop(ready)
            return sent

        grad_pre, low, grad = hidden_call(
            both, inner_cat, outer_cat, bias, up_hi, down_lo, down_hi, ff, advance(0)
        )
        share, *shares = share_call(place, grad_pre, inner_cat, chips, first)
        far.append(lax.psum_scatter(share, "col", scatter_dimension=0))
        moving.append(Shares(*shares, chips) if first else None)
        lows.append(LowSum(low, core, chips))
        grads = grad if grads is None else grads + grad
    hidden_part = (grads[:, :ff] * scale).astype(BF16)
    while lows[-1].left():
        ready = moving[-1].hop() if moving[-1] else []
        lows[-1].hop(ready)
    lows = [summing.result() for summing in lows]
    outs = []
    for shares, rest in zip(moving, far):
        outs += [shares.result(), rest] if shares else [rest]
    tokens_grad = jnp.concatenate(outs, axis=0)

    hidden_sums = sum_rows(hidden_part)
    inner_up_grad = hidden_sums[:rank]
    outer_down_grad = hidden_sums[rank:].T

    feature_part = 0.0
    for start, size, gated, low in zip(starts, sizes, gated_parts, lows):
        tokens = tokens_in[start : start + size]
        feature_part = feature_part + jnp.concatenate(
            [dot_tn(low[:, :rank], gated), dot_tn(low[:, rank:], tokens)], axis=0
        )
    feature_sums = sum_rows_at_once((feature_part * scale).astype(BF16))
    outer_up_grad = feature_sums[:rank]
    inner_down_grad = feature_sums[rank:].T
    return (tokens_grad, inner_down_grad, inner_up_grad, outer_down_grad, outer_up_grad)


def solution(mesh):
    placed = (
        P("row", "col"),
        P("row", "col"),
        P(),
        P(None, "col"),
        P("col"),
        P(None, "col"),
        P(),
        P(None, "col"),
        P("col", None),
        P(),
    )
    return jax.shard_map(
        local,
        mesh=mesh,
        in_specs=placed,
        out_specs=(P("row", "col"), P("col", None), P(None, "col"), P("col", None), P(None, "col")),
        check_vma=False,
    )
```

```python
import functools
import math

import jax
import jax.numpy as jnp
from jax import lax
from jax.experimental import pallas as pl
from jax.experimental.pallas import tpu as pltpu
from jax.sharding import PartitionSpec as P

SLOPE_SCALE = 0.7978845608028654
CUBIC = 0.044715
F32 = jnp.float32
BF16 = jnp.bfloat16
LANES = 128
COLS = 256
VMEM_BYTES = 52 * 1024 * 1024
COST = pl.CostEstimate(flops=20_000_000_000, bytes_accessed=36_000_000, transcendentals=0)
SPLIT = (304, 304, 416)


def dot_nn(left, right):
    return jnp.dot(left, right, preferred_element_type=F32)


def dot_nt(left, right):
    return lax.dot_general(left, right, (((1,), (1,)), ((), ())), preferred_element_type=F32)


def dot_tn(left, right):
    return lax.dot_general(left, right, (((0,), (0,)), ((), ())), preferred_element_type=F32)


def hidden_kernel(ff, place_ref, both_ref, inner_ref, outer_ref, bias_ref, up_ref, down_lo_ref, down_hi_ref, *refs):
    grad_ref, low_ref, grads_ref, pre_acc, hid_acc, hidden_ref = refs[-6:]
    step = pl.program_id(0)
    _, _, tokens, width = both_ref.shape
    padded = pre_acc.shape[1]

    def product(which, weight_ref):
        first, second = both_ref[0, which], both_ref[1, which]
        if width % LANES == 0:
            return dot_nt(jnp.concatenate([first, second], axis=1), weight_ref[...])
        return dot_nt(first, weight_ref[:, :width]) + dot_nt(second, weight_ref[:, width:])

    @pl.when(step == 0)
    def _():
        pre_acc[...] = product(0, inner_ref)
        hid_acc[...] = product(1, outer_ref)

    @pl.when(step > 0)
    def _():
        pre_acc[...] += product(0, inner_ref)
        hid_acc[...] += product(1, outer_ref)

    @pl.when(step == pl.num_programs(0) - 1)
    def _():
        tail = slice(padded - LANES, padded)
        inner_low = pre_acc[:, tail].astype(BF16)
        grad_low = hid_acc[:, tail].astype(BF16)
        rank = LANES // 2
        low = jnp.zeros((tokens, LANES), F32)
        for start in range(0, padded, COLS):
            cols = slice(start, start + COLS)
            pre = pre_acc[:, cols] + dot_nn(inner_low, up_ref[:, cols]) + bias_ref[:, cols]
            square = pre * pre
            tangent = jnp.tanh(SLOPE_SCALE * pre * (1.0 + CUBIC * square))
            half = 0.5 + 0.5 * tangent
            hidden = (pre * half).astype(BF16)
            slope = half + 0.5 * pre * (1.0 - tangent * tangent) * (
                SLOPE_SCALE + 3.0 * CUBIC * SLOPE_SCALE * square
            )
            grad_hidden = hid_acc[:, cols] + dot_nn(grad_low, down_hi_ref[:, cols])
            grad_pre = (grad_hidden * slope).astype(BF16)
            hidden_ref[:, cols] = hidden
            grad_ref[:, cols] = grad_pre
        low = dot_nt(hidden_ref[...], down_lo_ref[...]) + dot_nt(grad_ref[...], up_ref[...])
        low = low.astype(BF16)
        low_ref[...] = low
        grads_ref[:rank] = dot_tn(inner_low, grad_ref[...])[rank:]
        grads_ref[rank:] = dot_tn(grad_low, hidden_ref[...])[rank:]
        lane = lax.broadcasted_iota(jnp.int32, (tokens, LANES), 1)
        keep = lane + (padded - LANES) < ff
        filled = jnp.where(lane >= rank, low, jnp.zeros_like(low))
        grad_ref[:, tail] = jnp.where(keep, grad_ref[:, tail], filled)
        for start in range(0, padded - LANES, LANES):
            if start + LANES > ff:
                here = slice(start, start + LANES)
                grad_ref[:, here] = jnp.where(lane + start < ff, grad_ref[:, here], jnp.zeros_like(low))


def hidden_call(place, both, inner_cat, outer_cat, bias, up, down_lo, down_hi, ff, after=()):
    devices, _, tokens, width = both.shape
    padded = inner_cat.shape[0]
    steps = devices // 2
    whole = lambda k, place: (0, 0)
    there = lambda k, place: (0, lax.rem(place[0] + k, steps))
    return pl.pallas_call(
        functools.partial(hidden_kernel, ff),
        grid_spec=pltpu.PrefetchScalarGridSpec(
        num_scalar_prefetch=1,
        grid=(steps,),
        in_specs=[
            pl.BlockSpec((2, 2, tokens, width), lambda k, place: (k, 0, 0, 0)),
            pl.BlockSpec((padded, 2 * width), there),
            pl.BlockSpec((padded, 2 * width), there),
            pl.BlockSpec((1, padded), whole),
            pl.BlockSpec((LANES, padded), whole),
            pl.BlockSpec((LANES, padded), whole),
            pl.BlockSpec((LANES, padded), whole),
        ]
        + [pl.BlockSpec(memory_space=pl.ANY)] * len(after),
        out_specs=[
            pl.BlockSpec((tokens, padded), whole),
            pl.BlockSpec((tokens, LANES), whole),
            pl.BlockSpec((LANES, padded), whole),
        ],
        scratch_shapes=[
            pltpu.VMEM((tokens, padded), F32),
            pltpu.VMEM((tokens, padded), F32),
            pltpu.VMEM((tokens, padded), BF16),
        ],
        ),
        out_shape=[
            jax.ShapeDtypeStruct((tokens, padded), BF16),
            jax.ShapeDtypeStruct((tokens, LANES), BF16),
            jax.ShapeDtypeStruct((LANES, padded), F32),
        ],
        compiler_params=pltpu.CompilerParams(vmem_limit_bytes=VMEM_BYTES),
        cost_estimate=COST,
    )(place, both, inner_cat, outer_cat, bias, up, down_lo, down_hi, *after)


def share_kernel(grad_ref, weight_ref, *refs):
    share_ref = refs[-1]
    width = share_ref.shape[2]
    if width % LANES == 0:
        share = dot_nn(grad_ref[...], weight_ref[...]).astype(BF16)
        share_ref[0], share_ref[1] = share[:, :width], share[:, width:]
    else:
        for part in (0, 1):
            here = slice(part * width, (part + 1) * width)
            share_ref[part] = dot_nn(grad_ref[...], weight_ref[:, here]).astype(BF16)


def share_call(grad, weight, devices, after=()):
    tokens, padded = grad.shape
    width = weight.shape[1] // devices
    return pl.pallas_call(
        share_kernel,
        grid=(devices // 2,),
        in_specs=[
            pl.BlockSpec((tokens, padded), lambda j: (0, 0)),
            pl.BlockSpec((padded, 2 * width), lambda j: (0, j)),
        ]
        + [pl.BlockSpec(memory_space=pl.ANY)] * len(after),
        out_specs=pl.BlockSpec((2, tokens, width), lambda j: (j, 0, 0)),
        out_shape=jax.ShapeDtypeStruct((devices, tokens, width), BF16),
        compiler_params=pltpu.CompilerParams(vmem_limit_bytes=VMEM_BYTES),
        cost_estimate=COST,
    )(grad, weight, *after)


def gate(value, after):
    anywhere = pl.BlockSpec(memory_space=pl.ANY)
    return pl.pallas_call(
        lambda *refs: None,
        in_specs=[anywhere] * (1 + len(after)),
        out_specs=anywhere,
        out_shape=jax.ShapeDtypeStruct(value.shape, value.dtype),
        input_output_aliases={0: 0},
    )(value, *after)


def lane_pairs(pairs):
    return [(2 * a + core, 2 * b + core) for a, b in pairs for core in (0, 1)]


def send(value, pairs):
    return lax.ppermute(value, "col", lane_pairs(pairs))


def swap_cores(value, chips):
    return lax.ppermute(value, "col", [(i, i ^ 1) for i in range(2 * chips)])


def add(*terms):
    total = terms[0].astype(F32)
    for term in terms[1:]:
        total = total + term.astype(F32)
    return total


class Gather:
    def __init__(self, block, chips):
        self.own, self.chips = block, chips
        self.up, self.down = [block], [block]

    def hop(self, after=()):
        s, chips = len(self.up), self.chips
        if s == chips:
            return []
        up, down = (gate(value, after) if after else value for value in (self.up[-1], self.down[-1]))
        self.up.append(send(up, [(z, z + 1) for z in range(s - 1, chips - 1)]))
        self.down.append(send(down, [(z, z - 1) for z in range(1, chips - s + 1)]))
        return [up, down]

    def result(self, core):
        chips = self.chips
        while len(self.up) < chips:
            self.hop()
        mine = [self.own] + [self.down[j] + self.up[chips - j] for j in range(1, chips)]
        ends = sorted({1, chips - 1})
        rest = [j for j in range(chips) if j not in ends]
        other = [None] * chips
        for group in (rest, ends):
            got = swap_cores(jnp.stack([mine[j] for j in group]), chips)
            for place, j in enumerate(group):
                other[j] = got[place]
        pairs = [(jnp.where(core == 0, a, b), jnp.where(core == 0, b, a)) for a, b in zip(mine, other)]
        return jnp.stack([block for pair in pairs for block in pair])


class LowSum:
    def __init__(self, low, core, chips):
        self.core, self.chips, self.step = core, chips, 0
        half = low.shape[0] // 2
        first, second = low[:half], low[half:]
        got = swap_cores(jnp.where(core == 0, second, first), chips)
        self.mine = add(jnp.where(core == 0, first, second), got)
        self.up = self.down = jnp.zeros(self.mine.shape, F32)

    def hop(self):
        s, chips = self.step, self.chips
        self.step += 1
        to_up = (self.mine + self.up).astype(BF16)
        to_down = (self.mine + self.down).astype(BF16)
        self.up = self.up + send(to_up, [(s, s + 1)]).astype(F32)
        self.down = self.down + send(to_down, [(chips - 1 - s, chips - 2 - s)]).astype(F32)
        return [to_up, to_down]

    def left(self):
        return self.chips - 1 - self.step

    def result(self):
        total = (self.mine + self.up + self.down).astype(BF16)
        other = swap_cores(total, self.chips)
        return jnp.concatenate(
            [jnp.where(self.core == 0, total, other), jnp.where(self.core == 0, other, total)], axis=0
        )


def sum_rows(value):
    rows = lax.axis_size("row")
    if rows & (rows - 1):
        return lax.psum(value, "row").astype(F32)
    bits = [1 << b for b in range(rows.bit_length() - 1)]
    half = value.shape[0] // 2
    pieces = [(value[:half], bits), (value[half:], bits[::-1])]
    sums = []
    for piece, order in pieces:
        for bit in order:
            got = lax.ppermute(piece.astype(BF16), "row", [(i, i ^ bit) for i in range(rows)])
            piece = piece.astype(BF16).astype(F32) + got.astype(F32)
        sums.append(piece)
    return jnp.concatenate(sums, axis=0)


def sum_rows_at_once(value):
    rows = lax.axis_size("row")
    if rows & (rows - 1):
        return lax.psum(value, "row").astype(F32)
    terms = [value] + [
        lax.ppermute(value, "row", [(i, i ^ other) for i in range(rows)]) for other in range(1, rows)
    ]
    terms = [term.astype(F32) for term in terms]
    while len(terms) > 1:
        terms = [terms[i] + terms[i + 1] for i in range(0, len(terms), 2)]
    return terms[0]


def local(
    tokens_in, token_grad, gate_gain, inner_weight, inner_bias, outer_weight,
    inner_down, inner_up, outer_down, outer_up,
):
    chips = lax.axis_size("col") // 2
    col_index = lax.axis_index("col")
    core = lax.rem(col_index, 2)
    tok_rows, width = token_grad.shape
    features, ff = inner_weight.shape
    rank = inner_down.shape[1]
    padded = -(-(ff + rank) // COLS) * COLS
    scale = 1.0 / math.sqrt(tok_rows * lax.axis_size("row"))

    gain_local = lax.dynamic_slice_in_dim(gate_gain, col_index * width, width, 0)
    sizes = [tok_rows * part // sum(SPLIT) for part in SPLIT]
    starts = [sum(sizes[:i]) for i in range(len(sizes))]

    gathered, gated_parts = [], []
    for start, size in zip(starts, sizes):
        gated = (gain_local[None, :] * token_grad[start : start + size].astype(F32)).astype(BF16)
        both = jnp.stack([tokens_in[start : start + size], gated])
        late = start + size == tok_rows
        gathered.append(Gather(both, chips) if late else lax.all_gather(both, "col", axis=0))
        gated_parts.append(gated)

    gap = padded - ff - rank
    blank = jnp.zeros((gap, features), BF16)
    inner_cat = jnp.concatenate([inner_weight.T, blank, inner_down.T], axis=0)
    outer_cat = jnp.concatenate([outer_weight.T, blank, outer_up], axis=0)
    bias = jnp.pad(inner_bias, (0, padded - ff))[None, :]
    up_hi = jnp.pad(inner_up, ((LANES - rank, 0), (0, padded - ff)))
    down_hi = jnp.pad(outer_down.T, ((LANES - rank, 0), (0, padded - ff)))
    down_lo = jnp.pad(outer_down.T, ((0, LANES - rank), (0, padded - ff)))

    outs, lows, sums, grads = [], [], [], None
    here = jnp.stack([lax.div(col_index, 2)]).astype(jnp.int32)
    start_block = jnp.zeros_like(here)
    coming = gathered[-1]
    for index, both in enumerate(gathered):
        late = both is coming
        after, between = [], []
        if late:
            both = both.result(core)
        elif index:
            after = coming.up[1:] + coming.down[1:]
            if len(sums) == 1:
                sums.append(sums[0].result())
                after = after + sums[1:]
            coming.hop()
        grad_pre, low, grad = hidden_call(
            here if late else start_block, both, inner_cat, outer_cat, bias, up_hi, down_lo, down_hi, ff, after
        )
        if not late:
            between = coming.hop([low])
        share = share_call(grad_pre, inner_cat, 2 * chips, between)
        outs.append(lax.psum_scatter(share, "col", scatter_dimension=0))
        lows.append(low)
        if not index:
            sums.append(LowSum(gate(low, [share]), core, chips))
            while sums[0].left():
                sums[0].hop()
        grads = grad if grads is None else grads + grad
    hidden_part = (grads[:, :ff] * scale).astype(BF16)
    sums.append(LowSum(jnp.concatenate(lows[1:], axis=0), core, chips))
    while sums[-1].left():
        sums[-1].hop()
    low = jnp.concatenate([sums[1], sums[-1].result()], axis=0)
    tokens_grad = jnp.concatenate(outs, axis=0)

    hidden_sums = sum_rows(hidden_part)
    inner_up_grad = hidden_sums[:rank]
    outer_down_grad = hidden_sums[rank:].T

    gated = jnp.concatenate(gated_parts, axis=0)
    feature_part = jnp.concatenate([dot_tn(low[:, :rank], gated), dot_tn(low[:, rank:], tokens_in)], axis=0)
    feature_sums = sum_rows_at_once((feature_part * scale).astype(BF16))
    outer_up_grad = feature_sums[:rank]
    inner_down_grad = feature_sums[rank:].T
    return (tokens_grad, inner_down_grad, inner_up_grad, outer_down_grad, outer_up_grad)


def solution(mesh):
    placed = (
        P("row", "col"),
        P("row", "col"),
        P(),
        P(None, "col"),
        P("col"),
        P(None, "col"),
        P(),
        P(None, "col"),
        P("col", None),
        P(),
    )
    return jax.shard_map(
        local,
        mesh=mesh,
        in_specs=placed,
        out_specs=(P("row", "col"), P("col", None), P(None, "col"), P("col", None), P(None, "col")),
        check_vma=False,
    )
```

```python
import functools
import math

import jax
import jax.numpy as jnp
from jax import lax
from jax.experimental import pallas as pl
from jax.experimental.pallas import tpu as pltpu
from jax.sharding import PartitionSpec as P

SLOPE_SCALE = 0.7978845608028654
CUBIC = 0.044715
F32 = jnp.float32
BF16 = jnp.bfloat16
LANES = 128
COLS = 256
VMEM_BYTES = 52 * 1024 * 1024
COST = pl.CostEstimate(flops=20_000_000_000, bytes_accessed=36_000_000, transcendentals=0)
SPLIT = ((512, 320), (512, 0))


def dot_nn(left, right):
    return jnp.dot(left, right, preferred_element_type=F32)


def dot_nt(left, right):
    return lax.dot_general(left, right, (((1,), (1,)), ((), ())), preferred_element_type=F32)


def dot_tn(left, right):
    return lax.dot_general(left, right, (((0,), (0,)), ((), ())), preferred_element_type=F32)


def hidden_kernel(ff, both_ref, weight_ref, bias_ref, up_ref, down_lo_ref, down_hi_ref, *refs):
    grad_ref, low_ref, grads_ref, pre_acc, hid_acc, hidden_ref = refs[-6:]
    step, last = pl.program_id(0), pl.num_programs(0) - 1
    _, _, tokens, width = both_ref.shape
    padded = pre_acc.shape[1]
    rank = LANES // 2
    tail = slice(padded - LANES, padded)
    tiles = [slice(start, start + COLS) for start in range(0, padded, COLS)]

    def product():
        first, second = both_ref[0, 0], both_ref[1, 0]
        if width % LANES == 0:
            return dot_nt(jnp.concatenate([first, second], axis=1), weight_ref[...])
        return dot_nt(first, weight_ref[:, :width]) + dot_nt(second, weight_ref[:, width:])

    @pl.when(step == 0)
    def _():
        pre_acc[...] = product()

    @pl.when(step == 1)
    def _():
        hid_acc[...] = product()

    @pl.when(jnp.logical_and(step > 1, lax.rem(step, 2) == 0))
    def _():
        pre_acc[...] += product()

    @pl.when(jnp.logical_and(jnp.logical_and(step > 1, lax.rem(step, 2) == 1), step < last))
    def _():
        hid_acc[...] += product()

    @pl.when(step == last)
    def _():
        inner_low = pre_acc[:, tail].astype(BF16)
        value = product()
        for cols in tiles:
            pre = pre_acc[:, cols] + dot_nn(inner_low, up_ref[:, cols]) + bias_ref[:, cols]
            square = pre * pre
            tangent = jnp.tanh(pre * (SLOPE_SCALE + SLOPE_SCALE * CUBIC * square))
            half = 0.5 + 0.5 * tangent
            hidden_ref[:, cols] = (pre * half).astype(BF16)
            pre_acc[:, cols] = half + pre * (1.0 - tangent * tangent) * (
                0.5 * SLOPE_SCALE + 1.5 * CUBIC * SLOPE_SCALE * square
            )
        hid_acc[...] += value
        grad_low = hid_acc[:, tail].astype(BF16)
        for cols in tiles:
            grad_hidden = hid_acc[:, cols] + dot_nn(grad_low, down_hi_ref[:, cols])
            grad_ref[:, cols] = (grad_hidden * pre_acc[:, cols]).astype(BF16)
        low = dot_nt(hidden_ref[...], down_lo_ref[...]) + dot_nt(grad_ref[...], up_ref[...])
        low = low.astype(BF16)
        low_ref[...] = low
        grads_ref[:rank] = dot_tn(inner_low, grad_ref[...])[rank:]
        grads_ref[rank:] = dot_tn(grad_low, hidden_ref[...])[rank:]
        lane = lax.broadcasted_iota(jnp.int32, (tokens, LANES), 1)
        keep = lane + (padded - LANES) < ff
        filled = jnp.where(lane >= rank, low, jnp.zeros_like(low))
        grad_ref[:, tail] = jnp.where(keep, grad_ref[:, tail], filled)
        for start in range(0, padded - LANES, LANES):
            if start + LANES > ff:
                here = slice(start, start + LANES)
                grad_ref[:, here] = jnp.where(lane + start < ff, grad_ref[:, here], jnp.zeros_like(low))


def hidden_call(both, weights, bias, up, down_lo, down_hi, ff, after=()):
    devices, _, tokens, width = both.shape
    padded = weights.shape[0] // 2
    whole = lambda s: (0, 0)
    return pl.pallas_call(
        functools.partial(hidden_kernel, ff),
        grid=(devices,),
        in_specs=[
            pl.BlockSpec((2, 1, tokens, width), lambda s: (s // 2, s % 2, 0, 0)),
            pl.BlockSpec((padded, 2 * width), lambda s: (s % 2, s // 2)),
            pl.BlockSpec((1, padded), whole),
            pl.BlockSpec((LANES, padded), whole),
            pl.BlockSpec((LANES, padded), whole),
            pl.BlockSpec((LANES, padded), whole),
        ]
        + [pl.BlockSpec(memory_space=pl.ANY)] * len(after),
        out_specs=[
            pl.BlockSpec((tokens, padded), whole),
            pl.BlockSpec((tokens, LANES), whole),
            pl.BlockSpec((LANES, padded), whole),
        ],
        out_shape=[
            jax.ShapeDtypeStruct((tokens, padded), BF16),
            jax.ShapeDtypeStruct((tokens, LANES), BF16),
            jax.ShapeDtypeStruct((LANES, padded), F32),
        ],
        scratch_shapes=[
            pltpu.VMEM((tokens, padded), F32),
            pltpu.VMEM((tokens, padded), F32),
            pltpu.VMEM((tokens, padded), BF16),
        ],
        compiler_params=pltpu.CompilerParams(vmem_limit_bytes=VMEM_BYTES),
        cost_estimate=COST,
    )(both, weights, bias, up, down_lo, down_hi, *after)


def share_kernel(first, place_ref, grad_ref, weight_ref, *refs):
    share_ref, near_refs = (refs[-3], refs[-2:]) if first else (refs[-1], ())
    width = share_ref.shape[2]
    if width % LANES == 0:
        share = dot_nn(grad_ref[...], weight_ref[...]).astype(BF16)
        shares = [share[:, :width], share[:, width:]]
    else:
        shares = [
            dot_nn(grad_ref[...], weight_ref[:, part * width : (part + 1) * width]).astype(BF16)
            for part in (0, 1)
        ]
    for part in (0, 1):
        share_ref[part] = shares[part][first:]
    for turn, near_ref in enumerate(near_refs):

        @pl.when(place_ref[1] == 0)
        def _():
            near_ref[0] = shares[turn][:first]

        @pl.when(place_ref[1] != 0)
        def _():
            near_ref[0] = shares[1 - turn][:first]


def share_call(place, grad, weight, chips, first, after=()):
    tokens, padded = grad.shape
    width = weight.shape[1] // (2 * chips)
    there = lambda j, place: lax.rem(place[0] + j, chips)
    out_specs = [pl.BlockSpec((2, tokens - first, width), lambda j, place: (there(j, place), 0, 0))]
    out_shape = [jax.ShapeDtypeStruct((2 * chips, tokens - first, width), BF16)]
    if first:
        out_specs += [pl.BlockSpec((1, first, width), lambda j, place: (j, 0, 0))] * 2
        out_shape += [jax.ShapeDtypeStruct((chips, first, width), BF16)] * 2
    return pl.pallas_call(
        functools.partial(share_kernel, first),
        grid_spec=pltpu.PrefetchScalarGridSpec(
            num_scalar_prefetch=1,
            grid=(chips,),
            in_specs=[
                pl.BlockSpec((tokens, padded), lambda j, place: (0, 0)),
                pl.BlockSpec((padded, 2 * width), lambda j, place: (0, there(j, place))),
            ]
            + [pl.BlockSpec(memory_space=pl.ANY)] * len(after),
            out_specs=out_specs,
        ),
        out_shape=out_shape,
        compiler_params=pltpu.CompilerParams(vmem_limit_bytes=VMEM_BYTES),
        cost_estimate=COST,
    )(place, grad, weight, *after)


def gate(value, after):
    anywhere = pl.BlockSpec(memory_space=pl.ANY)
    return pl.pallas_call(
        lambda *refs: None,
        in_specs=[anywhere] * (1 + len(after)),
        out_specs=anywhere,
        out_shape=jax.ShapeDtypeStruct(value.shape, value.dtype),
        input_output_aliases={0: 0},
    )(value, *after)


def lane_pairs(pairs):
    return [(2 * a + core, 2 * b + core) for a, b in pairs for core in (0, 1)]


def send(value, pairs):
    return lax.ppermute(value, "col", lane_pairs(pairs))


def swap_cores(value, chips):
    return lax.ppermute(value, "col", [(i, i ^ 1) for i in range(2 * chips)])


def add(*terms):
    total = terms[0].astype(F32)
    for term in terms[1:]:
        total = total + term.astype(F32)
    return total


class Shares:
    def __init__(self, own, other, chips):
        arrived = swap_cores(other, chips)
        self.shares = [add(own[j], arrived[j]) for j in range(chips)]
        self.chips, self.step, self.up, self.down = chips, 0, None, None

    def hop(self):
        self.step += 1
        s, chips = self.step, self.chips
        up, down = self.shares[chips - s], self.shares[s]
        if s > 1:
            up, down = up + self.up.astype(F32), down + self.down.astype(F32)
        up, down = up.astype(BF16), down.astype(BF16)
        self.up = send(up, [(z, z + 1) for z in range(s)])
        self.down = send(down, [(z, z - 1) for z in range(chips - s, chips)])
        return [up, down]

    def left(self):
        return self.chips - 1 - self.step

    def result(self):
        return add(self.shares[0], self.up, self.down).astype(BF16)


class LowSum:
    def __init__(self, low, core, chips):
        self.core, self.chips, self.step = core, chips, 0
        half = low.shape[0] // 2
        first, second = low[:half], low[half:]
        got = swap_cores(jnp.where(core == 0, second, first), chips)
        self.mine = add(jnp.where(core == 0, first, second), got)
        self.up = self.down = jnp.zeros(self.mine.shape, F32)

    def hop(self, after):
        s, chips = self.step, self.chips
        self.step += 1
        to_up = (self.mine + self.up).astype(BF16)
        to_up = gate(to_up, after) if after else to_up
        to_down = (self.mine + self.down).astype(BF16)
        self.up = self.up + send(to_up, [(s, s + 1)]).astype(F32)
        self.down = self.down + send(to_down, [(chips - 1 - s, chips - 2 - s)]).astype(F32)
        return [to_up, to_down]

    def left(self):
        return self.chips - 1 - self.step

    def result(self):
        total = (self.mine + self.up + self.down).astype(BF16)
        other = swap_cores(total, self.chips)
        return jnp.concatenate(
            [jnp.where(self.core == 0, total, other), jnp.where(self.core == 0, other, total)], axis=0
        )


def sum_rows(value):
    rows = lax.axis_size("row")
    if rows & (rows - 1):
        return lax.psum(value, "row").astype(F32)
    bits = [1 << b for b in range(rows.bit_length() - 1)]
    half = value.shape[0] // 2
    pieces = [(value[:half], bits), (value[half:], bits[::-1])]
    sums = []
    for piece, order in pieces:
        for bit in order:
            got = lax.ppermute(piece.astype(BF16), "row", [(i, i ^ bit) for i in range(rows)])
            piece = piece.astype(BF16).astype(F32) + got.astype(F32)
        sums.append(piece)
    return jnp.concatenate(sums, axis=0)


def sum_rows_at_once(value):
    rows = lax.axis_size("row")
    if rows & (rows - 1):
        return lax.psum(value, "row").astype(F32)
    terms = [value] + [
        lax.ppermute(value, "row", [(i, i ^ other) for i in range(rows)]) for other in range(1, rows)
    ]
    terms = [term.astype(F32) for term in terms]
    while len(terms) > 1:
        terms = [terms[i] + terms[i + 1] for i in range(0, len(terms), 2)]
    return terms[0]


def local(
    tokens_in, token_grad, gate_gain, inner_weight, inner_bias, outer_weight,
    inner_down, inner_up, outer_down, outer_up,
):
    chips = lax.axis_size("col") // 2
    col_index = lax.axis_index("col")
    core = lax.rem(col_index, 2)
    place = jnp.stack([lax.div(col_index, 2), core]).astype(jnp.int32)
    tok_rows, width = token_grad.shape
    features, ff = inner_weight.shape
    rank = inner_down.shape[1]
    padded = -(-(ff + rank) // COLS) * COLS
    scale = 1.0 / math.sqrt(tok_rows * lax.axis_size("row"))

    gain_local = lax.dynamic_slice_in_dim(gate_gain, col_index * width, width, 0)
    sizes = [tok_rows * part // sum(part for part, _ in SPLIT) for part, _ in SPLIT]
    firsts = [size * share // 1024 // 16 * 16 for size, (_, share) in zip(sizes, SPLIT)]
    starts = [sum(sizes[:i]) for i in range(len(sizes))]

    gathered, gated_parts = [], []
    for start, size in zip(starts, sizes):
        gated = (gain_local[None, :] * token_grad[start : start + size].astype(F32)).astype(BF16)
        both = jnp.stack([tokens_in[start : start + size], gated])
        gathered.append(lax.all_gather(both, "col", axis=0))
        gated_parts.append(gated)

    gap = padded - ff - rank
    blank = jnp.zeros((gap, features), BF16)
    weights = jnp.concatenate(
        [inner_weight.T, blank, inner_down.T, outer_weight.T, blank, outer_up], axis=0
    )
    bias = jnp.pad(inner_bias, (0, padded - ff))[None, :]
    up_hi = jnp.pad(inner_up, ((LANES - rank, 0), (0, padded - ff)))
    down_hi = jnp.pad(outer_down.T, ((LANES - rank, 0), (0, padded - ff)))
    down_lo = jnp.pad(outer_down.T, ((0, LANES - rank), (0, padded - ff)))

    far, moving, lows, grads = [], [], [], None
    for index, (both, first) in enumerate(zip(gathered, firsts)):
        def advance(left):
            sent = []
            while index and lows[-1].left() > left:
                ready = moving[-1].hop() if moving[-1] else []
                sent = ready + lows[-1].hop(ready)
            return sent

        grad_pre, low, grad = hidden_call(
            both, weights, bias, up_hi, down_lo, down_hi, ff, advance(0)
        )
        if index:
            lows[-1] = lows[-1].result()
            after = [lows[-1]]
            if moving[-1]:
                moving[-1] = moving[-1].result()
                after.append(moving[-1])
        share, *shares = share_call(place, grad_pre, weights, chips, first, after if index else ())
        far.append(lax.psum_scatter(share, "col", scatter_dimension=0))
        moving.append(Shares(*shares, chips) if first else None)
        lows.append(LowSum(low, core, chips))
        grads = grad if grads is None else grads + grad
    hidden_part = (grads[:, :ff] * scale).astype(BF16)
    while lows[-1].left():
        ready = moving[-1].hop() if moving[-1] else []
        lows[-1].hop(ready)
    lows[-1] = lows[-1].result()
    if moving[-1]:
        moving[-1] = moving[-1].result()
    outs = []
    for near, rest in zip(moving, far):
        outs += [rest] if near is None else [near, rest]
    tokens_grad = jnp.concatenate(outs, axis=0)

    hidden_sums = sum_rows(hidden_part)
    inner_up_grad = hidden_sums[:rank]
    outer_down_grad = hidden_sums[rank:].T

    feature_part = 0.0
    for start, size, gated, low in zip(starts, sizes, gated_parts, lows):
        tokens = tokens_in[start : start + size]
        feature_part = feature_part + jnp.concatenate(
            [dot_tn(low[:, :rank], gated), dot_tn(low[:, rank:], tokens)], axis=0
        )
    feature_sums = sum_rows_at_once((feature_part * scale).astype(BF16))
    outer_up_grad = feature_sums[:rank]
    inner_down_grad = feature_sums[rank:].T
    return (tokens_grad, inner_down_grad, inner_up_grad, outer_down_grad, outer_up_grad)


def solution(mesh):
    placed = (
        P("row", "col"),
        P("row", "col"),
        P(),
        P(None, "col"),
        P("col"),
        P(None, "col"),
        P(),
        P(None, "col"),
        P("col", None),
        P(),
    )
    return jax.shard_map(
        local,
        mesh=mesh,
        in_specs=placed,
        out_specs=(P("row", "col"), P("col", None), P(None, "col"), P("col", None), P(None, "col")),
        check_vma=False,
    )
```

```python
import functools
import math

import jax
import jax.numpy as jnp
from jax import lax
from jax.experimental import pallas as pl
from jax.experimental.pallas import tpu as pltpu
from jax.sharding import PartitionSpec as P

SLOPE_SCALE = 0.7978845608028654
CUBIC = 0.044715
F32 = jnp.float32
BF16 = jnp.bfloat16
LANES = 128
COLS = 256
VMEM_BYTES = 52 * 1024 * 1024
COST = pl.CostEstimate(flops=20_000_000_000, bytes_accessed=36_000_000, transcendentals=0)
SPLIT = ((512, 384), (512, 0))


def dot_nn(left, right):
    return jnp.dot(left, right, preferred_element_type=F32)


def dot_nt(left, right):
    return lax.dot_general(left, right, (((1,), (1,)), ((), ())), preferred_element_type=F32)


def dot_tn(left, right):
    return lax.dot_general(left, right, (((0,), (0,)), ((), ())), preferred_element_type=F32)


def hidden_kernel(ff, both_ref, weight_ref, bias_ref, up_ref, down_lo_ref, down_hi_ref, *refs):
    grad_ref, low_ref, grads_ref, pre_acc, hid_acc, hidden_ref = refs[-6:]
    step, last = pl.program_id(0), pl.num_programs(0) - 1
    _, _, tokens, width = both_ref.shape
    padded = pre_acc.shape[1]
    rank = LANES // 2
    tail = slice(padded - LANES, padded)
    tiles = [slice(start, start + COLS) for start in range(0, padded, COLS)]

    def product():
        first, second = both_ref[0, 0], both_ref[1, 0]
        if width % LANES == 0:
            return dot_nt(jnp.concatenate([first, second], axis=1), weight_ref[...])
        return dot_nt(first, weight_ref[:, :width]) + dot_nt(second, weight_ref[:, width:])

    @pl.when(step == 0)
    def _():
        pre_acc[...] = product()

    @pl.when(step == 1)
    def _():
        hid_acc[...] = product()

    @pl.when(jnp.logical_and(step > 1, lax.rem(step, 2) == 0))
    def _():
        pre_acc[...] += product()

    @pl.when(jnp.logical_and(jnp.logical_and(step > 1, lax.rem(step, 2) == 1), step < last))
    def _():
        hid_acc[...] += product()

    @pl.when(step == last)
    def _():
        inner_low = pre_acc[:, tail].astype(BF16)
        value = product()
        for cols in tiles:
            pre = pre_acc[:, cols] + dot_nn(inner_low, up_ref[:, cols]) + bias_ref[:, cols]
            square = pre * pre
            tangent = jnp.tanh(pre * (SLOPE_SCALE + SLOPE_SCALE * CUBIC * square))
            half = 0.5 + 0.5 * tangent
            hidden_ref[:, cols] = (pre * half).astype(BF16)
            pre_acc[:, cols] = half + pre * (1.0 - tangent * tangent) * (
                0.5 * SLOPE_SCALE + 1.5 * CUBIC * SLOPE_SCALE * square
            )
        hid_acc[...] += value
        grad_low = hid_acc[:, tail].astype(BF16)
        for cols in tiles:
            grad_hidden = hid_acc[:, cols] + dot_nn(grad_low, down_hi_ref[:, cols])
            grad_ref[:, cols] = (grad_hidden * pre_acc[:, cols]).astype(BF16)
        low = dot_nt(hidden_ref[...], down_lo_ref[...]) + dot_nt(grad_ref[...], up_ref[...])
        low = low.astype(BF16)
        low_ref[...] = low
        grads_ref[:rank] = dot_tn(inner_low, grad_ref[...])[rank:]
        grads_ref[rank:] = dot_tn(grad_low, hidden_ref[...])[rank:]
        lane = lax.broadcasted_iota(jnp.int32, (tokens, LANES), 1)
        keep = lane + (padded - LANES) < ff
        filled = jnp.where(lane >= rank, low, jnp.zeros_like(low))
        grad_ref[:, tail] = jnp.where(keep, grad_ref[:, tail], filled)
        for start in range(0, padded - LANES, LANES):
            if start + LANES > ff:
                here = slice(start, start + LANES)
                grad_ref[:, here] = jnp.where(lane + start < ff, grad_ref[:, here], jnp.zeros_like(low))


def hidden_call(both, weights, bias, up, down_lo, down_hi, ff, after=()):
    devices, _, tokens, width = both.shape
    padded = weights.shape[0] // 2
    whole = lambda s: (0, 0)
    return pl.pallas_call(
        functools.partial(hidden_kernel, ff),
        grid=(devices,),
        in_specs=[
            pl.BlockSpec((2, 1, tokens, width), lambda s: (s // 2, s % 2, 0, 0)),
            pl.BlockSpec((padded, 2 * width), lambda s: (s % 2, s // 2)),
            pl.BlockSpec((1, padded), whole),
            pl.BlockSpec((LANES, padded), whole),
            pl.BlockSpec((LANES, padded), whole),
            pl.BlockSpec((LANES, padded), whole),
        ]
        + [pl.BlockSpec(memory_space=pl.ANY)] * len(after),
        out_specs=[
            pl.BlockSpec((tokens, padded), whole),
            pl.BlockSpec((tokens, LANES), whole),
            pl.BlockSpec((LANES, padded), whole),
        ],
        out_shape=[
            jax.ShapeDtypeStruct((tokens, padded), BF16),
            jax.ShapeDtypeStruct((tokens, LANES), BF16),
            jax.ShapeDtypeStruct((LANES, padded), F32),
        ],
        scratch_shapes=[
            pltpu.VMEM((tokens, padded), F32),
            pltpu.VMEM((tokens, padded), F32),
            pltpu.VMEM((tokens, padded), BF16),
        ],
        compiler_params=pltpu.CompilerParams(vmem_limit_bytes=VMEM_BYTES),
        cost_estimate=COST,
    )(both, weights, bias, up, down_lo, down_hi, *after)


def share_kernel(first, place_ref, grad_ref, weight_ref, *refs):
    share_ref, near_refs = (refs[-3], refs[-2:]) if first else (refs[-1], ())
    width = share_ref.shape[2]
    if width % LANES == 0:
        share = dot_nn(grad_ref[...], weight_ref[...]).astype(BF16)
        shares = [share[:, :width], share[:, width:]]
    else:
        shares = [
            dot_nn(grad_ref[...], weight_ref[:, part * width : (part + 1) * width]).astype(BF16)
            for part in (0, 1)
        ]
    for part in (0, 1):
        share_ref[part] = shares[part][first:]
    for turn, near_ref in enumerate(near_refs):

        @pl.when(place_ref[1] == 0)
        def _():
            near_ref[0] = shares[turn][:first]

        @pl.when(place_ref[1] != 0)
        def _():
            near_ref[0] = shares[1 - turn][:first]


def share_call(place, grad, weight, chips, first, after=()):
    tokens, padded = grad.shape
    width = weight.shape[1] // (2 * chips)
    there = lambda j, place: lax.rem(place[0] + j, chips)
    out_specs = [pl.BlockSpec((2, tokens - first, width), lambda j, place: (there(j, place), 0, 0))]
    out_shape = [jax.ShapeDtypeStruct((2 * chips, tokens - first, width), BF16)]
    if first:
        out_specs += [pl.BlockSpec((1, first, width), lambda j, place: (j, 0, 0))] * 2
        out_shape += [jax.ShapeDtypeStruct((chips, first, width), BF16)] * 2
    return pl.pallas_call(
        functools.partial(share_kernel, first),
        grid_spec=pltpu.PrefetchScalarGridSpec(
            num_scalar_prefetch=1,
            grid=(chips,),
            in_specs=[
                pl.BlockSpec((tokens, padded), lambda j, place: (0, 0)),
                pl.BlockSpec((padded, 2 * width), lambda j, place: (0, there(j, place))),
            ]
            + [pl.BlockSpec(memory_space=pl.ANY)] * len(after),
            out_specs=out_specs,
        ),
        out_shape=out_shape,
        compiler_params=pltpu.CompilerParams(vmem_limit_bytes=VMEM_BYTES),
        cost_estimate=COST,
    )(place, grad, weight, *after)


def gate(value, after):
    anywhere = pl.BlockSpec(memory_space=pl.ANY)
    return pl.pallas_call(
        lambda *refs: None,
        in_specs=[anywhere] * (1 + len(after)),
        out_specs=anywhere,
        out_shape=jax.ShapeDtypeStruct(value.shape, value.dtype),
        input_output_aliases={0: 0},
    )(value, *after)


def lane_pairs(pairs):
    return [(2 * a + core, 2 * b + core) for a, b in pairs for core in (0, 1)]


def send(value, pairs):
    return lax.ppermute(value, "col", lane_pairs(pairs))


def swap_cores(value, chips):
    return lax.ppermute(value, "col", [(i, i ^ 1) for i in range(2 * chips)])


def add(*terms):
    total = terms[0].astype(F32)
    for term in terms[1:]:
        total = total + term.astype(F32)
    return total


class Shares:
    def __init__(self, own, other, chips):
        arrived = swap_cores(other, chips)
        self.shares = [add(own[j], arrived[j]) for j in range(chips)]
        self.chips, self.step, self.up, self.down = chips, 0, None, None

    def hop(self):
        self.step += 1
        s, chips = self.step, self.chips
        up, down = self.shares[chips - s], self.shares[s]
        if s > 1:
            up, down = up + self.up.astype(F32), down + self.down.astype(F32)
        up, down = up.astype(BF16), down.astype(BF16)
        self.up = send(up, [(z, z + 1) for z in range(s)])
        self.down = send(down, [(z, z - 1) for z in range(chips - s, chips)])
        return [up, down]

    def left(self):
        return self.chips - 1 - self.step

    def result(self):
        return add(self.shares[0], self.up, self.down).astype(BF16)


class LowSum:
    def __init__(self, low, core, chips):
        self.core, self.chips, self.step = core, chips, 0
        half = low.shape[0] // 2
        first, second = low[:half], low[half:]
        got = swap_cores(jnp.where(core == 0, second, first), chips)
        self.mine = add(jnp.where(core == 0, first, second), got)
        self.up = self.down = jnp.zeros(self.mine.shape, F32)

    def hop(self, after):
        s, chips = self.step, self.chips
        self.step += 1
        to_up = (self.mine + self.up).astype(BF16)
        to_up = gate(to_up, after) if after else to_up
        to_down = (self.mine + self.down).astype(BF16)
        self.up = self.up + send(to_up, [(s, s + 1)]).astype(F32)
        self.down = self.down + send(to_down, [(chips - 1 - s, chips - 2 - s)]).astype(F32)
        return [to_up, to_down]

    def left(self):
        return self.chips - 1 - self.step

    def result(self):
        total = (self.mine + self.up + self.down).astype(BF16)
        other = swap_cores(total, self.chips)
        return jnp.concatenate(
            [jnp.where(self.core == 0, total, other), jnp.where(self.core == 0, other, total)], axis=0
        )


def sum_rows(value):
    rows = lax.axis_size("row")
    if rows & (rows - 1):
        return lax.psum(value, "row").astype(F32)
    bits = [1 << b for b in range(rows.bit_length() - 1)]
    half = value.shape[0] // 2
    pieces = [(value[:half], bits), (value[half:], bits[::-1])]
    sums = []
    for piece, order in pieces:
        for bit in order:
            got = lax.ppermute(piece.astype(BF16), "row", [(i, i ^ bit) for i in range(rows)])
            piece = piece.astype(BF16).astype(F32) + got.astype(F32)
        sums.append(piece)
    return jnp.concatenate(sums, axis=0)


def sum_rows_at_once(value):
    rows = lax.axis_size("row")
    if rows & (rows - 1):
        return lax.psum(value, "row").astype(F32)
    terms = [value] + [
        lax.ppermute(value, "row", [(i, i ^ other) for i in range(rows)]) for other in range(1, rows)
    ]
    terms = [term.astype(F32) for term in terms]
    while len(terms) > 1:
        terms = [terms[i] + terms[i + 1] for i in range(0, len(terms), 2)]
    return terms[0]


def local(
    tokens_in, token_grad, gate_gain, inner_weight, inner_bias, outer_weight,
    inner_down, inner_up, outer_down, outer_up,
):
    chips = lax.axis_size("col") // 2
    col_index = lax.axis_index("col")
    core = lax.rem(col_index, 2)
    place = jnp.stack([lax.div(col_index, 2), core]).astype(jnp.int32)
    tok_rows, width = token_grad.shape
    features, ff = inner_weight.shape
    rank = inner_down.shape[1]
    padded = -(-(ff + rank) // COLS) * COLS
    scale = 1.0 / math.sqrt(tok_rows * lax.axis_size("row"))

    gain_local = lax.dynamic_slice_in_dim(gate_gain, col_index * width, width, 0)
    sizes = [tok_rows * part // sum(part for part, _ in SPLIT) for part, _ in SPLIT]
    firsts = [size * share // 1024 // 16 * 16 for size, (_, share) in zip(sizes, SPLIT)]
    starts = [sum(sizes[:i]) for i in range(len(sizes))]

    gathered, gated_parts = [], []
    for start, size in zip(starts, sizes):
        gated = (gain_local[None, :] * token_grad[start : start + size].astype(F32)).astype(BF16)
        both = jnp.stack([tokens_in[start : start + size], gated])
        gathered.append(lax.all_gather(both, "col", axis=0))
        gated_parts.append(gated)

    gap = padded - ff - rank
    blank = jnp.zeros((gap, features), BF16)
    weights = jnp.concatenate(
        [inner_weight.T, blank, inner_down.T, outer_weight.T, blank, outer_up], axis=0
    )
    bias = jnp.pad(inner_bias, (0, padded - ff))[None, :]
    up_hi = jnp.pad(inner_up, ((LANES - rank, 0), (0, padded - ff)))
    down_hi = jnp.pad(outer_down.T, ((LANES - rank, 0), (0, padded - ff)))
    down_lo = jnp.pad(outer_down.T, ((0, LANES - rank), (0, padded - ff)))

    far, moving, lows, grads = [], [], [], None
    for index, (both, first) in enumerate(zip(gathered, firsts)):
        def advance(left):
            sent = []
            while index and moving[-1] and moving[-1].left() > left:
                sent = moving[-1].hop()
            return sent

        grad_pre, low, grad = hidden_call(
            both, weights, bias, up_hi, down_lo, down_hi, ff, advance(0)
        )
        after = []
        if index and moving[-1]:
            moving[-1] = moving[-1].result()
            after = moving[-1:]
        share, *shares = share_call(place, grad_pre, weights, chips, first, after)
        far.append(lax.psum_scatter(share, "col", scatter_dimension=0))
        moving.append(Shares(*shares, chips) if first else None)
        lows.append(low)
        grads = grad if grads is None else grads + grad
    hidden_part = (grads[:, :ff] * scale).astype(BF16)
    summing = LowSum(jnp.concatenate(lows, axis=0), core, chips)
    while summing.left():
        ready = moving[-1].hop() if moving[-1] else []
        summing.hop(ready)
    low = summing.result()
    if moving[-1]:
        moving[-1] = moving[-1].result()
    outs = []
    for near, rest in zip(moving, far):
        outs += [rest] if near is None else [near, rest]
    tokens_grad = jnp.concatenate(outs, axis=0)

    hidden_sums = sum_rows(hidden_part)
    inner_up_grad = hidden_sums[:rank]
    outer_down_grad = hidden_sums[rank:].T

    gated = jnp.concatenate(gated_parts, axis=0)
    feature_part = jnp.concatenate([dot_tn(low[:, :rank], gated), dot_tn(low[:, rank:], tokens_in)], axis=0)
    feature_sums = sum_rows_at_once((feature_part * scale).astype(BF16))
    outer_up_grad = feature_sums[:rank]
    inner_down_grad = feature_sums[rank:].T
    return (tokens_grad, inner_down_grad, inner_up_grad, outer_down_grad, outer_up_grad)


def solution(mesh):
    placed = (
        P("row", "col"),
        P("row", "col"),
        P(),
        P(None, "col"),
        P("col"),
        P(None, "col"),
        P(),
        P(None, "col"),
        P("col", None),
        P(),
    )
    return jax.shard_map(
        local,
        mesh=mesh,
        in_specs=placed,
        out_specs=(P("row", "col"), P("col", None), P(None, "col"), P("col", None), P(None, "col")),
        check_vma=False,
    )
```

```python
import functools
import math

import jax
import jax.numpy as jnp
from jax import lax
from jax.experimental import pallas as pl
from jax.experimental.pallas import tpu as pltpu
from jax.sharding import PartitionSpec as P

SLOPE_SCALE = 0.7978845608028654
CUBIC = 0.044715
F32 = jnp.float32
BF16 = jnp.bfloat16
LANES = 128
COLS = 256
VMEM_BYTES = 52 * 1024 * 1024
COST = pl.CostEstimate(flops=20_000_000_000, bytes_accessed=36_000_000, transcendentals=0)
SPLIT = ((512, 288), (512, 0))


def dot_nn(left, right):
    return jnp.dot(left, right, preferred_element_type=F32)


def dot_nt(left, right):
    return lax.dot_general(left, right, (((1,), (1,)), ((), ())), preferred_element_type=F32)


def dot_tn(left, right):
    return lax.dot_general(left, right, (((0,), (0,)), ((), ())), preferred_element_type=F32)


def hidden_kernel(ff, both_ref, weight_ref, bias_ref, up_ref, down_lo_ref, down_hi_ref, *refs):
    grad_ref, low_ref, grads_ref, pre_acc, hid_acc, hidden_ref = refs[-6:]
    step, last = pl.program_id(0), pl.num_programs(0) - 1
    _, _, tokens, width = both_ref.shape
    padded = pre_acc.shape[1]
    rank = LANES // 2
    tail = slice(padded - LANES, padded)
    tiles = [slice(start, start + COLS) for start in range(0, padded, COLS)]

    def product():
        first, second = both_ref[0, 0], both_ref[1, 0]
        if width % LANES == 0:
            return dot_nt(jnp.concatenate([first, second], axis=1), weight_ref[...])
        return dot_nt(first, weight_ref[:, :width]) + dot_nt(second, weight_ref[:, width:])

    @pl.when(step == 0)
    def _():
        pre_acc[...] = product()

    @pl.when(step == 1)
    def _():
        hid_acc[...] = product()

    @pl.when(jnp.logical_and(step > 1, lax.rem(step, 2) == 0))
    def _():
        pre_acc[...] += product()

    @pl.when(jnp.logical_and(jnp.logical_and(step > 1, lax.rem(step, 2) == 1), step < last))
    def _():
        hid_acc[...] += product()

    @pl.when(step == last)
    def _():
        inner_low = pre_acc[:, tail].astype(BF16)
        value = product()
        for cols in tiles:
            pre = pre_acc[:, cols] + dot_nn(inner_low, up_ref[:, cols]) + bias_ref[:, cols]
            square = pre * pre
            tangent = jnp.tanh(pre * (SLOPE_SCALE + SLOPE_SCALE * CUBIC * square))
            half = 0.5 + 0.5 * tangent
            hidden_ref[:, cols] = (pre * half).astype(BF16)
            pre_acc[:, cols] = half + pre * (1.0 - tangent * tangent) * (
                0.5 * SLOPE_SCALE + 1.5 * CUBIC * SLOPE_SCALE * square
            )
        hid_acc[...] += value
        grad_low = hid_acc[:, tail].astype(BF16)
        for cols in tiles:
            grad_hidden = hid_acc[:, cols] + dot_nn(grad_low, down_hi_ref[:, cols])
            grad_ref[:, cols] = (grad_hidden * pre_acc[:, cols]).astype(BF16)
        low = dot_nt(hidden_ref[...], down_lo_ref[...]) + dot_nt(grad_ref[...], up_ref[...])
        low = low.astype(BF16)
        low_ref[...] = low
        grads_ref[:rank] = dot_tn(inner_low, grad_ref[...])[rank:]
        grads_ref[rank:] = dot_tn(grad_low, hidden_ref[...])[rank:]
        lane = lax.broadcasted_iota(jnp.int32, (tokens, LANES), 1)
        keep = lane + (padded - LANES) < ff
        filled = jnp.where(lane >= rank, low, jnp.zeros_like(low))
        grad_ref[:, tail] = jnp.where(keep, grad_ref[:, tail], filled)
        for start in range(0, padded - LANES, LANES):
            if start + LANES > ff:
                here = slice(start, start + LANES)
                grad_ref[:, here] = jnp.where(lane + start < ff, grad_ref[:, here], jnp.zeros_like(low))


def hidden_call(both, weights, bias, up, down_lo, down_hi, ff, after=()):
    devices, _, tokens, width = both.shape
    padded = weights.shape[0] // 2
    whole = lambda s: (0, 0)
    return pl.pallas_call(
        functools.partial(hidden_kernel, ff),
        grid=(devices,),
        in_specs=[
            pl.BlockSpec((2, 1, tokens, width), lambda s: (s // 2, s % 2, 0, 0)),
            pl.BlockSpec((padded, 2 * width), lambda s: (s % 2, s // 2)),
            pl.BlockSpec((1, padded), whole),
            pl.BlockSpec((LANES, padded), whole),
            pl.BlockSpec((LANES, padded), whole),
            pl.BlockSpec((LANES, padded), whole),
        ]
        + [pl.BlockSpec(memory_space=pl.ANY)] * len(after),
        out_specs=[
            pl.BlockSpec((tokens, padded), whole),
            pl.BlockSpec((tokens, LANES), whole),
            pl.BlockSpec((LANES, padded), whole),
        ],
        out_shape=[
            jax.ShapeDtypeStruct((tokens, padded), BF16),
            jax.ShapeDtypeStruct((tokens, LANES), BF16),
            jax.ShapeDtypeStruct((LANES, padded), F32),
        ],
        scratch_shapes=[
            pltpu.VMEM((tokens, padded), F32),
            pltpu.VMEM((tokens, padded), F32),
            pltpu.VMEM((tokens, padded), BF16),
        ],
        compiler_params=pltpu.CompilerParams(vmem_limit_bytes=VMEM_BYTES),
        cost_estimate=COST,
    )(both, weights, bias, up, down_lo, down_hi, *after)


def share_kernel(first, place_ref, grad_ref, weight_ref, *refs):
    share_ref, near_refs = (refs[-3], refs[-2:]) if first else (refs[-1], ())
    width = share_ref.shape[2]
    if width % LANES == 0:
        share = dot_nn(grad_ref[...], weight_ref[...]).astype(BF16)
        shares = [share[:, :width], share[:, width:]]
    else:
        shares = [
            dot_nn(grad_ref[...], weight_ref[:, part * width : (part + 1) * width]).astype(BF16)
            for part in (0, 1)
        ]
    for part in (0, 1):
        share_ref[part] = shares[part][first:]
    for turn, near_ref in enumerate(near_refs):

        @pl.when(place_ref[1] == 0)
        def _():
            near_ref[0] = shares[turn][:first]

        @pl.when(place_ref[1] != 0)
        def _():
            near_ref[0] = shares[1 - turn][:first]


def share_call(place, grad, weight, chips, first, after=()):
    tokens, padded = grad.shape
    width = weight.shape[1] // (2 * chips)
    there = lambda j, place: lax.rem(place[0] + j, chips)
    out_specs = [pl.BlockSpec((2, tokens - first, width), lambda j, place: (there(j, place), 0, 0))]
    out_shape = [jax.ShapeDtypeStruct((2 * chips, tokens - first, width), BF16)]
    if first:
        out_specs += [pl.BlockSpec((1, first, width), lambda j, place: (j, 0, 0))] * 2
        out_shape += [jax.ShapeDtypeStruct((chips, first, width), BF16)] * 2
    return pl.pallas_call(
        functools.partial(share_kernel, first),
        grid_spec=pltpu.PrefetchScalarGridSpec(
            num_scalar_prefetch=1,
            grid=(chips,),
            in_specs=[
                pl.BlockSpec((tokens, padded), lambda j, place: (0, 0)),
                pl.BlockSpec((padded, 2 * width), lambda j, place: (0, there(j, place))),
            ]
            + [pl.BlockSpec(memory_space=pl.ANY)] * len(after),
            out_specs=out_specs,
        ),
        out_shape=out_shape,
        compiler_params=pltpu.CompilerParams(vmem_limit_bytes=VMEM_BYTES),
        cost_estimate=COST,
    )(place, grad, weight, *after)


def gate(value, after):
    anywhere = pl.BlockSpec(memory_space=pl.ANY)
    return pl.pallas_call(
        lambda *refs: None,
        in_specs=[anywhere] * (1 + len(after)),
        out_specs=anywhere,
        out_shape=jax.ShapeDtypeStruct(value.shape, value.dtype),
        input_output_aliases={0: 0},
    )(value, *after)


def lane_pairs(pairs):
    return [(2 * a + core, 2 * b + core) for a, b in pairs for core in (0, 1)]


def send(value, pairs):
    return lax.ppermute(value, "col", lane_pairs(pairs))


def swap_cores(value, chips):
    return lax.ppermute(value, "col", [(i, i ^ 1) for i in range(2 * chips)])


def add(*terms):
    total = terms[0].astype(F32)
    for term in terms[1:]:
        total = total + term.astype(F32)
    return total


class Shares:
    def __init__(self, own, other, chips):
        arrived = swap_cores(other, chips)
        self.shares = [add(own[j], arrived[j]) for j in range(chips)]
        self.chips, self.step, self.up, self.down = chips, 0, None, None

    def hop(self):
        self.step += 1
        s, chips = self.step, self.chips
        up, down = self.shares[chips - s], self.shares[s]
        if s > 1:
            up, down = up + self.up.astype(F32), down + self.down.astype(F32)
        up, down = up.astype(BF16), down.astype(BF16)
        self.up = send(up, [(z, z + 1) for z in range(s)])
        self.down = send(down, [(z, z - 1) for z in range(chips - s, chips)])
        return [up, down]

    def left(self):
        return self.chips - 1 - self.step

    def result(self):
        return add(self.shares[0], self.up, self.down).astype(BF16)


class LowSum:
    def __init__(self, low, core, chips):
        self.core, self.chips, self.step = core, chips, 0
        half = low.shape[0] // 2
        first, second = low[:half], low[half:]
        got = swap_cores(jnp.where(core == 0, second, first), chips)
        self.mine = add(jnp.where(core == 0, first, second), got)
        self.up = self.down = jnp.zeros(self.mine.shape, F32)

    def hop(self, after):
        s, chips = self.step, self.chips
        self.step += 1
        to_up = (self.mine + self.up).astype(BF16)
        to_up = gate(to_up, after) if after else to_up
        to_down = (self.mine + self.down).astype(BF16)
        self.up = self.up + send(to_up, [(s, s + 1)]).astype(F32)
        self.down = self.down + send(to_down, [(chips - 1 - s, chips - 2 - s)]).astype(F32)
        return [to_up, to_down]

    def left(self):
        return self.chips - 1 - self.step

    def result(self):
        total = (self.mine + self.up + self.down).astype(BF16)
        other = swap_cores(total, self.chips)
        return jnp.concatenate(
            [jnp.where(self.core == 0, total, other), jnp.where(self.core == 0, other, total)], axis=0
        )


def sum_rows(value):
    rows = lax.axis_size("row")
    if rows & (rows - 1):
        return lax.psum(value, "row").astype(F32)
    bits = [1 << b for b in range(rows.bit_length() - 1)]
    half = value.shape[0] // 2
    pieces = [(value[:half], bits), (value[half:], bits[::-1])]
    sums = []
    for piece, order in pieces:
        for bit in order:
            got = lax.ppermute(piece.astype(BF16), "row", [(i, i ^ bit) for i in range(rows)])
            piece = piece.astype(BF16).astype(F32) + got.astype(F32)
        sums.append(piece)
    return jnp.concatenate(sums, axis=0)


def sum_rows_at_once(value):
    rows = lax.axis_size("row")
    if rows & (rows - 1):
        return lax.psum(value, "row").astype(F32)
    terms = [value] + [
        lax.ppermute(value, "row", [(i, i ^ other) for i in range(rows)]) for other in range(1, rows)
    ]
    terms = [term.astype(F32) for term in terms]
    while len(terms) > 1:
        terms = [terms[i] + terms[i + 1] for i in range(0, len(terms), 2)]
    return terms[0]


def local(
    tokens_in, token_grad, gate_gain, inner_weight, inner_bias, outer_weight,
    inner_down, inner_up, outer_down, outer_up,
):
    chips = lax.axis_size("col") // 2
    col_index = lax.axis_index("col")
    core = lax.rem(col_index, 2)
    place = jnp.stack([lax.div(col_index, 2), core]).astype(jnp.int32)
    tok_rows, width = token_grad.shape
    features, ff = inner_weight.shape
    rank = inner_down.shape[1]
    padded = -(-(ff + rank) // COLS) * COLS
    scale = 1.0 / math.sqrt(tok_rows * lax.axis_size("row"))

    gain_local = lax.dynamic_slice_in_dim(gate_gain, col_index * width, width, 0)
    sizes = [tok_rows * part // sum(part for part, _ in SPLIT) for part, _ in SPLIT]
    firsts = [size * share // 1024 // 16 * 16 for size, (_, share) in zip(sizes, SPLIT)]
    starts = [sum(sizes[:i]) for i in range(len(sizes))]

    gathered, gated_parts = [], []
    for start, size in zip(starts, sizes):
        gated = (gain_local[None, :] * token_grad[start : start + size].astype(F32)).astype(BF16)
        both = jnp.stack([tokens_in[start : start + size], gated])
        gathered.append(lax.all_gather(both, "col", axis=0))
        gated_parts.append(gated)

    gap = padded - ff - rank
    blank = jnp.zeros((gap, features), BF16)
    weights = jnp.concatenate(
        [inner_weight.T, blank, inner_down.T, outer_weight.T, blank, outer_up], axis=0
    )
    bias = jnp.pad(inner_bias, (0, padded - ff))[None, :]
    up_hi = jnp.pad(inner_up, ((LANES - rank, 0), (0, padded - ff)))
    down_hi = jnp.pad(outer_down.T, ((LANES - rank, 0), (0, padded - ff)))
    down_lo = jnp.pad(outer_down.T, ((0, LANES - rank), (0, padded - ff)))

    far, moving, lows, grads = [], [], [], None
    for index, (both, first) in enumerate(zip(gathered, firsts)):
        def advance(left):
            sent = []
            while index and lows[-1].left() > left:
                ready = moving[-1].hop() if moving[-1] else []
                sent = ready + lows[-1].hop(ready)
            return sent

        grad_pre, low, grad = hidden_call(
            both, weights, bias, up_hi, down_lo, down_hi, ff, advance(0)
        )
        if index:
            lows[-1] = lows[-1].result()
            after = [lows[-1]]
            if moving[-1]:
                moving[-1] = moving[-1].result()
                after.append(moving[-1])
        share, *shares = share_call(place, grad_pre, weights, chips, first, after if index else ())
        far.append(lax.psum_scatter(share, "col", scatter_dimension=0))
        moving.append(Shares(*shares, chips) if first else None)
        lows.append(LowSum(low, core, chips))
        grads = grad if grads is None else grads + grad
    hidden_part = (grads[:, :ff] * scale).astype(BF16)
    while lows[-1].left():
        ready = moving[-1].hop() if moving[-1] else []
        lows[-1].hop(ready)
    lows[-1] = lows[-1].result()
    if moving[-1]:
        moving[-1] = moving[-1].result()
    outs = []
    for near, rest in zip(moving, far):
        outs += [rest] if near is None else [near, rest]
    ending = outs.pop()
    placed = jnp.concatenate(outs + [jnp.zeros_like(ending)], axis=0)
    tokens_grad = lax.dynamic_update_slice_in_dim(placed, ending, tok_rows - ending.shape[0], 0)

    hidden_sums = sum_rows(hidden_part)
    inner_up_grad = hidden_sums[:rank]
    outer_down_grad = hidden_sums[rank:].T

    feature_part = 0.0
    for start, size, gated, low in zip(starts, sizes, gated_parts, lows):
        tokens = tokens_in[start : start + size]
        feature_part = feature_part + jnp.concatenate(
            [dot_tn(low[:, :rank], gated), dot_tn(low[:, rank:], tokens)], axis=0
        )
    feature_sums = sum_rows_at_once((feature_part * scale).astype(BF16))
    outer_up_grad = feature_sums[:rank]
    inner_down_grad = feature_sums[rank:].T
    return (tokens_grad, inner_down_grad, inner_up_grad, outer_down_grad, outer_up_grad)


def solution(mesh):
    placed = (
        P("row", "col"),
        P("row", "col"),
        P(),
        P(None, "col"),
        P("col"),
        P(None, "col"),
        P(),
        P(None, "col"),
        P("col", None),
        P(),
    )
    return jax.shard_map(
        local,
        mesh=mesh,
        in_specs=placed,
        out_specs=(P("row", "col"), P("col", None), P(None, "col"), P("col", None), P(None, "col")),
        check_vma=False,
    )
```

```python
import functools
import math

import jax
import jax.numpy as jnp
from jax import lax
from jax.experimental import pallas as pl
from jax.experimental.pallas import tpu as pltpu
from jax.sharding import PartitionSpec as P

SLOPE_SCALE = 0.7978845608028654
CUBIC = 0.044715
F32 = jnp.float32
BF16 = jnp.bfloat16
LANES = 128
COLS = 256
VMEM_BYTES = 52 * 1024 * 1024
COST = pl.CostEstimate(flops=20_000_000_000, bytes_accessed=36_000_000, transcendentals=0)
SPLIT = ((480, 308), (544, 0))


def dot_nn(left, right):
    return jnp.dot(left, right, preferred_element_type=F32)


def dot_nt(left, right):
    return lax.dot_general(left, right, (((1,), (1,)), ((), ())), preferred_element_type=F32)


def dot_tn(left, right):
    return lax.dot_general(left, right, (((0,), (0,)), ((), ())), preferred_element_type=F32)


def hidden_kernel(ff, both_ref, weight_ref, bias_ref, up_ref, down_lo_ref, down_hi_ref, *refs):
    grad_ref, low_ref, grads_ref, pre_acc, hid_acc, hidden_ref = refs[-6:]
    step, last = pl.program_id(0), pl.num_programs(0) - 1
    _, _, tokens, width = both_ref.shape
    padded = pre_acc.shape[1]
    rank = LANES // 2
    tail = slice(padded - LANES, padded)
    tiles = [slice(start, start + COLS) for start in range(0, padded, COLS)]

    def product():
        first, second = both_ref[0, 0], both_ref[1, 0]
        if width % LANES == 0:
            return dot_nt(jnp.concatenate([first, second], axis=1), weight_ref[...])
        return dot_nt(first, weight_ref[:, :width]) + dot_nt(second, weight_ref[:, width:])

    @pl.when(step == 0)
    def _():
        pre_acc[...] = product()

    @pl.when(step == 1)
    def _():
        hid_acc[...] = product()

    @pl.when(jnp.logical_and(step > 1, lax.rem(step, 2) == 0))
    def _():
        pre_acc[...] += product()

    @pl.when(jnp.logical_and(jnp.logical_and(step > 1, lax.rem(step, 2) == 1), step < last))
    def _():
        hid_acc[...] += product()

    @pl.when(step == last)
    def _():
        inner_low = pre_acc[:, tail].astype(BF16)
        value = product()
        for cols in tiles:
            pre = pre_acc[:, cols] + dot_nn(inner_low, up_ref[:, cols]) + bias_ref[:, cols]
            square = pre * pre
            tangent = jnp.tanh(pre * (SLOPE_SCALE + SLOPE_SCALE * CUBIC * square))
            half = 0.5 + 0.5 * tangent
            hidden_ref[:, cols] = (pre * half).astype(BF16)
            pre_acc[:, cols] = half + pre * (1.0 - tangent * tangent) * (
                0.5 * SLOPE_SCALE + 1.5 * CUBIC * SLOPE_SCALE * square
            )
        hid_acc[...] += value
        grad_low = hid_acc[:, tail].astype(BF16)
        for cols in tiles:
            grad_hidden = hid_acc[:, cols] + dot_nn(grad_low, down_hi_ref[:, cols])
            grad_ref[:, cols] = (grad_hidden * pre_acc[:, cols]).astype(BF16)
        low = dot_nt(hidden_ref[...], down_lo_ref[...]) + dot_nt(grad_ref[...], up_ref[...])
        low = low.astype(BF16)
        low_ref[...] = low
        grads_ref[:rank] = dot_tn(inner_low, grad_ref[...])[rank:]
        grads_ref[rank:] = dot_tn(grad_low, hidden_ref[...])[rank:]
        lane = lax.broadcasted_iota(jnp.int32, (tokens, LANES), 1)
        keep = lane + (padded - LANES) < ff
        filled = jnp.where(lane >= rank, low, jnp.zeros_like(low))
        grad_ref[:, tail] = jnp.where(keep, grad_ref[:, tail], filled)
        for start in range(0, padded - LANES, LANES):
            if start + LANES > ff:
                here = slice(start, start + LANES)
                grad_ref[:, here] = jnp.where(lane + start < ff, grad_ref[:, here], jnp.zeros_like(low))


def hidden_call(both, weights, bias, up, down_lo, down_hi, ff, after=()):
    devices, _, tokens, width = both.shape
    padded = weights.shape[0] // 2
    whole = lambda s: (0, 0)
    return pl.pallas_call(
        functools.partial(hidden_kernel, ff),
        grid=(devices,),
        in_specs=[
            pl.BlockSpec((2, 1, tokens, width), lambda s: (s // 2, s % 2, 0, 0)),
            pl.BlockSpec((padded, 2 * width), lambda s: (s % 2, s // 2)),
            pl.BlockSpec((1, padded), whole),
            pl.BlockSpec((LANES, padded), whole),
            pl.BlockSpec((LANES, padded), whole),
            pl.BlockSpec((LANES, padded), whole),
        ]
        + [pl.BlockSpec(memory_space=pl.ANY)] * len(after),
        out_specs=[
            pl.BlockSpec((tokens, padded), whole),
            pl.BlockSpec((tokens, LANES), whole),
            pl.BlockSpec((LANES, padded), whole),
        ],
        out_shape=[
            jax.ShapeDtypeStruct((tokens, padded), BF16),
            jax.ShapeDtypeStruct((tokens, LANES), BF16),
            jax.ShapeDtypeStruct((LANES, padded), F32),
        ],
        scratch_shapes=[
            pltpu.VMEM((tokens, padded), F32),
            pltpu.VMEM((tokens, padded), F32),
            pltpu.VMEM((tokens, padded), BF16),
        ],
        compiler_params=pltpu.CompilerParams(vmem_limit_bytes=VMEM_BYTES),
        cost_estimate=COST,
    )(both, weights, bias, up, down_lo, down_hi, *after)


def share_kernel(first, place_ref, grad_ref, weight_ref, *refs):
    share_ref, near_refs = (refs[-3], refs[-2:]) if first else (refs[-1], ())
    width = share_ref.shape[2]
    if width % LANES == 0:
        share = dot_nn(grad_ref[...], weight_ref[...]).astype(BF16)
        shares = [share[:, :width], share[:, width:]]
    else:
        shares = [
            dot_nn(grad_ref[...], weight_ref[:, part * width : (part + 1) * width]).astype(BF16)
            for part in (0, 1)
        ]
    for part in (0, 1):
        share_ref[part] = shares[part][first:]
    for turn, near_ref in enumerate(near_refs):

        @pl.when(place_ref[1] == 0)
        def _():
            near_ref[0] = shares[turn][:first]

        @pl.when(place_ref[1] != 0)
        def _():
            near_ref[0] = shares[1 - turn][:first]


def share_call(place, grad, weight, chips, first, after=()):
    tokens, padded = grad.shape
    width = weight.shape[1] // (2 * chips)
    there = lambda j, place: lax.rem(place[0] + j, chips)
    out_specs = [pl.BlockSpec((2, tokens - first, width), lambda j, place: (there(j, place), 0, 0))]
    out_shape = [jax.ShapeDtypeStruct((2 * chips, tokens - first, width), BF16)]
    if first:
        out_specs += [pl.BlockSpec((1, first, width), lambda j, place: (j, 0, 0))] * 2
        out_shape += [jax.ShapeDtypeStruct((chips, first, width), BF16)] * 2
    return pl.pallas_call(
        functools.partial(share_kernel, first),
        grid_spec=pltpu.PrefetchScalarGridSpec(
            num_scalar_prefetch=1,
            grid=(chips,),
            in_specs=[
                pl.BlockSpec((tokens, padded), lambda j, place: (0, 0)),
                pl.BlockSpec((padded, 2 * width), lambda j, place: (0, there(j, place))),
            ]
            + [pl.BlockSpec(memory_space=pl.ANY)] * len(after),
            out_specs=out_specs,
        ),
        out_shape=out_shape,
        compiler_params=pltpu.CompilerParams(vmem_limit_bytes=VMEM_BYTES),
        cost_estimate=COST,
    )(place, grad, weight, *after)


def gate(value, after):
    anywhere = pl.BlockSpec(memory_space=pl.ANY)
    return pl.pallas_call(
        lambda *refs: None,
        in_specs=[anywhere] * (1 + len(after)),
        out_specs=anywhere,
        out_shape=jax.ShapeDtypeStruct(value.shape, value.dtype),
        input_output_aliases={0: 0},
    )(value, *after)


def lane_pairs(pairs):
    return [(2 * a + core, 2 * b + core) for a, b in pairs for core in (0, 1)]


def send(value, pairs):
    return lax.ppermute(value, "col", lane_pairs(pairs))


def swap_cores(value, chips):
    return lax.ppermute(value, "col", [(i, i ^ 1) for i in range(2 * chips)])


def add(*terms):
    total = terms[0].astype(F32)
    for term in terms[1:]:
        total = total + term.astype(F32)
    return total


class Shares:
    def __init__(self, own, other, chips):
        arrived = swap_cores(other, chips)
        self.shares = [add(own[j], arrived[j]) for j in range(chips)]
        self.chips, self.step, self.up, self.down = chips, 0, None, None

    def hop(self):
        self.step += 1
        s, chips = self.step, self.chips
        up, down = self.shares[chips - s], self.shares[s]
        if s > 1:
            up, down = up + self.up.astype(F32), down + self.down.astype(F32)
        up, down = up.astype(BF16), down.astype(BF16)
        self.up = send(up, [(z, z + 1) for z in range(s)])
        self.down = send(down, [(z, z - 1) for z in range(chips - s, chips)])
        return [up, down]

    def left(self):
        return self.chips - 1 - self.step

    def result(self):
        return add(self.shares[0], self.up, self.down).astype(BF16)


class LowSum:
    def __init__(self, low, core, chips):
        self.core, self.chips, self.step = core, chips, 0
        half = low.shape[0] // 2
        first, second = low[:half], low[half:]
        got = swap_cores(jnp.where(core == 0, second, first), chips)
        self.mine = add(jnp.where(core == 0, first, second), got)
        self.up = self.down = jnp.zeros(self.mine.shape, F32)

    def hop(self, after):
        s, chips = self.step, self.chips
        self.step += 1
        to_up = (self.mine + self.up).astype(BF16)
        to_up = gate(to_up, after) if after else to_up
        to_down = (self.mine + self.down).astype(BF16)
        self.up = self.up + send(to_up, [(s, s + 1)]).astype(F32)
        self.down = self.down + send(to_down, [(chips - 1 - s, chips - 2 - s)]).astype(F32)
        return [to_up, to_down]

    def left(self):
        return self.chips - 1 - self.step

    def result(self):
        total = (self.mine + self.up + self.down).astype(BF16)
        other = swap_cores(total, self.chips)
        return jnp.concatenate(
            [jnp.where(self.core == 0, total, other), jnp.where(self.core == 0, other, total)], axis=0
        )


def sum_rows(value):
    rows = lax.axis_size("row")
    if rows & (rows - 1):
        return lax.psum(value, "row").astype(F32)
    bits = [1 << b for b in range(rows.bit_length() - 1)]
    half = value.shape[0] // 2
    pieces = [(value[:half], bits), (value[half:], bits[::-1])]
    sums = []
    for piece, order in pieces:
        for bit in order:
            got = lax.ppermute(piece.astype(BF16), "row", [(i, i ^ bit) for i in range(rows)])
            piece = piece.astype(BF16).astype(F32) + got.astype(F32)
        sums.append(piece)
    return jnp.concatenate(sums, axis=0)


def sum_rows_at_once(value):
    rows = lax.axis_size("row")
    if rows & (rows - 1):
        return lax.psum(value, "row").astype(F32)
    terms = [value] + [
        lax.ppermute(value, "row", [(i, i ^ other) for i in range(rows)]) for other in range(1, rows)
    ]
    terms = [term.astype(F32) for term in terms]
    while len(terms) > 1:
        terms = [terms[i] + terms[i + 1] for i in range(0, len(terms), 2)]
    return terms[0]


def local(
    tokens_in, token_grad, gate_gain, inner_weight, inner_bias, outer_weight,
    inner_down, inner_up, outer_down, outer_up,
):
    chips = lax.axis_size("col") // 2
    col_index = lax.axis_index("col")
    core = lax.rem(col_index, 2)
    place = jnp.stack([lax.div(col_index, 2), core]).astype(jnp.int32)
    tok_rows, width = token_grad.shape
    features, ff = inner_weight.shape
    rank = inner_down.shape[1]
    padded = -(-(ff + rank) // COLS) * COLS
    scale = 1.0 / math.sqrt(tok_rows * lax.axis_size("row"))

    gain_local = lax.dynamic_slice_in_dim(gate_gain, col_index * width, width, 0)
    sizes = [tok_rows * part // sum(part for part, _ in SPLIT) for part, _ in SPLIT]
    firsts = [size * share // 1024 // 16 * 16 for size, (_, share) in zip(sizes, SPLIT)]
    starts = [sum(sizes[:i]) for i in range(len(sizes))]

    gathered, gated_parts = [], []
    for start, size in zip(starts, sizes):
        gated = (gain_local[None, :] * token_grad[start : start + size].astype(F32)).astype(BF16)
        both = jnp.stack([tokens_in[start : start + size], gated])
        gathered.append(lax.all_gather(both, "col", axis=0))
        gated_parts.append(gated)

    gap = padded - ff - rank
    blank = jnp.zeros((gap, features), BF16)
    weights = jnp.concatenate(
        [inner_weight.T, blank, inner_down.T, outer_weight.T, blank, outer_up], axis=0
    )
    bias = jnp.pad(inner_bias, (0, padded - ff))[None, :]
    up_hi = jnp.pad(inner_up, ((LANES - rank, 0), (0, padded - ff)))
    down_hi = jnp.pad(outer_down.T, ((LANES - rank, 0), (0, padded - ff)))
    down_lo = jnp.pad(outer_down.T, ((0, LANES - rank), (0, padded - ff)))

    far, moving, lows, grads = [], [], [], None
    for index, (both, first) in enumerate(zip(gathered, firsts)):
        def advance(left):
            sent = []
            while index and lows[-1].left() > left:
                ready = moving[-1].hop() if moving[-1] else []
                sent = ready + lows[-1].hop(ready)
            return sent

        grad_pre, low, grad = hidden_call(
            both, weights, bias, up_hi, down_lo, down_hi, ff, advance(0)
        )
        if index:
            lows[-1] = lows[-1].result()
            after = [lows[-1]]
            if moving[-1]:
                moving[-1] = moving[-1].result()
                after.append(moving[-1])
        share, *shares = share_call(place, grad_pre, weights, chips, first, after if index else ())
        far.append(lax.psum_scatter(share, "col", scatter_dimension=0))
        moving.append(Shares(*shares, chips) if first else None)
        lows.append(LowSum(low, core, chips))
        grads = grad if grads is None else grads + grad
    hidden_part = (grads[:, :ff] * scale).astype(BF16)
    while lows[-1].left():
        ready = moving[-1].hop() if moving[-1] else []
        lows[-1].hop(ready)
    lows[-1] = lows[-1].result()
    if moving[-1]:
        moving[-1] = moving[-1].result()
    outs = []
    for near, rest in zip(moving, far):
        outs += [rest] if near is None else [near, rest]
    ending = outs.pop()
    placed = jnp.concatenate(outs + [jnp.zeros_like(ending)], axis=0)
    tokens_grad = lax.dynamic_update_slice_in_dim(placed, ending, tok_rows - ending.shape[0], 0)

    hidden_sums = sum_rows(hidden_part)
    inner_up_grad = hidden_sums[:rank]
    outer_down_grad = hidden_sums[rank:].T

    feature_part = 0.0
    for start, size, gated, low in zip(starts, sizes, gated_parts, lows):
        tokens = tokens_in[start : start + size]
        feature_part = feature_part + jnp.concatenate(
            [dot_tn(low[:, :rank], gated), dot_tn(low[:, rank:], tokens)], axis=0
        )
    feature_sums = sum_rows_at_once((feature_part * scale).astype(BF16))
    outer_up_grad = feature_sums[:rank]
    inner_down_grad = feature_sums[rank:].T
    return (tokens_grad, inner_down_grad, inner_up_grad, outer_down_grad, outer_up_grad)


def solution(mesh):
    placed = (
        P("row", "col"),
        P("row", "col"),
        P(),
        P(None, "col"),
        P("col"),
        P(None, "col"),
        P(),
        P(None, "col"),
        P("col", None),
        P(),
    )
    return jax.shard_map(
        local,
        mesh=mesh,
        in_specs=placed,
        out_specs=(P("row", "col"), P("col", None), P(None, "col"), P("col", None), P(None, "col")),
        check_vma=False,
    )
```
